32 devices in a mesh: dp: 8 (over z, y), tensor: 4 (over x, core).
Axes of the slice: x: 2, y: 2, z: 4, core: 2. Of those that a mesh axis runs over, the one named last changes fastest.
Arguments:
- tokens: bfloat16 [5120, 2048], P('dp'), may hold values from -6 to 6
- cotangent: bfloat16 [5120, 2048], P('dp'), may hold values from -6 to 6
- lengths: int32 [8], P('dp'), may hold values from 213 to 640, as said below
- w_query: float32 [2048, 2048], P('dp', 'tensor'), may hold values from -0.125 to 0.125
- w_keyval: float32 [2048, 512], P('dp'), may hold values from -0.125 to 0.125
- w_output: float32 [2048, 2048], P('tensor', 'dp'), may hold values from -2.5 to 2.5
- w_gateup: float32 [2, 2048, 16384], P(None, 'dp', 'tensor'), may hold values from -0.125 to 0.125
- w_down: float32 [16384, 2048], P('tensor', 'dp'), may hold values from -0.046875 to 0.046875
- norm_gains: float32 [2, 2048], P(None, 'dp'), may hold values from 0.5 to 1.5
- first_query: float32 [2048, 2048], P('dp', 'tensor'), may hold values from -28 to 28
- first_keyval: float32 [2048, 512], P('dp'), may hold values from -80 to 80
- first_output: float32 [2048, 2048], P('tensor', 'dp'), may hold values from -3.5 to 3.5
- first_gateup: float32 [2, 2048, 16384], P(None, 'dp', 'tensor'), may hold values from -8 to 8
- first_down: float32 [16384, 2048], P('tensor', 'dp'), may hold values from -24 to 24
- first_gains: float32 [2, 2048], P(None, 'dp'), may hold values from -40 to 40
- second_query: float32 [2048, 2048], P('dp', 'tensor'), may hold values from 87.04 to 343.04
- second_keyval: float32 [2048, 512], P('dp'), may hold values from 819.2 to 81920
- second_output: float32 [2048, 2048], P('tensor', 'dp'), may hold values from 1.52 to 6
- second_gateup: float32 [2, 2048, 16384], P(None, 'dp', 'tensor'), may hold values from 9.28 to 37.12
- second_down: float32 [16384, 2048], P('tensor', 'dp'), may hold values from 74.24 to 296.96
- second_gains: float32 [2, 2048], P(None, 'dp'), may hold values from 204.8 to 20480
Outputs:
- block_output: float32 [5120, 2048], P('dp')
- input_grad: float32 [5120, 2048], P('dp')
- query_grad: float32 [2048, 2048], P('dp', 'tensor')
- query_first: float32 [2048, 2048], P('dp', 'tensor')
- query_second: float32 [2048, 2048], P('dp', 'tensor')
- query_update: float32 [2048, 2048], P('dp', 'tensor')
- keyval_grad: float32 [2048, 512], P('dp')
- keyval_first: float32 [2048, 512], P('dp')
- keyval_second: float32 [2048, 512], P('dp')
- keyval_update: float32 [2048, 512], P('dp')
- output_grad: float32 [2048, 2048], P('tensor', 'dp')
- output_first: float32 [2048, 2048], P('tensor', 'dp')
- output_second: float32 [2048, 2048], P('tensor', 'dp')
- output_update: float32 [2048, 2048], P('tensor', 'dp')
- gateup_grad: float32 [2, 2048, 16384], P(None, 'dp', 'tensor')
- gateup_first: float32 [2, 2048, 16384], P(None, 'dp', 'tensor')
- gateup_second: float32 [2, 2048, 16384], P(None, 'dp', 'tensor')
- gateup_update: float32 [2, 2048, 16384], P(None, 'dp', 'tensor')
- down_grad: float32 [16384, 2048], P('tensor', 'dp')
- down_first: float32 [16384, 2048], P('tensor', 'dp')
- down_second: float32 [16384, 2048], P('tensor', 'dp')
- down_update: float32 [16384, 2048], P('tensor', 'dp')
- gains_grad: float32 [2, 2048], P(None, 'dp')
- gains_first: float32 [2, 2048], P(None, 'dp')
- gains_second: float32 [2, 2048], P(None, 'dp')
- gains_update: float32 [2, 2048], P(None, 'dp')
The draws below stay inside these ranges and needn't reach their ends.
Inputs may be any that keep to these rules, and one draw needn't show every extreme that they name: Slot s holds a sequence in its first lengths[s] positions, the rest is padding; in every draw some slot is full (640 tokens) and some holds 213 tokens.
All inputs are finite; a program needn't handle non-finite values.
Results may differ from the reference program's by a relative error of at most 0.024.
Values may be sent and summed in bfloat16 or wider, within the bound.
A program may use at most 384 MiB of HBM per device.

```python
import math
import jax
import jax.numpy as jnp
from jax import lax

D = 2048
HEADS = 8
HD = 256
FF = 16384
SLOT = 640
SEQS = 8
TOKENS = 5120
N_TENSOR = 4


def draw_lengths(key, part):
    key = jax.random.fold_in(key, 7)
    slots = jnp.arange(SEQS).astype(jnp.int32)
    shortest = SLOT // 3
    ramp = shortest + (SLOT - shortest) * slots // max(SEQS - 1, 1)
    jitter = jax.random.randint(key, (SEQS,), -(SLOT // 8), SLOT // 8 + 1)
    drawn = jnp.clip(ramp + jitter, shortest, SLOT)
    drawn = jnp.where(slots == 0, shortest, drawn)
    drawn = jnp.where(slots == SEQS - 1, SLOT, drawn)
    return drawn.astype(jnp.int32)


def levels(stream_key, extent, cuts, smallest, top_value):
    factor_of, own = 1.0, jax.random.fold_in(stream_key, 6)
    for position, blocks in cuts:
        draws = jnp.exp(jax.random.uniform(jax.random.fold_in(own, position), (blocks,), jnp.float32, smallest / len(cuts), top_value / len(cuts)))
        factor_of = factor_of * jnp.repeat(draws, extent[position] // blocks).reshape([-1 if axis == position else 1 for axis in range(len(extent))])
    return factor_of


def normal_values(stream_key, extent, deviation, most, pieces=(), kind=jnp.bfloat16):
    array = jax.random.normal(stream_key, extent, jnp.float32) * deviation
    if len(pieces) > 0:
        array = levels(stream_key, extent, pieces, -0.22, 0.18) * array
    return jnp.clip(array, min=-most, max=most).astype(kind)


def setup_inputs(seed: int = 0) -> dict:
    keys = jax.random.split(jax.random.key(seed), 22)
    tokens = normal_values(keys[0], (TOKENS, D), 1.0, 6.0, ((0, 8),))
    cotangent = normal_values(keys[1], (TOKENS, D), 1.0, 6.0, ((0, 8),))
    lengths = draw_lengths(jax.random.fold_in(keys[21], 71), 0)
    w_query = normal_values(keys[3], (D, HEADS * HD), D ** -0.5, 0.125, ((0, 8), (1, 4)), jnp.float32)
    w_keyval = normal_values(keys[4], (D, 2 * HD), D ** -0.5, 0.125, ((0, 8),), jnp.float32)
    w_output = normal_values(keys[5], (HEADS * HD, D), (HEADS * HD * 2 // SLOT) ** -0.5, 2.5, ((0, 4), (1, 8)), jnp.float32)
    w_gateup = normal_values(keys[6], (2, D, FF), D ** -0.5, 0.125, ((1, 8), (2, 4)), jnp.float32)
    w_down = normal_values(keys[7], (FF, D), FF ** -0.5, 0.046875, ((0, 4), (1, 8)), jnp.float32)
    norm_gains = jnp.clip(1.0 + 0.1 * jax.random.normal(keys[8], (2, D), jnp.float32), 0.5, 1.5)
    first_query = normal_values(keys[9], (D, HEADS * HD), (0.063 * (TOKENS * D / (HEADS * HD)) ** 0.5), 28.0, ((0, 8), (1, 4)), jnp.float32)
    first_keyval = normal_values(keys[10], (D, 2 * HD), (0.063 * (TOKENS * D / HD) ** 0.5), 80.0, ((0, 8),), jnp.float32)
    first_output = normal_values(keys[11], (HEADS * HD, D), (0.21 * SEQS ** 0.5), 3.5, ((0, 4), (1, 8)), jnp.float32)
    first_gateup = normal_values(keys[12], (2, D, FF), (0.059 * (TOKENS * D / FF) ** 0.5), 8.0, ((1, 8), (2, 4)), jnp.float32)
    first_down = normal_values(keys[13], (FF, D), (0.059 * TOKENS ** 0.5), 24.0, ((0, 4), (1, 8)), jnp.float32)
    first_gains = normal_values(keys[14], (2, D), (0.09 * TOKENS ** 0.5), 40.0, ((1, 8),), jnp.float32)
    second_query = jnp.clip(jnp.exp(math.log(343.04) - 1.3714793 * jax.random.uniform(keys[15], (D, HEADS * HD), jnp.float32) ** levels(keys[15], (D, HEADS * HD), ((0, 8), (1, 4)), -0.2, 0.2)), 87.04, 343.04)
    second_keyval = jnp.clip(jnp.exp(math.log(81920.0) - 4.6051702 * jax.random.uniform(keys[16], (D, 2 * HD), jnp.float32) ** levels(keys[16], (D, 2 * HD), ((0, 8),), -0.2, 0.2)), 819.2, 81920.0)
    second_output = jnp.clip(jnp.exp(math.log(6.0) - 1.3730491 * jax.random.uniform(keys[17], (HEADS * HD, D), jnp.float32) ** levels(keys[17], (HEADS * HD, D), ((0, 4), (1, 8)), -0.2, 0.2)), 1.52, 6.0)
    second_gateup = jnp.clip(jnp.exp(math.log(37.12) - 1.3862944 * jax.random.uniform(keys[18], (2, D, FF), jnp.float32) ** levels(keys[18], (2, D, FF), ((1, 8), (2, 4)), -0.2, 0.2)), 9.28, 37.12)
    second_down = jnp.clip(jnp.exp(math.log(296.96) - 1.3862944 * jax.random.uniform(keys[19], (FF, D), jnp.float32) ** levels(keys[19], (FF, D), ((0, 4), (1, 8)), -0.2, 0.2)), 74.24, 296.96)
    second_gains = jnp.clip(jnp.exp(math.log(20480.0) - 4.6051702 * jax.random.uniform(keys[20], (2, D), jnp.float32) ** levels(keys[20], (2, D), ((1, 8),), -0.2, 0.2)), 204.8, 20480.0)
    return {"tokens": tokens, "cotangent": cotangent, "lengths": lengths, "w_query": w_query, "w_keyval": w_keyval, "w_output": w_output, "w_gateup": w_gateup, "w_down": w_down, "norm_gains": norm_gains, "first_query": first_query, "first_keyval": first_keyval, "first_output": first_output, "first_gateup": first_gateup, "first_down": first_down, "first_gains": first_gains, "second_query": second_query, "second_keyval": second_keyval, "second_output": second_output, "second_gateup": second_gateup, "second_down": second_down, "second_gains": second_gains}


@jax.custom_vjp
def low(v):
    return lax.optimization_barrier(v.astype(jnp.bfloat16)).astype(jnp.float32)

@jax.custom_vjp
def low_back(v):
    return v

def low_keep(v):
    return (low(v), None)

def low_pass(kept, grad):
    return (grad,)

def back_keep(v):
    return (v, None)

def back_low(kept, grad):
    return (low(grad),)
low.defvjp(low_keep, low_pass)
low_back.defvjp(back_keep, back_low)
norm_eps = 1e-06
beta_first = 0.9
beta_second = 0.95
learn_rate = 0.01
decay_rate = 0.1
adam_eps = 1e-08
masked_score = -1e+30
precise = lax.Precision.HIGHEST

def matmul_high(left, right):
    return jnp.dot(left, right, precision=precise, preferred_element_type=jnp.float32)

def rms_scale(values, gain):
    inverse = lax.rsqrt(lax.optimization_barrier(jnp.mean(values * values, axis=-1, keepdims=True)) + norm_eps)
    return values * inverse * gain

def attend(query, keyval, length):
    q3 = query.reshape(SLOT, HEADS, HD)
    raw = low_back(jnp.einsum('qhd,kd->hqk', q3, keyval[:, :HD], precision=precise))
    places = jnp.arange(SLOT).astype(jnp.int32)
    allowed = (places[None, :] <= places[:, None]) & (places[None, :] < length)
    scores = jnp.where(allowed[None], raw * HD ** (-0.5), masked_score)
    probs = jax.nn.softmax(scores, axis=-1)
    mixed = jnp.einsum('hqk,kd->qhd', low(probs), keyval[:, HD:], precision=precise)
    return mixed.reshape(SLOT, HEADS * HD)

def grouped(values, weight):
    parts = jnp.einsum('sgk,gkd->gsd', values.reshape(SLOT, N_TENSOR, -1), weight.reshape(N_TENSOR, -1, D), precision=precise)
    return low_back(lax.optimization_barrier(jnp.sum(low(parts), axis=0)))

def block_seq(x, length, weights):
    w_query, w_keyval, w_output, w_gateup, w_down, gains = weights
    normed_one = low(rms_scale(x, gains[0]))
    query = low(low_back(matmul_high(normed_one, w_query)))
    keyval = low(low_back(matmul_high(normed_one, w_keyval)))
    mixed = low(low_back(attend(query, keyval, length)))
    resid = x + grouped(mixed, w_output)
    normed_two = low(rms_scale(resid, gains[1]))
    gate = low_back(matmul_high(normed_two, w_gateup[0]))
    upper = low_back(matmul_high(normed_two, w_gateup[1]))
    hidden = low(jax.nn.gelu(gate, approximate=True) * upper)
    return resid + grouped(hidden, w_down)

def forward(x, lengths, weights):
    lowered = tuple((low(w) for w in weights))
    block = jax.checkpoint(block_seq)

    def step(carry, item):
        return (carry, block(item[0], item[1], lowered))
    _, outs = lax.scan(step, (), (x.reshape(SEQS, SLOT, D), lengths))
    return outs.reshape(TOKENS, D)

def adamw(weight, grad, first, second, decay):
    first_new = beta_first * first + (1.0 - beta_first) * grad
    second_new = beta_second * second + (1.0 - beta_second) * grad * grad
    update = -learn_rate * (first_new / (jnp.sqrt(second_new) + adam_eps) + decay * weight)
    return (grad, first_new, second_new, update)

def reference(tokens, cotangent, lengths, w_query, w_keyval, w_output, w_gateup, w_down, norm_gains, first_query, first_keyval, first_output, first_gateup, first_down, first_gains, second_query, second_keyval, second_output, second_gateup, second_down, second_gains):
    weights = (w_query, w_keyval, w_output, w_gateup, w_down, norm_gains)
    output, pullback = jax.vjp(lambda xs, ws: forward(xs, lengths, ws), tokens.astype(jnp.float32), weights)
    valid = (jnp.arange(SLOT).astype(jnp.int32)[None, :] < lengths[:, None]).reshape(TOKENS, 1)
    grad_input, grads = pullback(jnp.where(valid, cotangent.astype(jnp.float32), 0.0))
    qa = adamw(w_query, grads[0], first_query, second_query, decay_rate)
    ka = adamw(w_keyval, grads[1], first_keyval, second_keyval, decay_rate)
    oa = adamw(w_output, grads[2], first_output, second_output, decay_rate)
    ga = adamw(w_gateup, grads[3], first_gateup, second_gateup, decay_rate)
    da = adamw(w_down, grads[4], first_down, second_down, decay_rate)
    na = adamw(norm_gains, grads[5], first_gains, second_gains, 0.0)
    return (output, grad_input, qa[0], qa[1], qa[2], qa[3], ka[0], ka[1], ka[2], ka[3], oa[0], oa[1], oa[2], oa[3], ga[0], ga[1], ga[2], ga[3], da[0], da[1], da[2], da[3], na[0], na[1], na[2], na[3])
```

```python
import jax
import jax.numpy as jnp
from jax import lax
from jax.sharding import PartitionSpec as P

HD = 256
ZN = 4

norm_eps = 1e-06
beta_first = 0.9
beta_second = 0.95
learn_rate = 0.01
decay_rate = 0.1
adam_eps = 1e-08
masked_score = -1e30

bf = jnp.bfloat16
fl = jnp.float32


def rms_scale(values, gain):
    inverse = lax.rsqrt(jnp.mean(values * values, axis=-1, keepdims=True) + norm_eps)
    return values * inverse * gain


def dot(left, right):
    return jnp.dot(left, right, preferred_element_type=fl)


def inner_rows(left, right):
    return lax.dot_general(left, right, (((0,), (0,)), ((), ())), preferred_element_type=fl)


def times_trans(left, right):
    return lax.dot_general(left, right, (((1,), (1,)), ((), ())), preferred_element_type=fl)


def slot_scores(query, keyval, length):
    slot = query.shape[0]
    heads = query.shape[1] // HD
    places = jnp.arange(slot)
    allowed = (places[None, :] <= places[:, None]) & (places[None, :] < length)
    raw = jnp.einsum(
        "qhd,kd->hqk",
        query.reshape(slot, heads, HD),
        keyval[:, :HD],
        preferred_element_type=fl,
    )
    return jnp.where(allowed[None], raw * HD ** (-0.5), masked_score)


def slot_forward(query, keyval, length):
    scores = slot_scores(query, keyval, length)
    top = jnp.max(scores, axis=-1, keepdims=True)
    expo = jnp.exp(scores - top)
    total = jnp.sum(expo, axis=-1, keepdims=True)
    probs = expo / total
    mixed = jnp.einsum(
        "hqk,kd->qhd", probs.astype(bf), keyval[:, HD:], preferred_element_type=fl
    )
    return mixed.reshape(query.shape), (top + jnp.log(total))[..., 0]


def slot_backward(query, keyval, length, logsum, grad_mixed):
    slot, width = query.shape
    heads = width // HD
    probs = jnp.exp(slot_scores(query, keyval, length) - logsum[..., None])
    grad_three = grad_mixed.reshape(slot, heads, HD)
    grad_value = jnp.einsum("hqk,qhd->kd", probs.astype(bf), grad_three, preferred_element_type=fl)
    grad_probs = jnp.einsum("qhd,kd->hqk", grad_three, keyval[:, HD:], preferred_element_type=fl)
    grad_scores = probs * (grad_probs - jnp.sum(grad_probs * probs, axis=-1, keepdims=True))
    grad_raw = (grad_scores * HD ** (-0.5)).astype(bf)
    grad_query = jnp.einsum("hqk,kd->qhd", grad_raw, keyval[:, :HD], preferred_element_type=fl)
    grad_key = jnp.einsum(
        "hqk,qhd->kd", grad_raw, query.reshape(slot, heads, HD), preferred_element_type=fl
    )
    return grad_query.reshape(slot, width), jnp.concatenate([grad_key, grad_value], axis=1)


def adamw(weight, grad, first, second, decay):
    first_new = beta_first * first + (1.0 - beta_first) * grad
    second_new = beta_second * second + (1.0 - beta_second) * grad * grad
    update = -learn_rate * (first_new / (jnp.sqrt(second_new) + adam_eps) + decay * weight)
    return (grad, first_new, second_new, update)


def swap(value, step):
    axis, bit = step
    return lax.ppermute(value, axis, [(i, i ^ bit) for i in range(lax.axis_size(axis))])


def offset(position, steps, axis):
    total = 0
    for i, (name, bit) in enumerate(steps):
        if name == axis and position >> i & 1:
            total ^= bit
    return total


def gather(value, steps):
    parts = value[None]
    for step in steps:
        parts = jnp.concatenate([parts, swap(parts, step)], axis=0)
    return parts


def reduce(parts, steps):
    for step in reversed(steps):
        half = parts.shape[0] // 2
        got = swap(parts[half:].astype(bf), step)
        parts = parts[:half].astype(fl) + got.astype(fl)
    return parts[0]


def take(array, index, axis=0):
    return lax.dynamic_index_in_dim(array, index, axis, keepdims=False)


def pick(array, me, steps, axis_name, axis=0):
    return jnp.stack(
        [take(array, me ^ offset(p, steps, axis_name), axis) for p in range(2 ** len(steps))]
    )


def place(parts, me, steps, axis_name, axis=0):
    count = parts.shape[0]
    block = parts.shape[1:]
    shape = block[:axis] + (count,) + block[axis:]
    out = jnp.zeros(shape, parts.dtype)
    for p in range(count):
        out = lax.dynamic_update_index_in_dim(
            out, parts[p], me ^ offset(p, steps, axis_name), axis
        )
    return out


def shards(
    tokens,
    cotangent,
    lengths,
    w_query,
    w_keyval,
    w_output,
    w_gateup,
    w_down,
    norm_gains,
    first_query,
    first_keyval,
    first_output,
    first_gateup,
    first_down,
    first_gains,
    second_query,
    second_keyval,
    second_output,
    second_gateup,
    second_down,
    second_gains,
):
    dp = lax.axis_size("dp")
    tn = lax.axis_size("tensor")
    rn = dp // ZN
    me = lax.axis_index("dp")
    z, r = me // rn, me % rn
    t = lax.axis_index("tensor")
    z_steps = [("dp", 2 * rn), ("dp", rn)]
    r_steps = [("dp", 1 << i) for i in reversed(range(rn.bit_length() - 1))]
    t_steps = [("tensor", 1 << i) for i in reversed(range(tn.bit_length() - 1))]
    dp_steps = z_steps + r_steps
    group_steps = z_steps + t_steps

    model = tokens.shape[1]
    rows = model // dp
    slot = tokens.shape[0]
    quarter = slot // tn
    width = w_query.shape[1]
    kvt = w_keyval.shape[1] // tn
    ff = w_down.shape[0] // ZN

    gain_full = place(
        gather(norm_gains.astype(bf), dp_steps), me, dp_steps, "dp", axis=1
    ).reshape(2, model).astype(fl)
    own_keyval = lax.dynamic_slice_in_dim(w_keyval, t * kvt, kvt, 1)
    qkv_w = place(
        gather(jnp.concatenate([w_query, own_keyval], axis=1).astype(bf), dp_steps),
        me, dp_steps, "dp",
    ).reshape(model, width + kvt)
    output_w = place(
        gather(w_output.astype(bf), dp_steps), me, dp_steps, "dp", axis=1
    ).reshape(width, model)

    def zpos(k):
        return ("dp", k * rn)

    gateup_cols = w_gateup.astype(bf).reshape(2, rows, ZN, ff)
    down_rows = w_down.astype(bf).reshape(ZN, ff, rows)
    gateup_w = jnp.zeros((2, ZN, rn, rows, ff), bf)
    down_w = jnp.zeros((ff, ZN, rn, rows), bf)
    for k in range(ZN):
        block = take(gateup_cols, z ^ k, 2)
        if k:
            block = swap(block, zpos(k))
        block = place(gather(block, r_steps), r, r_steps, "dp", axis=1)
        gateup_w = lax.dynamic_update_index_in_dim(gateup_w, block, z ^ k, 1)
    for k in range(ZN):
        block = take(down_rows, z ^ k, 0)
        if k:
            block = swap(block, zpos(k))
        block = place(gather(block, r_steps), r, r_steps, "dp", axis=1)
        down_w = lax.dynamic_update_index_in_dim(down_w, block, z ^ k, 1)
    gateup_w = gateup_w.reshape(2, model, ff)
    down_w = down_w.reshape(ff, model)

    x = tokens.astype(fl)
    length = lengths[0]
    normed_one = rms_scale(x, gain_full[0]).astype(bf)
    projected = dot(normed_one, qkv_w).astype(bf)
    query = projected[:, :width]
    keyval = place(
        gather(projected[:, width:], t_steps), t, t_steps, "tensor", axis=1
    ).reshape(slot, tn * kvt)
    mixed, logsum = slot_forward(query, keyval, length)
    mixed = mixed.astype(bf)
    attn_part = dot(mixed, output_w).astype(bf).reshape(tn, quarter, model)
    attn = reduce(pick(attn_part, t, t_steps, "tensor"), t_steps)
    x_own = lax.dynamic_slice_in_dim(x, t * quarter, quarter, 0)
    resid = x_own + attn
    normed_two_own = rms_scale(resid, gain_full[1]).astype(bf)

    group = ZN * tn * quarter
    normed_two = gather(normed_two_own, group_steps).reshape(group, model)
    cot_own = lax.dynamic_slice_in_dim(cotangent, t * quarter, quarter, 0)
    valid = (t * quarter + jnp.arange(quarter) < length)[:, None]
    grad_own = jnp.where(valid, cot_own, jnp.zeros_like(cot_own))
    grad_low = gather(grad_own, group_steps).reshape(group, model)

    gate = dot(normed_two, gateup_w[0])
    upper = dot(normed_two, gateup_w[1])
    hidden = (jax.nn.gelu(gate, approximate=True) * upper).astype(bf)
    ff_part = dot(hidden, down_w).astype(bf).reshape(ZN * tn, quarter, model)
    out_own = resid + reduce(ff_part, group_steps)
    block_output = place(gather(out_own, t_steps), t, t_steps, "tensor").reshape(slot, model)

    grad_hidden = times_trans(grad_low, down_w)
    _, pull_gelu = jax.vjp(
        lambda left, right: jax.nn.gelu(left, approximate=True) * right, gate, upper
    )
    grad_gate, grad_up = pull_gelu(grad_hidden)
    grad_gate = grad_gate.astype(bf)
    grad_up = grad_up.astype(bf)
    grad_normed = (times_trans(grad_gate, gateup_w[0]) + times_trans(grad_up, gateup_w[1])).astype(bf)
    grad_normed_two = reduce(grad_normed.reshape(ZN * tn, quarter, model), group_steps)

    def columns(array, j):
        return take(array.reshape(group, ZN, rn, rows), r ^ j, 2).reshape(group, ZN * rows)

    def scatter_z(sums, axis):
        parts = []
        for k in range(ZN):
            block = take(sums, z ^ k, 0).astype(bf)
            parts.append(swap(block, zpos(k)) if k else block)
        shape = parts[0].shape
        out = jnp.zeros(shape[:axis] + (ZN,) + shape[axis:], bf)
        for k in range(ZN):
            out = lax.dynamic_update_index_in_dim(out, parts[k], z ^ k, axis)
        return out

    r_offsets = [offset(p, r_steps, "dp") for p in range(rn)]
    down_parts = jnp.stack(
        [
            inner_rows(hidden, columns(grad_low, j)).astype(bf).reshape(ff, ZN, rows)
            for j in r_offsets
        ]
    )
    down_sum = reduce(down_parts, r_steps)
    down_shard = scatter_z(jnp.moveaxis(down_sum, 1, 0), 0).reshape(ZN * ff, rows).astype(fl)

    shards_gu = []
    for grad in (grad_gate, grad_up):
        parts = jnp.stack(
            [
                inner_rows(columns(normed_two, j), grad).astype(bf).reshape(ZN, rows, ff)
                for j in r_offsets
            ]
        )
        sums = reduce(parts, r_steps)
        shards_gu.append(scatter_z(sums, 1).reshape(rows, ZN * ff).astype(fl))
    gateup_shard = jnp.stack(shards_gu)

    _, pull_second = jax.vjp(rms_scale, resid, gain_full[1])
    grad_resid_norm, grad_gain_two = pull_second(grad_normed_two)
    grad_resid = grad_own.astype(fl) + grad_resid_norm
    grad_attn = place(gather(grad_resid.astype(bf), t_steps), t, t_steps, "tensor").reshape(slot, model)

    output_grad = inner_rows(mixed, grad_attn).astype(bf)
    grad_mixed = times_trans(grad_attn, output_w).astype(bf)
    grad_query, grad_keyval = slot_backward(query, keyval, length, logsum, grad_mixed)
    keyval_parts = grad_keyval.astype(bf).reshape(slot, tn, kvt)
    keyval_low = reduce(pick(keyval_parts, t, t_steps, "tensor", axis=1), t_steps).astype(bf)
    grad_projected = jnp.concatenate([grad_query.astype(bf), keyval_low], axis=1)
    one_parts = times_trans(grad_projected, qkv_w).astype(bf).reshape(tn, quarter, model)
    grad_normed_one = reduce(pick(one_parts, t, t_steps, "tensor"), t_steps)
    qkv_grad = inner_rows(normed_one, grad_projected).astype(bf)
    _, pull_first = jax.vjp(rms_scale, x_own, gain_full[0])
    grad_x_norm, grad_gain_one = pull_first(grad_normed_one)
    input_own = grad_resid + grad_x_norm
    input_grad = place(gather(input_own, t_steps), t, t_steps, "tensor").reshape(slot, model)

    qkv_shard = reduce(
        pick(qkv_grad.reshape(dp, rows, width + kvt), me, dp_steps, "dp"), dp_steps
    )
    query_shard = qkv_shard[:, :width]
    keyval_shard = place(
        gather(qkv_shard[:, width:].astype(bf), t_steps), t, t_steps, "tensor", axis=1
    ).reshape(rows, tn * kvt).astype(fl)
    output_shard = reduce(
        pick(output_grad.reshape(width, dp, rows), me, dp_steps, "dp", axis=1), dp_steps
    )
    gains_grad = jnp.stack([grad_gain_one, grad_gain_two]).reshape(2, dp, rows)
    gains_parts = pick(gains_grad, me, dp_steps, "dp", axis=1)
    for step in reversed(dp_steps):
        half = gains_parts.shape[0] // 2
        gains_parts = gains_parts[:half] + swap(gains_parts[half:], step)
    gains_shard = gains_parts[0]
    for step in t_steps:
        gains_shard = gains_shard + swap(gains_shard, step)

    qa = adamw(w_query, query_shard, first_query, second_query, decay_rate)
    ka = adamw(w_keyval, keyval_shard, first_keyval, second_keyval, decay_rate)
    oa = adamw(w_output, output_shard, first_output, second_output, decay_rate)
    ga = adamw(w_gateup, gateup_shard, first_gateup, second_gateup, decay_rate)
    da = adamw(w_down, down_shard, first_down, second_down, decay_rate)
    na = adamw(norm_gains, gains_shard, first_gains, second_gains, 0.0)
    return (block_output, input_grad, *qa, *ka, *oa, *ga, *da, *na)


def solution(mesh):
    query = P("dp", "tensor")
    keyval = P("dp", None)
    output = P("tensor", "dp")
    gateup = P(None, "dp", "tensor")
    gains = P(None, "dp")
    weights = (query, keyval, output, gateup, output, gains)
    return jax.shard_map(
        shards,
        mesh=mesh,
        in_specs=(P("dp", None), P("dp", None), P("dp")) + weights * 3,
        out_specs=(P("dp", None), P("dp", None)) + tuple(w for w in weights for _ in range(4)),
        check_vma=False,
    )
```

```python
import functools

import jax
import jax.numpy as jnp
from jax import lax
from jax.experimental import pallas as pl
from jax.experimental.pallas import tpu as pltpu
from jax.sharding import PartitionSpec as P

HD = 256
ZN = 4

norm_eps = 1e-06
beta_first = 0.9
beta_second = 0.95
learn_rate = 0.01
decay_rate = 0.1
adam_eps = 1e-08
masked_score = -1e30

bf = jnp.bfloat16
fl = jnp.float32


def rms_scale(values, gain):
    inverse = lax.rsqrt(jnp.mean(values * values, axis=-1, keepdims=True) + norm_eps)
    return values * inverse * gain


def dot(left, right):
    return jnp.dot(left, right, preferred_element_type=fl)


def inner_rows(left, right):
    return lax.dot_general(left, right, (((0,), (0,)), ((), ())), preferred_element_type=fl)


def times_trans(left, right):
    return lax.dot_general(left, right, (((1,), (1,)), ((), ())), preferred_element_type=fl)


def slot_scores(query, keyval, length):
    slot = query.shape[0]
    heads = query.shape[1] // HD
    places = jnp.arange(slot)
    allowed = (places[None, :] <= places[:, None]) & (places[None, :] < length)
    raw = jnp.einsum(
        "qhd,kd->hqk",
        query.reshape(slot, heads, HD),
        keyval[:, :HD],
        preferred_element_type=fl,
    )
    return jnp.where(allowed[None], raw * HD ** (-0.5), masked_score)


def slot_forward(query, keyval, length):
    scores = slot_scores(query, keyval, length)
    top = jnp.max(scores, axis=-1, keepdims=True)
    expo = jnp.exp(scores - top)
    total = jnp.sum(expo, axis=-1, keepdims=True)
    probs = expo / total
    mixed = jnp.einsum(
        "hqk,kd->qhd", probs.astype(bf), keyval[:, HD:], preferred_element_type=fl
    )
    return mixed.reshape(query.shape), (top + jnp.log(total))[..., 0]


def slot_backward(query, keyval, length, logsum, grad_mixed):
    slot, width = query.shape
    heads = width // HD
    probs = jnp.exp(slot_scores(query, keyval, length) - logsum[..., None])
    grad_three = grad_mixed.reshape(slot, heads, HD)
    grad_value = jnp.einsum("hqk,qhd->kd", probs.astype(bf), grad_three, preferred_element_type=fl)
    grad_probs = jnp.einsum("qhd,kd->hqk", grad_three, keyval[:, HD:], preferred_element_type=fl)
    grad_scores = probs * (grad_probs - jnp.sum(grad_probs * probs, axis=-1, keepdims=True))
    grad_raw = (grad_scores * HD ** (-0.5)).astype(bf)
    grad_query = jnp.einsum("hqk,kd->qhd", grad_raw, keyval[:, :HD], preferred_element_type=fl)
    grad_key = jnp.einsum(
        "hqk,qhd->kd", grad_raw, query.reshape(slot, heads, HD), preferred_element_type=fl
    )
    return grad_query.reshape(slot, width), jnp.concatenate([grad_key, grad_value], axis=1)


def adamw(weight, grad, first, second, decay):
    first_new = beta_first * first + (1.0 - beta_first) * grad
    second_new = beta_second * second + (1.0 - beta_second) * grad * grad
    update = -learn_rate * (first_new / (jnp.sqrt(second_new) + adam_eps) + decay * weight)
    return (grad, first_new, second_new, update)


def swap(value, step):
    axis, bit = step
    return lax.ppermute(value, axis, [(i, i ^ bit) for i in range(lax.axis_size(axis))])


def offset(position, steps, axis):
    total = 0
    for i, (name, bit) in enumerate(steps):
        if name == axis and position >> i & 1:
            total ^= bit
    return total


def gather(value, steps):
    parts = value[None]
    for step in steps:
        parts = jnp.concatenate([parts, swap(parts, step)], axis=0)
    return parts


def reduce(parts, steps):
    for step in reversed(steps):
        half = parts.shape[0] // 2
        got = swap(parts[half:].astype(bf), step)
        parts = parts[:half].astype(fl) + got.astype(fl)
    return parts[0]


def take(array, index, axis=0):
    return lax.dynamic_index_in_dim(array, index, axis, keepdims=False)


def pick(array, me, steps, axis_name, axis=0):
    return jnp.stack(
        [take(array, me ^ offset(p, steps, axis_name), axis) for p in range(2 ** len(steps))]
    )


def place(parts, me, steps, axis_name, axis=0):
    count = parts.shape[0]
    block = parts.shape[1:]
    shape = block[:axis] + (count,) + block[axis:]
    out = jnp.zeros(shape, parts.dtype)
    for p in range(count):
        out = lax.dynamic_update_index_in_dim(
            out, parts[p], me ^ offset(p, steps, axis_name), axis
        )
    return out


def general(
    tokens,
    cotangent,
    lengths,
    w_query,
    w_keyval,
    w_output,
    w_gateup,
    w_down,
    norm_gains,
    first_query,
    first_keyval,
    first_output,
    first_gateup,
    first_down,
    first_gains,
    second_query,
    second_keyval,
    second_output,
    second_gateup,
    second_down,
    second_gains,
):
    dp = lax.axis_size("dp")
    tn = lax.axis_size("tensor")
    rn = dp // ZN
    me = lax.axis_index("dp")
    z, r = me // rn, me % rn
    t = lax.axis_index("tensor")
    z_steps = [("dp", 2 * rn), ("dp", rn)]
    r_steps = [("dp", 1 << i) for i in reversed(range(rn.bit_length() - 1))]
    t_steps = [("tensor", 1 << i) for i in reversed(range(tn.bit_length() - 1))]
    dp_steps = z_steps + r_steps
    group_steps = z_steps + t_steps

    model = tokens.shape[1]
    rows = model // dp
    slot = tokens.shape[0]
    quarter = slot // tn
    width = w_query.shape[1]
    kvt = w_keyval.shape[1] // tn
    ff = w_down.shape[0] // ZN

    gain_full = place(
        gather(norm_gains.astype(bf), dp_steps), me, dp_steps, "dp", axis=1
    ).reshape(2, model).astype(fl)
    own_keyval = lax.dynamic_slice_in_dim(w_keyval, t * kvt, kvt, 1)
    qkv_w = place(
        gather(jnp.concatenate([w_query, own_keyval], axis=1).astype(bf), dp_steps),
        me, dp_steps, "dp",
    ).reshape(model, width + kvt)
    output_w = place(
        gather(w_output.astype(bf), dp_steps), me, dp_steps, "dp", axis=1
    ).reshape(width, model)

    def zpos(k):
        return ("dp", k * rn)

    gateup_cols = w_gateup.astype(bf).reshape(2, rows, ZN, ff)
    down_rows = w_down.astype(bf).reshape(ZN, ff, rows)
    gateup_w = jnp.zeros((2, ZN, rn, rows, ff), bf)
    down_w = jnp.zeros((ff, ZN, rn, rows), bf)
    for k in range(ZN):
        block = take(gateup_cols, z ^ k, 2)
        if k:
            block = swap(block, zpos(k))
        block = place(gather(block, r_steps), r, r_steps, "dp", axis=1)
        gateup_w = lax.dynamic_update_index_in_dim(gateup_w, block, z ^ k, 1)
    for k in range(ZN):
        block = take(down_rows, z ^ k, 0)
        if k:
            block = swap(block, zpos(k))
        block = place(gather(block, r_steps), r, r_steps, "dp", axis=1)
        down_w = lax.dynamic_update_index_in_dim(down_w, block, z ^ k, 1)
    gateup_w = gateup_w.reshape(2, model, ff)
    down_w = down_w.reshape(ff, model)

    x = tokens.astype(fl)
    length = lengths[0]
    normed_one = rms_scale(x, gain_full[0]).astype(bf)
    projected = dot(normed_one, qkv_w).astype(bf)
    query = projected[:, :width]
    keyval = place(
        gather(projected[:, width:], t_steps), t, t_steps, "tensor", axis=1
    ).reshape(slot, tn * kvt)
    mixed, logsum = slot_forward(query, keyval, length)
    mixed = mixed.astype(bf)
    attn_part = dot(mixed, output_w).astype(bf).reshape(tn, quarter, model)
    attn = reduce(pick(attn_part, t, t_steps, "tensor"), t_steps)
    x_own = lax.dynamic_slice_in_dim(x, t * quarter, quarter, 0)
    resid = x_own + attn
    normed_two_own = rms_scale(resid, gain_full[1]).astype(bf)

    group = ZN * tn * quarter
    normed_two = gather(normed_two_own, group_steps).reshape(group, model)
    cot_own = lax.dynamic_slice_in_dim(cotangent, t * quarter, quarter, 0)
    valid = (t * quarter + jnp.arange(quarter) < length)[:, None]
    grad_own = jnp.where(valid, cot_own, jnp.zeros_like(cot_own))
    grad_low = gather(grad_own, group_steps).reshape(group, model)

    gate = dot(normed_two, gateup_w[0])
    upper = dot(normed_two, gateup_w[1])
    hidden = (jax.nn.gelu(gate, approximate=True) * upper).astype(bf)
    ff_part = dot(hidden, down_w).astype(bf).reshape(ZN * tn, quarter, model)
    out_own = resid + reduce(ff_part, group_steps)
    block_output = place(gather(out_own, t_steps), t, t_steps, "tensor").reshape(slot, model)

    grad_hidden = times_trans(grad_low, down_w)
    _, pull_gelu = jax.vjp(
        lambda left, right: jax.nn.gelu(left, approximate=True) * right, gate, upper
    )
    grad_gate, grad_up = pull_gelu(grad_hidden)
    grad_gate = grad_gate.astype(bf)
    grad_up = grad_up.astype(bf)
    grad_normed = (times_trans(grad_gate, gateup_w[0]) + times_trans(grad_up, gateup_w[1])).astype(bf)
    grad_normed_two = reduce(grad_normed.reshape(ZN * tn, quarter, model), group_steps)

    def columns(array, j):
        return take(array.reshape(group, ZN, rn, rows), r ^ j, 2).reshape(group, ZN * rows)

    def scatter_z(sums, axis):
        parts = []
        for k in range(ZN):
            block = take(sums, z ^ k, 0).astype(bf)
            parts.append(swap(block, zpos(k)) if k else block)
        shape = parts[0].shape
        out = jnp.zeros(shape[:axis] + (ZN,) + shape[axis:], bf)
        for k in range(ZN):
            out = lax.dynamic_update_index_in_dim(out, parts[k], z ^ k, axis)
        return out

    r_offsets = [offset(p, r_steps, "dp") for p in range(rn)]
    down_parts = jnp.stack(
        [
            inner_rows(hidden, columns(grad_low, j)).astype(bf).reshape(ff, ZN, rows)
            for j in r_offsets
        ]
    )
    down_sum = reduce(down_parts, r_steps)
    down_shard = scatter_z(jnp.moveaxis(down_sum, 1, 0), 0).reshape(ZN * ff, rows).astype(fl)

    shards_gu = []
    for grad in (grad_gate, grad_up):
        parts = jnp.stack(
            [
                inner_rows(columns(normed_two, j), grad).astype(bf).reshape(ZN, rows, ff)
                for j in r_offsets
            ]
        )
        sums = reduce(parts, r_steps)
        shards_gu.append(scatter_z(sums, 1).reshape(rows, ZN * ff).astype(fl))
    gateup_shard = jnp.stack(shards_gu)

    _, pull_second = jax.vjp(rms_scale, resid, gain_full[1])
    grad_resid_norm, grad_gain_two = pull_second(grad_normed_two)
    grad_resid = grad_own.astype(fl) + grad_resid_norm
    grad_attn = place(gather(grad_resid.astype(bf), t_steps), t, t_steps, "tensor").reshape(slot, model)

    output_grad = inner_rows(mixed, grad_attn).astype(bf)
    grad_mixed = times_trans(grad_attn, output_w).astype(bf)
    grad_query, grad_keyval = slot_backward(query, keyval, length, logsum, grad_mixed)
    keyval_parts = grad_keyval.astype(bf).reshape(slot, tn, kvt)
    keyval_low = reduce(pick(keyval_parts, t, t_steps, "tensor", axis=1), t_steps).astype(bf)
    grad_projected = jnp.concatenate([grad_query.astype(bf), keyval_low], axis=1)
    one_parts = times_trans(grad_projected, qkv_w).astype(bf).reshape(tn, quarter, model)
    grad_normed_one = reduce(pick(one_parts, t, t_steps, "tensor"), t_steps)
    qkv_grad = inner_rows(normed_one, grad_projected).astype(bf)
    _, pull_first = jax.vjp(rms_scale, x_own, gain_full[0])
    grad_x_norm, grad_gain_one = pull_first(grad_normed_one)
    input_own = grad_resid + grad_x_norm
    input_grad = place(gather(input_own, t_steps), t, t_steps, "tensor").reshape(slot, model)

    qkv_shard = reduce(
        pick(qkv_grad.reshape(dp, rows, width + kvt), me, dp_steps, "dp"), dp_steps
    )
    query_shard = qkv_shard[:, :width]
    keyval_shard = place(
        gather(qkv_shard[:, width:].astype(bf), t_steps), t, t_steps, "tensor", axis=1
    ).reshape(rows, tn * kvt).astype(fl)
    output_shard = reduce(
        pick(output_grad.reshape(width, dp, rows), me, dp_steps, "dp", axis=1), dp_steps
    )
    gains_grad = jnp.stack([grad_gain_one, grad_gain_two]).reshape(2, dp, rows)
    gains_parts = pick(gains_grad, me, dp_steps, "dp", axis=1)
    for step in reversed(dp_steps):
        half = gains_parts.shape[0] // 2
        gains_parts = gains_parts[:half] + swap(gains_parts[half:], step)
    gains_shard = gains_parts[0]
    for step in t_steps:
        gains_shard = gains_shard + swap(gains_shard, step)

    qa = adamw(w_query, query_shard, first_query, second_query, decay_rate)
    ka = adamw(w_keyval, keyval_shard, first_keyval, second_keyval, decay_rate)
    oa = adamw(w_output, output_shard, first_output, second_output, decay_rate)
    ga = adamw(w_gateup, gateup_shard, first_gateup, second_gateup, decay_rate)
    da = adamw(w_down, down_shard, first_down, second_down, decay_rate)
    na = adamw(norm_gains, gains_shard, first_gains, second_gains, 0.0)
    return (block_output, input_grad, *qa, *ka, *oa, *ga, *da, *na)


MESH = pl.DeviceIdType.MESH
ANY = pl.BlockSpec(memory_space=pl.ANY)
VMEM = pl.BlockSpec(memory_space=pltpu.VMEM)
LIMIT = 62 * 1024 * 1024


def position():
    me = lax.axis_index("dp")
    t = lax.axis_index("tensor")
    return me // 2, me % 2, t


def at_z(z, r, t, k):
    return ((z ^ k) * 2 + r, t)


def greet(partners):
    barrier = pltpu.get_barrier_semaphore()
    for device in partners:
        pl.semaphore_signal(barrier, inc=1, device_id=device, device_id_type=MESH)
    pl.semaphore_wait(barrier, len(partners))


class Copies:
    def __init__(self, send, recv):
        self.send, self.recv, self.made = send, recv, {}

    def start(self, name, src, dst, device):
        i = len(self.made)
        copy = pltpu.make_async_remote_copy(
            src_ref=src,
            dst_ref=dst,
            send_sem=self.send.at[i],
            recv_sem=self.recv.at[i],
            device_id=device,
            device_id_type=MESH,
        )
        copy.start()
        self.made[name] = copy

    def arrived(self, name):
        self.made[name].wait_recv()

    def left(self, name):
        self.made[name].wait_send()


def remote_params(number, limit=LIMIT):
    return pltpu.CompilerParams(
        collective_id=number, has_side_effects=True, vmem_limit_bytes=limit
    )


def block_rows(z, t, quarter):
    return pl.ds(pl.multiple_of((z * 4 + t) * quarter, quarter), quarter)


class TokenGather:
    count = 15

    def __init__(self, copies, own, out, tag):
        self.copies, self.own, self.out, self.tag = copies, own, out, tag
        self.z, self.r, self.t = position()
        self.quarter = own.shape[0]

    def rows(self, k, j):
        return self.out.at[block_rows(self.z ^ k, self.t ^ j, self.quarter)]

    def source(self, k, j):
        return self.own if k == 0 and j == 0 else self.rows(k, j)

    def send(self, name, k, j, device):
        self.copies.start(self.tag + name, self.source(k, j), self.rows(k, j), device)

    def send_z(self):
        self.send("z2", 0, 0, at_z(self.z, self.r, self.t, 2))
        self.send("z1", 0, 0, at_z(self.z, self.r, self.t, 1))

    def send_x(self, k):
        me = self.z * 2 + self.r
        self.send(f"x{k}", k, 0, (me, self.t ^ 2))
        self.send(f"c{k}0", k, 0, (me, self.t ^ 1))

    def take_z(self, k):
        self.copies.arrived(f"{self.tag}z{k}")
        if k == 2:
            self.send("z3", 2, 0, at_z(self.z, self.r, self.t, 1))
        self.send_x(k)

    def take_x(self, k):
        self.copies.arrived(f"{self.tag}x{k}")
        self.send(f"c{k}1", k, 2, (self.z * 2 + self.r, self.t ^ 1))

    def finish(self):
        for k in range(4):
            for j in range(2):
                self.copies.arrived(f"{self.tag}c{k}{j}")
        for name, copy in self.copies.made.items():
            if name.startswith(self.tag):
                copy.wait_send()


def partners_of(z, r, t, zs=(1, 2, 3), y=True, tensor=True):
    out = [at_z(z, r, t, k) for k in zs]
    if y:
        out.append((z * 2 + (r ^ 1), t))
    if tensor:
        out += [(z * 2 + r, t ^ 2), (z * 2 + r, t ^ 1)]
    return out


def gather_kernel(own, out, send, recv, local):
    z, r, t = position()
    keep = pltpu.make_async_copy(own, out.at[block_rows(z, t, own.shape[0])], local)
    keep.start()
    greet(partners_of(z, r, t, zs=(1, 2), y=False))
    g = TokenGather(Copies(send, recv), own, out, "n")
    g.send_z()
    g.send_x(0)
    g.take_z(1)
    g.take_z(2)
    g.take_x(0)
    g.take_z(3)
    for k in (1, 2, 3):
        g.take_x(k)
    g.finish()
    keep.wait()


def gather_tokens(own):
    quarter, model = own.shape
    n = TokenGather.count
    return pl.pallas_call(
        gather_kernel,
        out_shape=jax.ShapeDtypeStruct((16 * quarter, model), own.dtype),
        in_specs=[ANY],
        out_specs=ANY,
        scratch_shapes=[
            pltpu.SemaphoreType.DMA((n,)),
            pltpu.SemaphoreType.DMA((n,)),
            pltpu.SemaphoreType.DMA,
        ],
        compiler_params=remote_params(1),
        name="gather_tokens",
    )(own)


def weights_kernel(pack, three, dy, pack_out, three_out, dy_out, send, recv, local):
    z, r, t = position()
    rows = pack.shape[0]
    ff = three_out.shape[2]
    quarter = dy.shape[0]
    me = z * 2 + r
    other = (z * 2 + (r ^ 1), t)

    def rows_of(k):
        return pl.ds(pl.multiple_of(((z ^ k) * 2 + r) * rows, rows), rows)

    def cols_of(k):
        return pl.ds(pl.multiple_of((z ^ k) * ff, ff), ff)

    keeps = [
        pltpu.make_async_copy(pack, pack_out.at[rows_of(0)], local.at[0]),
        pltpu.make_async_copy(dy, dy_out.at[block_rows(z, t, quarter)], local.at[1]),
        pltpu.make_async_copy(three.at[:, :, cols_of(0)], three_out.at[:, rows_of(0)], local.at[2]),
    ]
    for keep in keeps:
        keep.start()
    greet(partners_of(z, r, t))
    copies = Copies(send, recv)
    g = TokenGather(copies, dy, dy_out, "d")

    def pack_send(name, k, device):
        src = pack if k == 0 else pack_out.at[rows_of(k)]
        copies.start(name, src, pack_out.at[rows_of(k)], device)

    pack_send("pz2", 0, at_z(z, r, t, 2))
    pack_send("pz1", 0, at_z(z, r, t, 1))
    pack_send("py0", 0, other)
    copies.arrived("pz1")
    pack_send("py1", 1, other)
    copies.arrived("pz2")
    pack_send("pz3", 2, at_z(z, r, t, 1))
    pack_send("py2", 2, other)
    g.send_x(0)
    copies.arrived("pz3")
    pack_send("py3", 3, other)

    for k in (2, 3, 1):
        for m in range(3):
            copies.start(
                f"wz{k}{m}",
                three.at[m, :, cols_of(k)],
                three_out.at[m, rows_of(0)],
                at_z(z, r, t, k),
            )
    g.send_z()

    def forward(k, m):
        src = three.at[m, :, cols_of(0)] if k == 0 else three_out.at[m, rows_of(k)]
        copies.start(f"wy{k}{m}", src, three_out.at[m, rows_of(k)], other)

    for m in range(3):
        forward(0, m)
    for m in range(3):
        copies.arrived(f"wz1{m}")
        forward(1, m)
    g.take_z(1)
    g.take_x(0)
    for m in range(3):
        copies.arrived(f"wz2{m}")
        forward(2, m)
    g.take_z(2)
    g.take_x(1)
    g.take_z(3)
    for m in range(3):
        copies.arrived(f"wz3{m}")
        forward(3, m)
    g.take_x(2)
    g.take_x(3)
    g.finish()
    for k in range(4):
        copies.arrived(f"py{k}")
        for m in range(3):
            copies.arrived(f"wy{k}{m}")
    for name, copy in copies.made.items():
        if not name.startswith("d"):
            copy.wait_send()
    for keep in keeps:
        keep.wait()


def gather_weights(pack, three, dy):
    rows, width = pack.shape
    n = 7 + 21 + TokenGather.count
    return pl.pallas_call(
        weights_kernel,
        out_shape=(
            jax.ShapeDtypeStruct((8 * rows, width), bf),
            jax.ShapeDtypeStruct((3, 8 * rows, three.shape[2] // ZN), bf),
            jax.ShapeDtypeStruct((16 * dy.shape[0], dy.shape[1]), bf),
        ),
        in_specs=[ANY] * 3,
        out_specs=(ANY,) * 3,
        scratch_shapes=[
            pltpu.SemaphoreType.DMA((n,)),
            pltpu.SemaphoreType.DMA((n,)),
            pltpu.SemaphoreType.DMA((3,)),
        ],
        compiler_params=remote_params(2),
        name="gather_weights",
    )(pack, three, dy)


ROOT = 0.7978845608028654
CUBE = 0.044715


def ff_kernel(
    nt_hbm, dy_hbm, w_hbm, hgu_hbm, sums,
    w, xin, hgu, sendc, recvc, sendx, kept, recvx, recvz,
    send, recv, load, wload, store,
):
    z, r, t = position()
    x, c = t // 2, t % 2
    me = z * 2 + r
    quarter = sums.shape[1]
    model, ff = w.shape[1], w.shape[2]
    tile = 256

    loads = [pltpu.make_async_copy(w_hbm.at[m], w.at[m], wload.at[m]) for m in range(3)]
    for copy in loads:
        copy.start()

    order = (1, 3, 2, 0)

    def rows(i, b):
        cc = c if i % 2 else c ^ 1
        xx = x if b else x ^ 1
        return block_rows(z ^ order[i // 2], xx * 2 + cc, quarter)

    def fetch(i):
        out = []
        for a, src in enumerate((nt_hbm, dy_hbm)):
            for b in range(2):
                copy = pltpu.make_async_copy(
                    src.at[rows(i, b)],
                    xin.at[i % 2, a, pl.ds(b * quarter, quarter)],
                    load.at[i % 2, a, b],
                )
                copy.start()
                out.append(copy)
        return out

    pending = fetch(0)
    greet(partners_of(z, r, t, zs=(1, 2), y=False))
    copies = Copies(send, recv)
    for copy in loads:
        copy.wait()

    def take_x(s):
        copies.arrived(f"x{s}")
        if s == 2:
            copies.arrived("z1")
        if s == 3:
            copies.arrived("z0")
            copies.arrived("z2")

        @pl.loop(0, model // tile)
        def _(n):
            cols = pl.ds(pl.multiple_of(n * tile, tile), tile)
            for a in range(2):
                total = kept[s, a, :, cols].astype(fl) + recvx[s, a, :, cols].astype(fl)
                if s == 2:
                    total += recvz[1, a, :, cols].astype(fl)
                if s == 3:
                    total += recvz[0, a, :, cols].astype(fl) + recvz[2, a, :, cols].astype(fl)
                    sums[a, :, cols] = total
                else:
                    recvx[s, a, :, cols] = total.astype(bf)

        if s < 3:
            copies.start(f"z{s}", recvx.at[s], recvz.at[s], at_z(z, r, t, 2 if s == 2 else 1))

    stores = {}
    for i in range(8):
        s, own = i // 2, i % 2
        for copy in pending:
            copy.wait()
        if i < 7:
            pending = fetch(i + 1)
        if i >= 2:
            for copy in stores[i - 2]:
                copy.wait()

        @pl.loop(0, ff // tile)
        def _(n):
            cols = pl.ds(pl.multiple_of(n * tile, tile), tile)
            gate = jnp.dot(xin[i % 2, 0], w[0, :, cols], preferred_element_type=fl)
            upper = jnp.dot(xin[i % 2, 0], w[1, :, cols], preferred_element_type=fl)
            dh = jnp.dot(xin[i % 2, 1], w[2, :, cols], preferred_element_type=fl)
            square = gate * gate
            bend = jnp.tanh(ROOT * gate * (1.0 + CUBE * square))
            half = 0.5 * (1.0 + bend)
            gelu = gate * half
            slope = half + 0.5 * gate * (1.0 - bend * bend) * (ROOT * (1.0 + 3.0 * CUBE * square))
            hgu[i % 2, 0, :, cols] = (gelu * upper).astype(bf)
            hgu[i % 2, 1, :, cols] = (dh * upper * slope).astype(bf)
            hgu[i % 2, 2, :, cols] = (dh * gelu).astype(bf)

        stores[i] = []
        for m in range(3):
            for b in range(2):
                copy = pltpu.make_async_copy(
                    hgu.at[i % 2, m, pl.ds(b * quarter, quarter)],
                    hgu_hbm.at[m, rows(i, b)],
                    store.at[i % 2, m, b],
                )
                copy.start()
                stores[i].append(copy)

        if own:
            copies.arrived(f"c{s}")
            if s >= 2:
                copies.left(f"x{s - 2}")
        elif s >= 1:
            copies.left(f"c{s - 1}")

        @pl.loop(0, model // tile)
        def _(n):
            cols = pl.ds(pl.multiple_of(n * tile, tile), tile)
            out = times_trans(hgu[i % 2, 0], w[2, cols])
            back = times_trans(hgu[i % 2, 1], w[0, cols]) + times_trans(hgu[i % 2, 2], w[1, cols])
            for a, part in enumerate((out, back)):
                if own:
                    total = part + recvc[s % 2, a, :, cols].astype(fl)
                    sendx[s % 2, a, :, cols] = total[:quarter].astype(bf)
                    kept[s, a, :, cols] = total[quarter:].astype(bf)
                else:
                    sendc[a, :, cols] = part.astype(bf)

        if own:
            copies.start(f"x{s}", sendx.at[s % 2], recvx.at[s], (me, t ^ 2))
            if s >= 2:
                take_x(s - 2)
        else:
            copies.start(f"c{s}", sendc, recvc.at[s % 2], (me, t ^ 1))

    take_x(2)
    take_x(3)
    for i in (6, 7):
        for copy in stores[i]:
            copy.wait()
    for name in ("c3", "x2", "x3", "z0", "z1", "z2"):
        copies.left(name)


def feed_forward(nt, dy, w):
    group, model = nt.shape
    ff = w.shape[2]
    quarter = group // 16
    return pl.pallas_call(
        ff_kernel,
        out_shape=(
            jax.ShapeDtypeStruct((3, group, ff), bf),
            jax.ShapeDtypeStruct((2, quarter, model), fl),
        ),
        in_specs=[ANY] * 3,
        out_specs=(ANY, VMEM),
        scratch_shapes=[
            pltpu.VMEM((3, model, ff), bf),
            pltpu.VMEM((2, 2, 2 * quarter, model), bf),
            pltpu.VMEM((2, 3, 2 * quarter, ff), bf),
            pltpu.VMEM((2, 2 * quarter, model), bf),
            pltpu.VMEM((2, 2, 2 * quarter, model), bf),
            pltpu.VMEM((2, 2, quarter, model), bf),
            pltpu.VMEM((4, 2, quarter, model), bf),
            pltpu.VMEM((4, 2, quarter, model), bf),
            pltpu.VMEM((3, 2, quarter, model), bf),
            pltpu.SemaphoreType.DMA((11,)),
            pltpu.SemaphoreType.DMA((11,)),
            pltpu.SemaphoreType.DMA((2, 2, 2)),
            pltpu.SemaphoreType.DMA((3,)),
            pltpu.SemaphoreType.DMA((2, 3, 2)),
        ],
        compiler_params=remote_params(3),
        name="feed_forward",
    )(nt, dy, w)


def grads_kernel(
    nt_hbm, dy_hbm, hgu_hbm, out,
    hgu, lhs, sendy, recvy, sendz,
    send, recv, load, hload, local,
):
    z, r, t = position()
    rows = lhs.shape[3]
    ff = hgu.shape[2]
    other = (z * 2 + (r ^ 1), t)

    loads = [pltpu.make_async_copy(hgu_hbm.at[m], hgu.at[m], hload.at[m]) for m in range(3)]
    zorder = (2, 3, 1, 0)

    def fetch(i):
        k, rr = zorder[i % 4], (r if i >= 4 else r ^ 1)
        cols = pl.ds(pl.multiple_of(((z ^ k) * 2 + rr) * rows, rows), rows)
        out = []
        for a, src in enumerate((nt_hbm, dy_hbm)):
            copy = pltpu.make_async_copy(src.at[:, cols], lhs.at[i % 2, a], load.at[i % 2, a])
            copy.start()
            out.append(copy)
        return out

    pending = fetch(0)
    for m in (1, 2, 0):
        loads[m].start()
    greet(partners_of(z, r, t, tensor=False))
    copies = Copies(send, recv)
    for i in range(8):
        k = zorder[i % 4]
        for copy in pending:
            copy.wait()
        if i < 7:
            pending = fetch(i + 1)
        for m, (h, a) in enumerate(((1, 0), (2, 0), (0, 1))):
            if i == 0:
                loads[h].wait()
            if i >= 4:
                copies.arrived(f"y{k}{m}")

            @pl.loop(0, ff // 512)
            def _(n):
                cols = pl.ds(pl.multiple_of(n * 512, 512), 512)
                grad = inner_rows(lhs[i % 2, a], hgu[h, :, cols])
                if i < 4:
                    sendy[i, m, :, cols] = grad.astype(bf)
                else:
                    sendz[i - 4, m, :, cols] = (grad + recvy[i - 4, m, :, cols].astype(fl)).astype(bf)

            if i < 4:
                copies.start(f"y{k}{m}", sendy.at[i, m], recvy.at[i, m], other)
            else:
                place = out.at[m, :, pl.ds(pl.multiple_of(z * ff, ff), ff)]
                if k:
                    copies.start(f"z{k}{m}", sendz.at[i - 4, m], place, at_z(z, r, t, k))
                else:
                    pltpu.make_async_copy(sendz.at[i - 4, m], place, local.at[m]).start()
    for m in range(3):
        place = out.at[m, :, pl.ds(pl.multiple_of(z * ff, ff), ff)]
        pltpu.make_async_copy(sendz.at[3, m], place, local.at[m]).wait()
        for k in range(1, 4):
            copies.arrived(f"z{k}{m}")
    for copy in copies.made.values():
        copy.wait_send()


def weight_grads(nt, dy, hgu):
    group, model = nt.shape
    ff = hgu.shape[2]
    rows = model // 8
    return pl.pallas_call(
        grads_kernel,
        out_shape=jax.ShapeDtypeStruct((3, rows, ZN * ff), bf),
        in_specs=[ANY] * 3,
        out_specs=ANY,
        scratch_shapes=[
            pltpu.VMEM((3, group, ff), bf),
            pltpu.VMEM((2, 2, group, rows), bf),
            pltpu.VMEM((4, 3, rows, ff), bf),
            pltpu.VMEM((4, 3, rows, ff), bf),
            pltpu.VMEM((4, 3, rows, ff), bf),
            pltpu.SemaphoreType.DMA((21,)),
            pltpu.SemaphoreType.DMA((21,)),
            pltpu.SemaphoreType.DMA((2, 2)),
            pltpu.SemaphoreType.DMA((3,)),
            pltpu.SemaphoreType.DMA((3,)),
        ],
        compiler_params=remote_params(4),
        name="weight_grads",
    )(nt, dy, hgu)


def fast(
    tokens,
    cotangent,
    lengths,
    w_query,
    w_keyval,
    w_output,
    w_gateup,
    w_down,
    norm_gains,
    first_query,
    first_keyval,
    first_output,
    first_gateup,
    first_down,
    first_gains,
    second_query,
    second_keyval,
    second_output,
    second_gateup,
    second_down,
    second_gains,
):
    dp = lax.axis_size("dp")
    tn = lax.axis_size("tensor")
    me = lax.axis_index("dp")
    t = lax.axis_index("tensor")
    dp_steps = [("dp", 4), ("dp", 2), ("dp", 1)]
    t_steps = [("tensor", 2), ("tensor", 1)]

    slot, model = tokens.shape
    rows = model // dp
    quarter = slot // tn
    width = w_query.shape[1]
    kvt = w_keyval.shape[1] // tn
    length = lengths[0]

    gain_full = place(
        gather(norm_gains.astype(bf), dp_steps), me, dp_steps, "dp", axis=1
    ).reshape(2, model).astype(fl)
    own_keyval = lax.dynamic_slice_in_dim(w_keyval, t * kvt, kvt, 1)
    pack = jnp.concatenate([w_query, own_keyval, w_output.T], axis=1).astype(bf)
    three = jnp.concatenate([w_gateup.astype(bf), w_down.astype(bf).T[None]], axis=0)
    cot_own = lax.dynamic_slice_in_dim(cotangent, t * quarter, quarter, 0)
    valid = (t * quarter + jnp.arange(quarter) < length)[:, None]
    grad_own = jnp.where(valid, cot_own, jnp.zeros_like(cot_own))
    pack, three, dy = gather_weights(pack, three, grad_own)
    qkv_w = pack[:, : width + kvt]
    output_t = pack[:, width + kvt :]

    x = tokens.astype(fl)
    normed_one = rms_scale(x, gain_full[0]).astype(bf)
    projected = dot(normed_one, qkv_w).astype(bf)
    query = projected[:, :width]
    keyval = place(
        gather(projected[:, width:], t_steps), t, t_steps, "tensor", axis=1
    ).reshape(slot, tn * kvt)
    mixed, logsum = slot_forward(query, keyval, length)
    mixed = mixed.astype(bf)
    attn_part = times_trans(mixed, output_t).astype(bf).reshape(tn, quarter, model)
    attn = reduce(pick(attn_part, t, t_steps, "tensor"), t_steps)
    x_own = lax.dynamic_slice_in_dim(x, t * quarter, quarter, 0)
    resid = x_own + attn
    normed_two = gather_tokens(rms_scale(resid, gain_full[1]).astype(bf))

    hgu, sums = feed_forward(normed_two, dy, three)
    out_own = resid + sums[0]
    block_output = place(gather(out_own, t_steps), t, t_steps, "tensor").reshape(slot, model)
    ff_grads = weight_grads(normed_two, dy, hgu)
    gateup_shard = ff_grads[:2].astype(fl)
    down_shard = ff_grads[2].T.astype(fl)

    _, pull_second = jax.vjp(rms_scale, resid, gain_full[1])
    grad_resid_norm, grad_gain_two = pull_second(sums[1].astype(bf).astype(fl))
    grad_resid = grad_own.astype(fl) + grad_resid_norm
    grad_attn = place(gather(grad_resid.astype(bf), t_steps), t, t_steps, "tensor").reshape(slot, model)

    grad_mixed = dot(grad_attn, output_t).astype(bf)
    grad_query, grad_keyval = slot_backward(query, keyval, length, logsum, grad_mixed)
    keyval_parts = grad_keyval.astype(bf).reshape(slot, tn, kvt)
    keyval_low = reduce(pick(keyval_parts, t, t_steps, "tensor", axis=1), t_steps).astype(bf)
    grad_projected = jnp.concatenate([grad_query.astype(bf), keyval_low], axis=1)
    one_parts = times_trans(grad_projected, qkv_w).astype(bf).reshape(tn, quarter, model)
    grad_normed_one = reduce(pick(one_parts, t, t_steps, "tensor"), t_steps)
    pack_grad = jnp.concatenate(
        [inner_rows(normed_one, grad_projected).astype(bf), inner_rows(grad_attn, mixed).astype(bf)], axis=1
    )
    _, pull_first = jax.vjp(rms_scale, x_own, gain_full[0])
    grad_x_norm, grad_gain_one = pull_first(grad_normed_one)
    input_own = grad_resid + grad_x_norm
    input_grad = place(gather(input_own, t_steps), t, t_steps, "tensor").reshape(slot, model)

    pack_shard = reduce(pick(pack_grad.reshape(dp, rows, -1), me, dp_steps, "dp"), dp_steps)
    query_shard = pack_shard[:, :width]
    keyval_shard = place(
        gather(pack_shard[:, width : width + kvt].astype(bf), t_steps), t, t_steps, "tensor", axis=1
    ).reshape(rows, tn * kvt).astype(fl)
    output_shard = pack_shard[:, width + kvt :].T
    gains_grad = jnp.stack([grad_gain_one, grad_gain_two]).reshape(2, dp, rows)
    gains_parts = pick(gains_grad, me, dp_steps, "dp", axis=1)
    for step in reversed(dp_steps):
        half = gains_parts.shape[0] // 2
        gains_parts = gains_parts[:half] + swap(gains_parts[half:], step)
    gains_shard = gains_parts[0]
    for step in t_steps:
        gains_shard = gains_shard + swap(gains_shard, step)

    qa = adamw(w_query, query_shard, first_query, second_query, decay_rate)
    ka = adamw(w_keyval, keyval_shard, first_keyval, second_keyval, decay_rate)
    oa = adamw(w_output, output_shard, first_output, second_output, decay_rate)
    ga = adamw(w_gateup, gateup_shard, first_gateup, second_gateup, decay_rate)
    da = adamw(w_down, down_shard, first_down, second_down, decay_rate)
    na = adamw(norm_gains, gains_shard, first_gains, second_gains, 0.0)
    return (block_output, input_grad, *qa, *ka, *oa, *ga, *da, *na)


def solution(mesh):
    query = P("dp", "tensor")
    keyval = P("dp", None)
    output = P("tensor", "dp")
    gateup = P(None, "dp", "tensor")
    gains = P(None, "dp")
    weights = (query, keyval, output, gateup, output, gains)
    return jax.shard_map(
        fast if mesh.shape["dp"] == 2 * ZN and mesh.shape["tensor"] == 4 else general,
        mesh=mesh,
        in_specs=(P("dp", None), P("dp", None), P("dp")) + weights * 3,
        out_specs=(P("dp", None), P("dp", None)) + tuple(w for w in weights for _ in range(4)),
        check_vma=False,
    )
```

```python
import functools

import jax
import jax.numpy as jnp
from jax import lax
from jax.experimental import pallas as pl
from jax.experimental.pallas import tpu as pltpu
from jax.sharding import PartitionSpec as P

HD = 256
ZN = 4

norm_eps = 1e-06
beta_first = 0.9
beta_second = 0.95
learn_rate = 0.01
decay_rate = 0.1
adam_eps = 1e-08
masked_score = -1e30

bf = jnp.bfloat16
fl = jnp.float32


def rms_scale(values, gain):
    inverse = lax.rsqrt(jnp.mean(values * values, axis=-1, keepdims=True) + norm_eps)
    return values * inverse * gain


def dot(left, right):
    return jnp.dot(left, right, preferred_element_type=fl)


def inner_rows(left, right):
    return lax.dot_general(left, right, (((0,), (0,)), ((), ())), preferred_element_type=fl)


def times_trans(left, right):
    return lax.dot_general(left, right, (((1,), (1,)), ((), ())), preferred_element_type=fl)


def slot_scores(query, keyval, length):
    slot = query.shape[0]
    heads = query.shape[1] // HD
    places = jnp.arange(slot)
    allowed = (places[None, :] <= places[:, None]) & (places[None, :] < length)
    raw = jnp.einsum(
        "qhd,kd->hqk",
        query.reshape(slot, heads, HD),
        keyval[:, :HD],
        preferred_element_type=fl,
    )
    return jnp.where(allowed[None], raw * HD ** (-0.5), masked_score)


def slot_forward(query, keyval, length):
    scores = slot_scores(query, keyval, length)
    top = jnp.max(scores, axis=-1, keepdims=True)
    expo = jnp.exp(scores - top)
    total = jnp.sum(expo, axis=-1, keepdims=True)
    probs = expo / total
    mixed = jnp.einsum(
        "hqk,kd->qhd", probs.astype(bf), keyval[:, HD:], preferred_element_type=fl
    )
    return mixed.reshape(query.shape), (top + jnp.log(total))[..., 0]


def slot_backward(query, keyval, length, logsum, grad_mixed):
    slot, width = query.shape
    heads = width // HD
    probs = jnp.exp(slot_scores(query, keyval, length) - logsum[..., None])
    grad_three = grad_mixed.reshape(slot, heads, HD)
    grad_value = jnp.einsum("hqk,qhd->kd", probs.astype(bf), grad_three, preferred_element_type=fl)
    grad_probs = jnp.einsum("qhd,kd->hqk", grad_three, keyval[:, HD:], preferred_element_type=fl)
    grad_scores = probs * (grad_probs - jnp.sum(grad_probs * probs, axis=-1, keepdims=True))
    grad_raw = (grad_scores * HD ** (-0.5)).astype(bf)
    grad_query = jnp.einsum("hqk,kd->qhd", grad_raw, keyval[:, :HD], preferred_element_type=fl)
    grad_key = jnp.einsum(
        "hqk,qhd->kd", grad_raw, query.reshape(slot, heads, HD), preferred_element_type=fl
    )
    return grad_query.reshape(slot, width), jnp.concatenate([grad_key, grad_value], axis=1)


def adamw(weight, grad, first, second, decay):
    first_new = beta_first * first + (1.0 - beta_first) * grad
    second_new = beta_second * second + (1.0 - beta_second) * grad * grad
    update = -learn_rate * (first_new / (jnp.sqrt(second_new) + adam_eps) + decay * weight)
    return (grad, first_new, second_new, update)


def swap(value, step):
    axis, bit = step
    return lax.ppermute(value, axis, [(i, i ^ bit) for i in range(lax.axis_size(axis))])


def offset(position, steps, axis):
    total = 0
    for i, (name, bit) in enumerate(steps):
        if name == axis and position >> i & 1:
            total ^= bit
    return total


def gather(value, steps):
    parts = value[None]
    for step in steps:
        parts = jnp.concatenate([parts, swap(parts, step)], axis=0)
    return parts


def reduce(parts, steps):
    for step in reversed(steps):
        half = parts.shape[0] // 2
        got = swap(parts[half:].astype(bf), step)
        parts = parts[:half].astype(fl) + got.astype(fl)
    return parts[0]


def take(array, index, axis=0):
    return lax.dynamic_index_in_dim(array, index, axis, keepdims=False)


def pick(array, me, steps, axis_name, axis=0):
    return jnp.stack(
        [take(array, me ^ offset(p, steps, axis_name), axis) for p in range(2 ** len(steps))]
    )


def place(parts, me, steps, axis_name, axis=0):
    count = parts.shape[0]
    block = parts.shape[1:]
    shape = block[:axis] + (count,) + block[axis:]
    out = jnp.zeros(shape, parts.dtype)
    for p in range(count):
        out = lax.dynamic_update_index_in_dim(
            out, parts[p], me ^ offset(p, steps, axis_name), axis
        )
    return out


def general(
    tokens,
    cotangent,
    lengths,
    w_query,
    w_keyval,
    w_output,
    w_gateup,
    w_down,
    norm_gains,
    first_query,
    first_keyval,
    first_output,
    first_gateup,
    first_down,
    first_gains,
    second_query,
    second_keyval,
    second_output,
    second_gateup,
    second_down,
    second_gains,
):
    dp = lax.axis_size("dp")
    tn = lax.axis_size("tensor")
    rn = dp // ZN
    me = lax.axis_index("dp")
    z, r = me // rn, me % rn
    t = lax.axis_index("tensor")
    z_steps = [("dp", 2 * rn), ("dp", rn)]
    r_steps = [("dp", 1 << i) for i in reversed(range(rn.bit_length() - 1))]
    t_steps = [("tensor", 1 << i) for i in reversed(range(tn.bit_length() - 1))]
    dp_steps = z_steps + r_steps
    group_steps = z_steps + t_steps

    model = tokens.shape[1]
    rows = model // dp
    slot = tokens.shape[0]
    quarter = slot // tn
    width = w_query.shape[1]
    kvt = w_keyval.shape[1] // tn
    ff = w_down.shape[0] // ZN

    gain_full = place(
        gather(norm_gains.astype(bf), dp_steps), me, dp_steps, "dp", axis=1
    ).reshape(2, model).astype(fl)
    own_keyval = lax.dynamic_slice_in_dim(w_keyval, t * kvt, kvt, 1)
    qkv_w = place(
        gather(jnp.concatenate([w_query, own_keyval], axis=1).astype(bf), dp_steps),
        me, dp_steps, "dp",
    ).reshape(model, width + kvt)
    output_w = place(
        gather(w_output.astype(bf), dp_steps), me, dp_steps, "dp", axis=1
    ).reshape(width, model)

    def zpos(k):
        return ("dp", k * rn)

    gateup_cols = w_gateup.astype(bf).reshape(2, rows, ZN, ff)
    down_rows = w_down.astype(bf).reshape(ZN, ff, rows)
    gateup_w = jnp.zeros((2, ZN, rn, rows, ff), bf)
    down_w = jnp.zeros((ff, ZN, rn, rows), bf)
    for k in range(ZN):
        block = take(gateup_cols, z ^ k, 2)
        if k:
            block = swap(block, zpos(k))
        block = place(gather(block, r_steps), r, r_steps, "dp", axis=1)
        gateup_w = lax.dynamic_update_index_in_dim(gateup_w, block, z ^ k, 1)
    for k in range(ZN):
        block = take(down_rows, z ^ k, 0)
        if k:
            block = swap(block, zpos(k))
        block = place(gather(block, r_steps), r, r_steps, "dp", axis=1)
        down_w = lax.dynamic_update_index_in_dim(down_w, block, z ^ k, 1)
    gateup_w = gateup_w.reshape(2, model, ff)
    down_w = down_w.reshape(ff, model)

    x = tokens.astype(fl)
    length = lengths[0]
    normed_one = rms_scale(x, gain_full[0]).astype(bf)
    projected = dot(normed_one, qkv_w).astype(bf)
    query = projected[:, :width]
    keyval = place(
        gather(projected[:, width:], t_steps), t, t_steps, "tensor", axis=1
    ).reshape(slot, tn * kvt)
    mixed, logsum = slot_forward(query, keyval, length)
    mixed = mixed.astype(bf)
    attn_part = dot(mixed, output_w).astype(bf).reshape(tn, quarter, model)
    attn = reduce(pick(attn_part, t, t_steps, "tensor"), t_steps)
    x_own = lax.dynamic_slice_in_dim(x, t * quarter, quarter, 0)
    resid = x_own + attn
    normed_two_own = rms_scale(resid, gain_full[1]).astype(bf)

    group = ZN * tn * quarter
    normed_two = gather(normed_two_own, group_steps).reshape(group, model)
    cot_own = lax.dynamic_slice_in_dim(cotangent, t * quarter, quarter, 0)
    valid = (t * quarter + jnp.arange(quarter) < length)[:, None]
    grad_own = jnp.where(valid, cot_own, jnp.zeros_like(cot_own))
    grad_low = gather(grad_own, group_steps).reshape(group, model)

    gate = dot(normed_two, gateup_w[0])
    upper = dot(normed_two, gateup_w[1])
    hidden = (jax.nn.gelu(gate, approximate=True) * upper).astype(bf)
    ff_part = dot(hidden, down_w).astype(bf).reshape(ZN * tn, quarter, model)
    out_own = resid + reduce(ff_part, group_steps)
    block_output = place(gather(out_own, t_steps), t, t_steps, "tensor").reshape(slot, model)

    grad_hidden = times_trans(grad_low, down_w)
    _, pull_gelu = jax.vjp(
        lambda left, right: jax.nn.gelu(left, approximate=True) * right, gate, upper
    )
    grad_gate, grad_up = pull_gelu(grad_hidden)
    grad_gate = grad_gate.astype(bf)
    grad_up = grad_up.astype(bf)
    grad_normed = (times_trans(grad_gate, gateup_w[0]) + times_trans(grad_up, gateup_w[1])).astype(bf)
    grad_normed_two = reduce(grad_normed.reshape(ZN * tn, quarter, model), group_steps)

    def columns(array, j):
        return take(array.reshape(group, ZN, rn, rows), r ^ j, 2).reshape(group, ZN * rows)

    def scatter_z(sums, axis):
        parts = []
        for k in range(ZN):
            block = take(sums, z ^ k, 0).astype(bf)
            parts.append(swap(block, zpos(k)) if k else block)
        shape = parts[0].shape
        out = jnp.zeros(shape[:axis] + (ZN,) + shape[axis:], bf)
        for k in range(ZN):
            out = lax.dynamic_update_index_in_dim(out, parts[k], z ^ k, axis)
        return out

    r_offsets = [offset(p, r_steps, "dp") for p in range(rn)]
    down_parts = jnp.stack(
        [
            inner_rows(hidden, columns(grad_low, j)).astype(bf).reshape(ff, ZN, rows)
            for j in r_offsets
        ]
    )
    down_sum = reduce(down_parts, r_steps)
    down_shard = scatter_z(jnp.moveaxis(down_sum, 1, 0), 0).reshape(ZN * ff, rows).astype(fl)

    shards_gu = []
    for grad in (grad_gate, grad_up):
        parts = jnp.stack(
            [
                inner_rows(columns(normed_two, j), grad).astype(bf).reshape(ZN, rows, ff)
                for j in r_offsets
            ]
        )
        sums = reduce(parts, r_steps)
        shards_gu.append(scatter_z(sums, 1).reshape(rows, ZN * ff).astype(fl))
    gateup_shard = jnp.stack(shards_gu)

    _, pull_second = jax.vjp(rms_scale, resid, gain_full[1])
    grad_resid_norm, grad_gain_two = pull_second(grad_normed_two)
    grad_resid = grad_own.astype(fl) + grad_resid_norm
    grad_attn = place(gather(grad_resid.astype(bf), t_steps), t, t_steps, "tensor").reshape(slot, model)

    output_grad = inner_rows(mixed, grad_attn).astype(bf)
    grad_mixed = times_trans(grad_attn, output_w).astype(bf)
    grad_query, grad_keyval = slot_backward(query, keyval, length, logsum, grad_mixed)
    keyval_parts = grad_keyval.astype(bf).reshape(slot, tn, kvt)
    keyval_low = reduce(pick(keyval_parts, t, t_steps, "tensor", axis=1), t_steps).astype(bf)
    grad_projected = jnp.concatenate([grad_query.astype(bf), keyval_low], axis=1)
    one_parts = times_trans(grad_projected, qkv_w).astype(bf).reshape(tn, quarter, model)
    grad_normed_one = reduce(pick(one_parts, t, t_steps, "tensor"), t_steps)
    qkv_grad = inner_rows(normed_one, grad_projected).astype(bf)
    _, pull_first = jax.vjp(rms_scale, x_own, gain_full[0])
    grad_x_norm, grad_gain_one = pull_first(grad_normed_one)
    input_own = grad_resid + grad_x_norm
    input_grad = place(gather(input_own, t_steps), t, t_steps, "tensor").reshape(slot, model)

    qkv_shard = reduce(
        pick(qkv_grad.reshape(dp, rows, width + kvt), me, dp_steps, "dp"), dp_steps
    )
    query_shard = qkv_shard[:, :width]
    keyval_shard = place(
        gather(qkv_shard[:, width:].astype(bf), t_steps), t, t_steps, "tensor", axis=1
    ).reshape(rows, tn * kvt).astype(fl)
    output_shard = reduce(
        pick(output_grad.reshape(width, dp, rows), me, dp_steps, "dp", axis=1), dp_steps
    )
    gains_grad = jnp.stack([grad_gain_one, grad_gain_two]).reshape(2, dp, rows)
    gains_parts = pick(gains_grad, me, dp_steps, "dp", axis=1)
    for step in reversed(dp_steps):
        half = gains_parts.shape[0] // 2
        gains_parts = gains_parts[:half] + swap(gains_parts[half:], step)
    gains_shard = gains_parts[0]
    for step in t_steps:
        gains_shard = gains_shard + swap(gains_shard, step)

    qa = adamw(w_query, query_shard, first_query, second_query, decay_rate)
    ka = adamw(w_keyval, keyval_shard, first_keyval, second_keyval, decay_rate)
    oa = adamw(w_output, output_shard, first_output, second_output, decay_rate)
    ga = adamw(w_gateup, gateup_shard, first_gateup, second_gateup, decay_rate)
    da = adamw(w_down, down_shard, first_down, second_down, decay_rate)
    na = adamw(norm_gains, gains_shard, first_gains, second_gains, 0.0)
    return (block_output, input_grad, *qa, *ka, *oa, *ga, *da, *na)


MESH = pl.DeviceIdType.MESH
ANY = pl.BlockSpec(memory_space=pl.ANY)
VMEM = pl.BlockSpec(memory_space=pltpu.VMEM)
LIMIT = 62 * 1024 * 1024
WINDOW = 4


def position():
    me = lax.axis_index("dp")
    t = lax.axis_index("tensor")
    return me // 2, me % 2, t


def at_z(z, r, t, k):
    return ((z ^ k) * 2 + r, t)


def greet(partners):
    barrier = pltpu.get_barrier_semaphore()
    for device in partners:
        pl.semaphore_signal(barrier, inc=1, device_id=device, device_id_type=MESH)
    pl.semaphore_wait(barrier, len(partners))


class Copies:
    def __init__(self, send, recv):
        self.send, self.recv, self.made, self.gone = send, recv, {}, set()

    def start(self, name, src, dst, device):
        i = len(self.made)
        self.made[name] = lambda: pltpu.make_async_remote_copy(
            src_ref=src() if callable(src) else src,
            dst_ref=dst() if callable(dst) else dst,
            send_sem=self.send.at[i],
            recv_sem=self.recv.at[i],
            device_id=device,
            device_id_type=MESH,
        )
        self.made[name]().start()

    def arrived(self, name):
        self.made[name]().wait_recv()

    def left(self, name):
        if name not in self.gone:
            self.gone.add(name)
            self.made[name]().wait_send()

    def all_left(self, keep=lambda name: True):
        for name in self.made:
            if keep(name):
                self.left(name)


def remote_params(number, limit=LIMIT):
    return pltpu.CompilerParams(
        collective_id=number, has_side_effects=True, vmem_limit_bytes=limit
    )


def block_rows(z, t, quarter):
    return pl.ds(pl.multiple_of((z * 4 + t) * quarter, quarter), quarter)


class TokenGather:
    count = 15

    def __init__(self, copies, own, out, tag):
        self.copies, self.own, self.out, self.tag = copies, own, out, tag
        self.z, self.r, self.t = position()
        self.quarter = own.shape[0]

    def rows(self, k, j):
        return self.out.at[block_rows(self.z ^ k, self.t ^ j, self.quarter)]

    def source(self, k, j):
        return self.own if k == 0 and j == 0 else self.rows(k, j)

    def send(self, name, k, j, device):
        self.copies.start(self.tag + name, self.source(k, j), self.rows(k, j), device)

    def send_z(self):
        self.send("z2", 0, 0, at_z(self.z, self.r, self.t, 2))
        self.send("z1", 0, 0, at_z(self.z, self.r, self.t, 1))

    def send_x(self, k):
        me = self.z * 2 + self.r
        self.send(f"x{k}", k, 0, (me, self.t ^ 2))
        self.send(f"c{k}0", k, 0, (me, self.t ^ 1))

    def take_z(self, k):
        self.copies.arrived(f"{self.tag}z{k}")
        if k == 2:
            self.send("z3", 2, 0, at_z(self.z, self.r, self.t, 1))
        self.send_x(k)

    def take_x(self, k):
        self.copies.arrived(f"{self.tag}x{k}")
        self.send(f"c{k}1", k, 2, (self.z * 2 + self.r, self.t ^ 1))

    def finish(self):
        for k in range(4):
            for j in range(2):
                self.copies.arrived(f"{self.tag}c{k}{j}")
        self.copies.all_left(lambda name: name.startswith(self.tag))


def partners_of(z, r, t, zs=(1, 2, 3), y=True, tensor=True):
    out = [at_z(z, r, t, k) for k in zs]
    if y:
        out.append((z * 2 + (r ^ 1), t))
    if tensor:
        out += [(z * 2 + r, t ^ 2), (z * 2 + r, t ^ 1)]
    return out


def rms_into(src, gain, dst, slab=16):
    @pl.loop(0, dst.shape[0] // slab)
    def _(i):
        rows = pl.ds(pl.multiple_of(i * slab, slab), slab)
        v = src[rows].astype(fl)
        inverse = lax.rsqrt(jnp.mean(v * v, axis=-1, keepdims=True) + norm_eps)
        dst[rows] = (v * inverse * gain).astype(bf)


def cast_into(src, dst, slab=16):
    @pl.loop(0, src.shape[0] // slab)
    def _(i):
        rows = pl.ds(pl.multiple_of(i * slab, slab), slab)
        dst[rows] = src[rows].astype(bf)


def probabilities(q, key, length, first):
    scores = times_trans(q, key) * HD ** (-0.5)
    row = first + lax.broadcasted_iota(jnp.int32, scores.shape, 0)
    col = lax.broadcasted_iota(jnp.int32, scores.shape, 1)
    scores = jnp.where((col <= row) & (col < length), scores, masked_score)
    expo = jnp.exp(scores - jnp.max(scores, axis=-1, keepdims=True))
    return expo / jnp.sum(expo, axis=-1, keepdims=True)


def forward_kernel(
    lengths, wq, wkv, wo, wgu, wd, gains, tokens, dy,
    gu_out, d_out, dy_out, nt_out, resid_out, one_out, q_out, kv_out, mixed_out, qkv_out, o_out, gain_out,
    wq_f, wkv_f, wo_f, gu_f, d_f, gu_b, d_b, x, qkv, o, gain, one, q, kv, mixed,
    part, recvc, sendx, recvx, resid, nt_own,
    send, recv, load, store,
):
    z, r, t = position()
    me = z * 2 + r
    rows = wq.shape[0]
    slot, model = tokens.shape
    quarter = dy.shape[0]
    width = wq.shape[1]
    kvt = qkv.shape[1] - width
    ff = d_out.shape[0]
    other = (z * 2 + (r ^ 1), t)
    x_peer, core_peer, far_peer = (me, t ^ 2), (me, t ^ 1), (me, t ^ 3)

    def d_block(k):
        return pl.ds(pl.multiple_of(((z ^ k) * 2 + r) * rows, rows), rows)

    def f_block(k):
        return pl.ds(pl.multiple_of((z ^ k) * ff, ff), ff)

    kv_cols = pl.ds(pl.multiple_of(t * kvt, kvt), kvt)
    loads = [
        pltpu.make_async_copy(wq, wq_f, load.at[0]),
        pltpu.make_async_copy(wkv.at[:, kv_cols], wkv_f, load.at[1]),
        pltpu.make_async_copy(wo, wo_f, load.at[2]),
        pltpu.make_async_copy(gains, gain.at[:, d_block(0)], load.at[3]),
        pltpu.make_async_copy(tokens, x, load.at[4]),
        pltpu.make_async_copy(wgu, gu_f, load.at[5]),
        pltpu.make_async_copy(wd, d_f, load.at[6]),
    ]
    for copy in loads:
        copy.start()
    stores = []

    def keep(src, dst):
        copy = pltpu.make_async_copy(src, dst, store.at[len(stores)])
        copy.start()
        stores.append(copy)

    keep(dy, dy_out.at[block_rows(z, t, quarter)])
    for copy in loads[:4]:
        copy.wait()

    @pl.loop(0, rows // 16)
    def _(i):
        own = pl.ds(pl.multiple_of(me * rows + i * 16, 16), 16)
        at = pl.ds(pl.multiple_of(i * 16, 16), 16)
        qkv[own, pl.ds(0, width)] = wq_f[at].astype(bf)
        qkv[own, pl.ds(width, kvt)] = wkv_f[at].astype(bf)

    @pl.loop(0, width // 16)
    def _(i):
        at = pl.ds(pl.multiple_of(i * 16, 16), 16)
        o[at, d_block(0)] = wo_f[at].astype(bf)

    greet(partners_of(z, r, t, zs=(1, 2, 3)) + [far_peer] + [((z ^ k) * 2 + (r ^ 1), t) for k in (1, 2, 3)])
    copies = Copies(send, recv)
    d = TokenGather(copies, dy, dy_out, "d")

    for k in range(4):
        for j in range(2):
            if k or j:
                copies.start(
                    f"g{k}{j}", gain.at[:, d_block(0)], gain.at[:, d_block(0)], ((z ^ k) * 2 + (r ^ j), t)
                )

    def pack_send(name, k, device):
        copies.start("q" + name, qkv.at[d_block(k)], qkv.at[d_block(k)], device)
        copies.start("o" + name, o.at[:, d_block(k)], o.at[:, d_block(k)], device)

    def pack_arrived(name):
        copies.arrived("q" + name)
        copies.arrived("o" + name)

    pack_send("z2", 0, at_z(z, r, t, 2))
    pack_send("z1", 0, at_z(z, r, t, 1))
    pack_send("y0", 0, other)
    d.send_z()
    d.send_x(0)

    for copy in loads[4:]:
        copy.wait()
    for m in range(2):
        cast_into(gu_f.at[m], gu_b.at[m])
    cast_into(d_f, d_b, 64)

    pieces = 2

    def owned(m, k, p):
        if m == 2:
            n = ff // pieces
            return d_b.at[pl.ds(pl.multiple_of((z ^ k) * ff + p * n, n), n)]
        n = rows // pieces
        return gu_b.at[m, p * n : (p + 1) * n, f_block(k)]

    def landed(m, k, p):
        if m == 2:
            n = ff // pieces
            return d_out.at[p * n : (p + 1) * n, d_block(k)]
        n = rows // pieces
        return gu_out.at[m, pl.ds(pl.multiple_of(((z ^ k) * 2 + r) * rows + p * n, n), n)]

    flows = [(m, k, p) for m in range(3) for k in (1, 3, 2) for p in range(pieces)]
    counts = [0, 0]

    def issue():
        if counts[0] < len(flows):
            m, k, p = flows[counts[0]]
            copies.start(f"wz{k}{m}{p}", owned(m, k, p), landed(m, 0, p), at_z(z, r, t, k))
            counts[0] += 1

    def forward(m, k, p):
        copies.start(f"wy{k}{m}{p}", owned(m, 0, p) if k == 0 else landed(m, k, p), landed(m, k, p), other)

    def pump(n, more=True):
        for _ in range(n):
            if counts[1] < counts[0]:
                m, k, p = flows[counts[1]]
                copies.arrived(f"wz{k}{m}{p}")
                forward(m, k, p)
                counts[1] += 1
            if more:
                issue()

    for _ in range(WINDOW):
        issue()
    for m in range(3):
        for p in range(pieces):
            keep(owned(m, 0, p), landed(m, 0, p))

    for k in range(4):
        for j in range(2):
            if k or j:
                copies.arrived(f"g{k}{j}")
    keep(gain, gain_out)
    rms_into(x, gain[0:1, :], one)
    keep(one, one_out)

    pack_arrived("z1")
    pack_send("y1", 1, other)
    pack_arrived("z2")
    pack_send("z3", 2, at_z(z, r, t, 1))
    pack_send("y2", 2, other)
    d.take_z(1)
    d.take_z(2)
    pack_arrived("z3")
    pack_send("y3", 3, other)
    pump(2)
    for k in range(4):
        pack_arrived(f"y{k}")
    for m in range(3):
        for p in range(pieces):
            forward(m, 0, p)
    keep(qkv, qkv_out)
    keep(o, o_out)

    kv[:, kv_cols] = dot(one[...], qkv[:, width:]).astype(bf)
    for name, peer in (("k1", core_peer), ("k2", x_peer), ("k3", far_peer)):
        copies.start(name, kv.at[:, kv_cols], kv.at[:, kv_cols], peer)
    q[...] = dot(one[...], qkv[:, :width]).astype(bf)
    keep(q, q_out)
    pump(1)
    for name in ("k1", "k2", "k3"):
        copies.arrived(name)
    keep(kv, kv_out)
    length = lengths[0]
    step = 128
    for h in range(width // HD):
        for i in range(slot // step):
            at, upto = pl.ds(i * step, step), pl.ds(0, (i + 1) * step)
            probs = probabilities(q[at, h * HD : (h + 1) * HD], kv[upto, :HD], length, i * step)
            mixed[at, h * HD : (h + 1) * HD] = dot(probs.astype(bf), kv[upto, HD:]).astype(bf)
        pump(1)
    keep(mixed, mixed_out)

    def part_of(j, store_part):
        at = pl.ds(pl.multiple_of((t ^ j) * quarter, quarter), quarter)
        for n in range(0, model, 512):
            store_part(dot(mixed[at], o[:, n : n + 512]), slice(n, n + 512))

    def into_part(i):
        def put(value, cols):
            part[i, :, cols] = value.astype(bf)

        return put

    part_of(3, into_part(0))
    part_of(1, into_part(1))
    copies.start("a1", part, recvc, core_peer)
    d.take_x(0)
    d.take_z(3)
    copies.arrived("a1")

    def into_x(value, cols):
        sendx[:, cols] = (value + recvc[0, :, cols].astype(fl)).astype(bf)

    part_of(2, into_x)
    copies.start("a2", sendx, recvx, x_peer)

    def into_resid(value, cols):
        resid[:, cols] = value + recvc[1, :, cols].astype(fl)

    part_of(0, into_resid)
    copies.arrived("a2")
    first_row = t * quarter

    @pl.loop(0, quarter // 16)
    def _(i):
        at = pl.ds(pl.multiple_of(i * 16, 16), 16)
        mine = pl.ds(pl.multiple_of(first_row + i * 16, 16), 16)
        v = x[mine].astype(fl) + (resid[at] + recvx[at].astype(fl))
        resid[at] = v
        inverse = lax.rsqrt(jnp.mean(v * v, axis=-1, keepdims=True) + norm_eps)
        nt_own[at] = (v * inverse * gain[1:2, :]).astype(bf)

    keep(resid, resid_out)
    keep(nt_own, nt_out.at[block_rows(z, t, quarter)])
    n = TokenGather(copies, nt_own, nt_out, "n")
    n.send_z()
    n.send_x(0)
    d.take_x(1)
    pump(WINDOW, more=False)
    n.take_z(1)
    n.take_z(2)
    for _ in range(WINDOW):
        issue()
    d.take_x(2)
    d.take_x(3)
    n.take_x(0)
    pump(2)
    n.take_z(3)
    n.take_x(1)
    pump(2)
    n.take_x(2)
    pump(2)
    n.take_x(3)
    pump(len(flows))
    n.finish()
    d.finish()
    for k in range(4):
        for m in range(3):
            for p in range(pieces):
                copies.arrived(f"wy{k}{m}{p}")
    copies.all_left(lambda name: name[0] not in "nd")
    for copy in stores:
        copy.wait()


def forward_part(lengths, wq, wkv, wo, wgu, wd, gains, tokens, dy):
    rows, width = wq.shape
    slot, model = tokens.shape
    quarter = dy.shape[0]
    kvt = wkv.shape[1] // 4
    ff = wd.shape[0] // ZN
    n = 7 + 14 + 42 + 3 + 2 + 2 * TokenGather.count
    shape = jax.ShapeDtypeStruct
    return pl.pallas_call(
        forward_kernel,
        out_shape=(
            shape((2, model, ff), bf),
            shape((ff, model), bf),
            shape((16 * quarter, model), bf),
            shape((16 * quarter, model), bf),
            shape((quarter, model), fl),
            shape((slot, model), bf),
            shape((slot, width), bf),
            shape((slot, 4 * kvt), bf),
            shape((slot, width), bf),
            shape((model, width + kvt), bf),
            shape((width, model), bf),
            shape((8, model), fl),
        ),
        in_specs=[pl.BlockSpec(memory_space=pltpu.SMEM)] + [ANY] * 8,
        out_specs=(ANY,) * 12,
        scratch_shapes=[
            pltpu.VMEM((rows, width), fl),
            pltpu.VMEM((rows, kvt), fl),
            pltpu.VMEM((width, rows), fl),
            pltpu.VMEM(wgu.shape, fl),
            pltpu.VMEM(wd.shape, fl),
            pltpu.VMEM(wgu.shape, bf),
            pltpu.VMEM(wd.shape, bf),
            pltpu.VMEM((slot, model), bf),
            pltpu.VMEM((model, width + kvt), bf),
            pltpu.VMEM((width, model), bf),
            pltpu.VMEM((8, model), fl),
            pltpu.VMEM((slot, model), bf),
            pltpu.VMEM((slot, width), bf),
            pltpu.VMEM((slot, 4 * kvt), bf),
            pltpu.VMEM((slot, width), bf),
            pltpu.VMEM((2, quarter, model), bf),
            pltpu.VMEM((2, quarter, model), bf),
            pltpu.VMEM((quarter, model), bf),
            pltpu.VMEM((quarter, model), bf),
            pltpu.VMEM((quarter, model), fl),
            pltpu.VMEM((quarter, model), bf),
            pltpu.SemaphoreType.DMA((n,)),
            pltpu.SemaphoreType.DMA((n,)),
            pltpu.SemaphoreType.DMA((7,)),
            pltpu.SemaphoreType.DMA((16,)),
        ],
        compiler_params=remote_params(1),
        name="forward_part",
    )(lengths, wq, wkv, wo, wgu, wd, gains, tokens, dy)


ROOT = 0.7978845608028654
CUBE = 0.044715


def ff_kernel(
    nt_hbm, dy_hbm, gu_hbm, d_hbm, hgu_hbm, sums,
    wgu, wd, dots, xin, hgu, sendc, recvc, sendx, kept, recvx, recvz,
    send, recv, load, wload, store,
):
    z, r, t = position()
    x, c = t // 2, t % 2
    me = z * 2 + r
    quarter = sums.shape[1]
    ff, model = wd.shape
    tile = 256
    wide = 1024

    loads = [pltpu.make_async_copy(gu_hbm.at[m], wgu.at[m], wload.at[m]) for m in range(2)]
    loads.append(pltpu.make_async_copy(d_hbm, wd, wload.at[2]))
    for copy in loads:
        copy.start()

    order = (3, 2, 1, 0)

    def rows(i, b):
        cc = c if i % 2 else c ^ 1
        xx = x if b else x ^ 1
        return block_rows(z ^ order[i // 2], xx * 2 + cc, quarter)

    def fetch(i):
        out = []
        for a, src in enumerate((nt_hbm, dy_hbm)):
            for b in range(2):
                copy = pltpu.make_async_copy(
                    src.at[rows(i, b)],
                    xin.at[i % 2, a, pl.ds(b * quarter, quarter)],
                    load.at[i % 2, a, b],
                )
                copy.start()
                out.append(copy)
        return out

    pending = fetch(0)
    greet(partners_of(z, r, t, zs=(1, 2), y=False))
    copies = Copies(send, recv)
    for copy in loads:
        copy.wait()

    def take_x(s):
        copies.arrived(f"x{s}")
        if s == 1:
            copies.arrived("z0")
        if s == 3:
            copies.arrived("z2")
            copies.arrived("z1")

        @pl.loop(0, model // tile)
        def _(n):
            cols = pl.ds(pl.multiple_of(n * tile, tile), tile)
            for a in range(2):
                total = kept[s, a, :, cols].astype(fl) + recvx[s, a, :, cols].astype(fl)
                if s == 1:
                    total += recvz[0, a, :, cols].astype(fl)
                if s == 3:
                    total += recvz[1, a, :, cols].astype(fl) + recvz[2, a, :, cols].astype(fl)
                    sums[a, :, cols] = total
                else:
                    recvx[s, a, :, cols] = total.astype(bf)

        if s < 3:
            copies.start(f"z{s}", recvx.at[s], recvz.at[s], at_z(z, r, t, 2 if s == 1 else 1))

    stores = {}
    for i in range(8):
        s, own = i // 2, i % 2
        for copy in pending:
            copy.wait()
        if i < 7:
            pending = fetch(i + 1)
        if i >= 2:
            for copy in stores[i - 2]:
                copy.wait()

        dots[0] = dot(xin[i % 2, 0], wgu[0])
        dots[1] = dot(xin[i % 2, 0], wgu[1])
        dots[2] = times_trans(xin[i % 2, 1], wd[...])

        @pl.loop(0, 2 * quarter // 16)
        def _(n):
            at = pl.ds(pl.multiple_of(n * 16, 16), 16)
            for half in range(0, ff, 512):
                cols = slice(half, half + 512)
                gate, upper, dh = dots[0, at, cols], dots[1, at, cols], dots[2, at, cols]
                square = gate * gate
                bend = jnp.tanh(ROOT * gate * (1.0 + CUBE * square))
                share = 0.5 * (1.0 + bend)
                gelu = gate * share
                slope = share + 0.5 * gate * (1.0 - bend * bend) * (ROOT * (1.0 + 3.0 * CUBE * square))
                hgu[i % 2, 0, at, cols] = (gelu * upper).astype(bf)
                hgu[i % 2, 1, at, cols] = (dh * upper * slope).astype(bf)
                hgu[i % 2, 2, at, cols] = (dh * gelu).astype(bf)

        stores[i] = []
        for m in range(3):
            for b in range(2):
                copy = pltpu.make_async_copy(
                    hgu.at[i % 2, m, pl.ds(b * quarter, quarter)],
                    hgu_hbm.at[m, rows(i, b)],
                    store.at[i % 2, m, b],
                )
                copy.start()
                stores[i].append(copy)

        if own:
            copies.arrived(f"c{s}")
            if s >= 2:
                copies.left(f"x{s - 2}")
        elif s >= 1:
            copies.left(f"c{s - 1}")

        @pl.loop(0, model // wide)
        def _(n):
            cols = pl.ds(pl.multiple_of(n * wide, wide), wide)
            out = dot(hgu[i % 2, 0], wd[:, cols])
            back = times_trans(hgu[i % 2, 1], wgu[0, cols]) + times_trans(hgu[i % 2, 2], wgu[1, cols])
            for a, part in enumerate((out, back)):
                if own:
                    total = part + recvc[s % 2, a, :, cols].astype(fl)
                    sendx[s % 2, a, :, cols] = total[:quarter].astype(bf)
                    kept[s, a, :, cols] = total[quarter:].astype(bf)
                else:
                    sendc[a, :, cols] = part.astype(bf)

        if own:
            copies.start(f"x{s}", sendx.at[s % 2], recvx.at[s], (me, t ^ 2))
            if s >= 2:
                take_x(s - 2)
        else:
            copies.start(f"c{s}", sendc, recvc.at[s % 2], (me, t ^ 1))

    take_x(2)
    take_x(3)
    for i in (6, 7):
        for copy in stores[i]:
            copy.wait()
    for name in ("c3", "x2", "x3", "z0", "z1", "z2"):
        copies.left(name)


def feed_forward(nt, dy, wgu, wd):
    group, model = nt.shape
    ff = wd.shape[0]
    quarter = group // 16
    return pl.pallas_call(
        ff_kernel,
        out_shape=(
            jax.ShapeDtypeStruct((3, group, ff), bf),
            jax.ShapeDtypeStruct((2, quarter, model), fl),
        ),
        in_specs=[ANY] * 4,
        out_specs=(ANY, VMEM),
        scratch_shapes=[
            pltpu.VMEM((2, model, ff), bf),
            pltpu.VMEM((ff, model), bf),
            pltpu.VMEM((3, 2 * quarter, ff), fl),
            pltpu.VMEM((2, 2, 2 * quarter, model), bf),
            pltpu.VMEM((2, 3, 2 * quarter, ff), bf),
            pltpu.VMEM((2, 2 * quarter, model), bf),
            pltpu.VMEM((2, 2, 2 * quarter, model), bf),
            pltpu.VMEM((2, 2, quarter, model), bf),
            pltpu.VMEM((4, 2, quarter, model), bf),
            pltpu.VMEM((4, 2, quarter, model), bf),
            pltpu.VMEM((3, 2, quarter, model), bf),
            pltpu.SemaphoreType.DMA((11,)),
            pltpu.SemaphoreType.DMA((11,)),
            pltpu.SemaphoreType.DMA((2, 2, 2)),
            pltpu.SemaphoreType.DMA((3,)),
            pltpu.SemaphoreType.DMA((2, 3, 2)),
        ],
        compiler_params=remote_params(3),
        name="feed_forward",
    )(nt, dy, wgu, wd)


def backward_kernel(
    lengths, nt_hbm, dy_hbm, hgu_hbm, sums, resid, dy_own, x_own, gain, one_hbm, q_hbm, kv_hbm, mixed_hbm, qkv_hbm, o_hbm,
    gu_out, d_out, qkv_grad, kv_grad, o_grad, block_out, input_out, gains_out,
    sendy_gu, sendy_d, recvy_gu, recvy_d, own_gu, own_d,
    a, d_resid, out_own, gacc, grecv, gmine, grecv_t,
    gp, dkv_send, dkv_recv, dkv_x, dkv_rx, part, precv, sendx, recvx,
    pk_send, po_send, pk_recv, po_recv, pk_own, po_own, pk_z, po_z,
    send, recv, load, local,
):
    z, r, t = position()
    me = z * 2 + r
    quarter, model = resid.shape
    slot = 4 * quarter
    rows = model // 8
    ff = own_d.shape[1]
    kvt = dkv_x.shape[1]
    width = gp.shape[1] - kvt
    other = (z * 2 + (r ^ 1), t)
    x_peer, core_peer, far_peer = (me, t ^ 2), (me, t ^ 1), (me, t ^ 3)

    def d_block(k, j=0):
        return pl.ds(pl.multiple_of(((z ^ k) * 2 + (r ^ j)) * rows, rows), rows)

    def own_rows(j):
        return pl.ds(pl.multiple_of((t ^ j) * quarter, quarter), quarter)

    loads = [
        pltpu.make_async_copy(sums.at[1], d_resid, load.at[0]),
        pltpu.make_async_copy(sums.at[0], out_own, load.at[1]),
    ]
    for copy in loads:
        copy.start()
    greet(partners_of(z, r, t, zs=(1, 2, 3)) + [far_peer] + [((z ^ k) * 2 + (r ^ 1), t) for k in (1, 2, 3)])
    copies = Copies(send, recv)
    locals_ = []
    counter = list(range(8))

    def keep(src, dst):
        copy = pltpu.make_async_copy(src, dst, local.at[counter.pop(0)])
        copy.start()
        locals_.append(copy)
        return copy

    def norm_back(v, grad, row):
        inverse = lax.rsqrt(jnp.mean(v * v, axis=-1, keepdims=True) + norm_eps)
        scaled = v * inverse
        gacc[row : row + 1, :] += jnp.sum(grad * scaled, axis=0, keepdims=True)
        inner = grad * gain[row : row + 1, :]
        return inverse * (inner - scaled * jnp.mean(inner * scaled, axis=-1, keepdims=True))

    gacc[...] = jnp.zeros_like(gacc)
    for copy in loads:
        copy.wait()

    @pl.loop(0, quarter // 16)
    def _(i):
        at = pl.ds(pl.multiple_of(i * 16, 16), 16)
        mine = pl.ds(pl.multiple_of(t * quarter + i * 16, 16), 16)
        v = resid[at]
        total = dy_own[at].astype(fl) + norm_back(v, d_resid[at], 1)
        d_resid[at] = total
        a[mine] = total.astype(bf)
        out_own[at] += v

    copies.start("ax", a.at[own_rows(0)], a.at[own_rows(0)], x_peer)
    copies.start("ac", a.at[own_rows(0)], a.at[own_rows(0)], core_peer)
    keep(out_own, block_out.at[own_rows(0)])
    in_own = out_own
    copies.start("bx", out_own, block_out.at[own_rows(0)], x_peer)
    copies.start("bc", out_own, block_out.at[own_rows(0)], core_peer)

    zorder = (1, 3, 2, 0)

    def send_y(i):
        k = zorder[i]
        for m in range(2):
            copies.start(f"y{k}{m}", lambda m=m: sendy_gu.at[i, m], lambda m=m: recvy_gu.at[i, m], other)
        copies.start(f"y{k}2", lambda: sendy_d.at[i], lambda: recvy_d.at[i], other)

    def feed_forward_grads(hgu, lhs):
        loads = [pltpu.make_async_copy(hgu_hbm.at[m], hgu.at[m], load.at[m]) for m in range(3)]

        def fetch(i):
            cols = d_block(zorder[i % 4], 0 if i >= 4 else 1)
            made = []
            for n, src in enumerate((nt_hbm, dy_hbm)):
                copy = pltpu.make_async_copy(src.at[:, cols], lhs.at[i % 2, n], load.at[3 + 2 * (i % 2) + n])
                copy.start()
                made.append(copy)
            return made

        pending = fetch(0)
        for m in (1, 2, 0):
            loads[m].start()
        for i in range(8):
            for copy in pending:
                copy.wait()
            if i < 7:
                pending = fetch(i + 1)
            to_gu, to_d = (sendy_gu, sendy_d) if i < 4 else (own_gu, own_d)
            for m, (h, n) in enumerate(((1, 0), (2, 0), (0, 1))):
                if i == 0:
                    loads[h].wait()

                @pl.loop(0, ff // 512)
                def _(c):
                    cols = pl.ds(pl.multiple_of(c * 512, 512), 512)
                    grad = inner_rows(lhs[i % 2, n], hgu[h, :, cols])
                    if m < 2:
                        to_gu[i % 4, m, :, cols] = grad.astype(bf)
                    else:
                        to_d[i % 4, cols, :] = grad.T.astype(bf)

            if i < 3:
                send_y(i)

    group = nt_hbm.shape[0]
    pl.run_scoped(
        feed_forward_grads, pltpu.VMEM((3, group, ff), bf), pltpu.VMEM((2, 2, group, rows), bf)
    )

    flows = [(i, m) for i in range(3) for m in range(3)]
    taken = [0]

    def own_of(i, m):
        return own_d.at[i] if m == 2 else own_gu.at[i, m]

    def add_y(i, m):
        mine, theirs = own_of(i, m), (recvy_d.at[i] if m == 2 else recvy_gu.at[i, m])

        @pl.loop(0, mine.shape[0] // 64)
        def _(n):
            at = pl.ds(pl.multiple_of(n * 64, 64), 64)
            mine[at] = (mine[at].astype(fl) + theirs[at].astype(fl)).astype(bf)

    def place(m):
        cols = pl.ds(pl.multiple_of(z * ff, ff), ff)
        return d_out.at[cols] if m == 2 else gu_out.at[m, :, cols]

    at_zs = [at_z(z, r, t, k) for k in range(4)]

    def pump(n):
        for _ in range(n):
            if taken[0] < len(flows):
                i, m = flows[taken[0]]
                k = zorder[i]
                copies.arrived(f"y{k}{m}")
                add_y(i, m)
                copies.start(f"z{k}{m}", lambda i=i, m=m: own_of(i, m), lambda m=m: place(m), at_zs[k])
                taken[0] += 1

    pump(3)
    copies.arrived("ax")
    copies.start("af", a.at[own_rows(2)], a.at[own_rows(2)], core_peer)
    copies.arrived("bx")
    copies.start("bf", block_out.at[own_rows(2)], block_out.at[own_rows(2)], core_peer)

    def attention(q, kv, mixed, qkv, o, one, dm, dkv):
        loads = [
            pltpu.make_async_copy(src, dst, load.at[i])
            for i, (src, dst) in enumerate(
                ((o_hbm, o), (q_hbm, q), (kv_hbm, kv), (mixed_hbm, mixed), (qkv_hbm, qkv), (one_hbm, one))
            )
        ]
        for copy in loads:
            copy.start()
        copies.arrived("ac")
        copies.arrived("af")
        for copy in loads:
            copy.wait()
        dm[...] = times_trans(a[...], o[...]).astype(bf)
        length = lengths[0]
        step = 128
        dkv[...] = jnp.zeros_like(dkv)
        for h in range(width // HD):
            head = slice(h * HD, (h + 1) * HD)
            for i in range(slot // step):
                at, upto = pl.ds(i * step, step), pl.ds(0, (i + 1) * step)
                probs = probabilities(q[at, head], kv[upto, :HD], length, i * step)
                d_probs = times_trans(dm[at, head], kv[upto, HD:])
                d_scores = probs * (d_probs - jnp.sum(d_probs * probs, axis=-1, keepdims=True))
                d_raw = (d_scores * HD ** (-0.5)).astype(bf)
                gp[at, head] = dot(d_raw, kv[upto, :HD]).astype(bf)
                dkv[upto, :HD] += inner_rows(d_raw, q[at, head])
                dkv[upto, HD:] += inner_rows(probs.astype(bf), dm[at, head])
            pump(1)

        def kv_cols(j):
            return pl.ds(pl.multiple_of((t ^ j) * kvt, kvt), kvt)

        dkv_send[0] = dkv[:, kv_cols(1)].astype(bf)
        dkv_send[1] = dkv[:, kv_cols(3)].astype(bf)
        copies.start("kc", lambda: dkv_send, lambda: dkv_recv, core_peer)
        copies.arrived("kc")
        dkv_x[...] = (dkv[:, kv_cols(2)] + dkv_recv[1].astype(fl)).astype(bf)
        copies.start("kx", lambda: dkv_x, lambda: dkv_rx, x_peer)
        mine = dkv[:, kv_cols(0)] + dkv_recv[0].astype(fl)
        copies.arrived("kx")
        gp[:, width:] = (mine + dkv_rx[...].astype(fl)).astype(bf)

        def part_of(j, store_part):
            at = own_rows(j)
            for n in range(0, model, 512):
                store_part(times_trans(gp[at], qkv[n : n + 512]), slice(n, n + 512))

        def into_part(i):
            def put(value, cols):
                part[i, :, cols] = value.astype(bf)

            return put

        part_of(3, into_part(0))
        part_of(1, into_part(1))
        copies.start("pc", lambda: part, lambda: precv, core_peer)

        def pack_grads(k, j, to_k, to_o):
            cols = d_block(k, j)
            to_k[...] = inner_rows(one[:, cols], gp[...]).astype(to_k.dtype)
            to_o[...] = inner_rows(mixed[...], a[:, cols]).astype(to_o.dtype)

        for i, k in enumerate(zorder):
            pack_grads(k, 1, pk_send.at[i], po_send.at[i])
            copies.start(f"yp{k}", lambda i=i: pk_send.at[i], lambda i=i: pk_recv.at[i], other)
            copies.start(f"yo{k}", lambda i=i: po_send.at[i], lambda i=i: po_recv.at[i], other)
        send_y(3)

        copies.arrived("pc")

        def into_x(value, cols):
            sendx[:, cols] = (value + precv[0, :, cols].astype(fl)).astype(bf)

        part_of(2, into_x)
        copies.start("px", lambda: sendx, lambda: recvx, x_peer)

        copies.left("bx")
        copies.left("bc")
        locals_.pop(0).wait()

        def into_own(value, cols):
            in_own[:, cols] = value + precv[1, :, cols].astype(fl)

        part_of(0, into_own)
        for i, k in enumerate(zorder):
            pack_grads(k, 0, pk_own.at[i], po_own.at[i])
        copies.arrived("px")

    pl.run_scoped(
        attention,
        pltpu.VMEM((slot, width), bf),
        pltpu.VMEM((slot, 2 * HD), bf),
        pltpu.VMEM((slot, width), bf),
        pltpu.VMEM((model, width + kvt), bf),
        pltpu.VMEM((width, model), bf),
        pltpu.VMEM((slot, model), bf),
        pltpu.VMEM((slot, width), bf),
        pltpu.VMEM((slot, 2 * HD), fl),
    )

    @pl.loop(0, quarter // 16)
    def _(i):
        at = pl.ds(pl.multiple_of(i * 16, 16), 16)
        grad = in_own[at] + recvx[at].astype(fl)
        in_own[at] = d_resid[at] + norm_back(x_own[at].astype(fl), grad, 0)

    keep(in_own, input_out.at[own_rows(0)])
    copies.start("ix", in_own, input_out.at[own_rows(0)], x_peer)
    copies.start("ic", in_own, input_out.at[own_rows(0)], core_peer)

    for k in range(4):
        for j in range(2):
            if k or j:
                copies.start(
                    f"g{k}{j}", gacc.at[:, d_block(k, j)], grecv.at[2 * k + j], ((z ^ k) * 2 + (r ^ j), t)
                )
    pump(9)

    def add_pack(i):
        k = zorder[i]
        copies.arrived(f"yp{k}")
        copies.arrived(f"yo{k}")
        for mine, theirs in ((pk_own.at[i], pk_recv.at[i]), (po_own.at[i], po_recv.at[i])):
            mine[...] = (mine[...].astype(fl) + theirs[...].astype(fl)).astype(mine.dtype)

    for i in range(3):
        add_pack(i)
        k = zorder[i]
        copies.start(f"zp{k}", pk_own.at[i], pk_z.at[i], at_z(z, r, t, k))
        copies.start(f"zo{k}", po_own.at[i], po_z.at[i], at_z(z, r, t, k))
    add_pack(3)
    total = gacc[:, d_block(0)]
    for k in range(4):
        for j in range(2):
            if k or j:
                copies.arrived(f"g{k}{j}")
                total += grecv[2 * k + j]
    gmine[...] = total
    for j, peer in ((1, core_peer), (2, x_peer), (3, far_peer)):
        copies.start(f"gt{j}", gmine, grecv_t.at[j], peer)
    copies.arrived("ix")
    copies.start("if", input_out.at[own_rows(2)], input_out.at[own_rows(2)], core_peer)

    for m in range(3):
        copies.arrived(f"y0{m}")
        add_y(3, m)
        keep(own_of(3, m), place(m))
    for i in range(3):
        copies.arrived(f"zp{zorder[i]}")
        copies.arrived(f"zo{zorder[i]}")
    pk_sum = pk_own[3].astype(fl)
    po_sum = po_own[3].astype(fl)
    for i in range(3):
        pk_sum += pk_z[i].astype(fl)
        po_sum += po_z[i].astype(fl)
    qkv_grad[...] = pk_sum
    o_grad[...] = po_sum
    mine = pl.ds(pl.multiple_of(t * kvt, kvt), kvt)
    kv_grad[:, mine] = pk_sum[:, width:]
    for j, peer in ((1, core_peer), (2, x_peer), (3, far_peer)):
        copies.start(f"kg{j}", kv_grad.at[:, mine], kv_grad.at[:, mine], peer)
    total = gmine[...]
    for j in (1, 2, 3):
        copies.arrived(f"gt{j}")
        total += grecv_t[j]
    gains_out[...] = total
    for name in ("ic", "if", "bc", "bf", "kg1", "kg2", "kg3"):
        copies.arrived(name)
    for i in range(3):
        for m in range(3):
            copies.arrived(f"z{zorder[i]}{m}")
    copies.all_left()
    for copy in locals_:
        copy.wait()


def backward_part(lengths, nt, dy, hgu, sums, resid, dy_own, x_own, gain, one, q, kv, mixed, qkv, o):
    group, model = nt.shape
    ff = hgu.shape[2]
    rows = model // 8
    quarter = resid.shape[0]
    slot, width = q.shape
    kvt = qkv.shape[1] - width
    n = 2 + 2 + 2 + 12 + 9 + 2 + 8 + 2 + 3 + 7 + 6 + 3 + 3
    shape = jax.ShapeDtypeStruct
    buf = pltpu.VMEM
    return pl.pallas_call(
        backward_kernel,
        out_shape=(
            shape((2, rows, ZN * ff), bf),
            shape((ZN * ff, rows), bf),
            shape((rows, width + kvt), fl),
            shape((rows, 4 * kvt), fl),
            shape((width, rows), fl),
            shape((slot, model), fl),
            shape((slot, model), fl),
            shape((8, rows), fl),
        ),
        in_specs=[pl.BlockSpec(memory_space=pltpu.SMEM)] + [ANY] * 4 + [VMEM] * 4 + [ANY] * 6,
        out_specs=(ANY, ANY, VMEM, VMEM, VMEM, ANY, ANY, VMEM),
        scratch_shapes=[
            buf((4, 2, rows, ff), bf), buf((4, ff, rows), bf),
            buf((4, 2, rows, ff), bf), buf((4, ff, rows), bf),
            buf((4, 2, rows, ff), bf), buf((4, ff, rows), bf),
            buf((slot, model), bf), buf((quarter, model), fl), buf((quarter, model), fl),
            buf((8, model), fl), buf((8, 8, rows), fl), buf((8, rows), fl), buf((4, 8, rows), fl),
            buf((slot, width + kvt), bf), buf((2, slot, kvt), bf), buf((2, slot, kvt), bf),
            buf((slot, kvt), bf), buf((slot, kvt), bf),
            buf((2, quarter, model), bf), buf((2, quarter, model), bf),
            buf((quarter, model), bf), buf((quarter, model), bf),
            buf((4, rows, width + kvt), bf), buf((4, width, rows), bf),
            buf((4, rows, width + kvt), bf), buf((4, width, rows), bf),
            buf((4, rows, width + kvt), bf), buf((4, width, rows), bf),
            buf((3, rows, width + kvt), bf), buf((3, width, rows), bf),
            pltpu.SemaphoreType.DMA((n,)),
            pltpu.SemaphoreType.DMA((n,)),
            pltpu.SemaphoreType.DMA((7,)),
            pltpu.SemaphoreType.DMA((8,)),
        ],
        compiler_params=remote_params(4),
        name="backward_part",
    )(lengths, nt, dy, hgu, sums, resid, dy_own, x_own, gain, one, q, kv, mixed, qkv, o)


def fast(
    tokens,
    cotangent,
    lengths,
    w_query,
    w_keyval,
    w_output,
    w_gateup,
    w_down,
    norm_gains,
    first_query,
    first_keyval,
    first_output,
    first_gateup,
    first_down,
    first_gains,
    second_query,
    second_keyval,
    second_output,
    second_gateup,
    second_down,
    second_gains,
):
    t = lax.axis_index("tensor")
    quarter = tokens.shape[0] // lax.axis_size("tensor")
    length = lengths[0]

    cot_own = lax.dynamic_slice_in_dim(cotangent, t * quarter, quarter, 0)
    valid = (t * quarter + jnp.arange(quarter) < length)[:, None]
    grad_own = jnp.where(valid, cot_own, jnp.zeros_like(cot_own))
    gains_low = jnp.pad(norm_gains.astype(bf).astype(fl), ((0, 6), (0, 0)))
    (
        gateup, down, dy, normed_two, resid, normed_one, query, keyval, mixed, qkv_w, output_w, gain_full,
    ) = forward_part(lengths, w_query, w_keyval, w_output, w_gateup, w_down, gains_low, tokens, grad_own)
    x_own = lax.dynamic_slice_in_dim(tokens, t * quarter, quarter, 0)

    hgu, sums = feed_forward(normed_two, dy, gateup, down)
    (
        gateup_grad, down_grad, qkv_grad, keyval_shard, output_shard, block_output, input_grad, gains_grad,
    ) = backward_part(
        lengths, normed_two, dy, hgu, sums, resid, grad_own, x_own, gain_full,
        normed_one, query, keyval, mixed, qkv_w, output_w,
    )
    query_shard = qkv_grad[:, : w_query.shape[1]]
    gateup_shard = gateup_grad.astype(fl)
    down_shard = down_grad.astype(fl)
    gains_shard = gains_grad[:2]

    qa = adamw(w_query, query_shard, first_query, second_query, decay_rate)
    ka = adamw(w_keyval, keyval_shard, first_keyval, second_keyval, decay_rate)
    oa = adamw(w_output, output_shard, first_output, second_output, decay_rate)
    ga = adamw(w_gateup, gateup_shard, first_gateup, second_gateup, decay_rate)
    da = adamw(w_down, down_shard, first_down, second_down, decay_rate)
    na = adamw(norm_gains, gains_shard, first_gains, second_gains, 0.0)
    return (block_output, input_grad, *qa, *ka, *oa, *ga, *da, *na)


def solution(mesh):
    query = P("dp", "tensor")
    keyval = P("dp", None)
    output = P("tensor", "dp")
    gateup = P(None, "dp", "tensor")
    gains = P(None, "dp")
    weights = (query, keyval, output, gateup, output, gains)
    return jax.shard_map(
        fast if mesh.shape["dp"] == 2 * ZN and mesh.shape["tensor"] == 4 else general,
        mesh=mesh,
        in_specs=(P("dp", None), P("dp", None), P("dp")) + weights * 3,
        out_specs=(P("dp", None), P("dp", None)) + tuple(w for w in weights for _ in range(4)),
        check_vma=False,
    )
```

```python
import functools

import jax
import jax.numpy as jnp
from jax import lax
from jax.experimental import pallas as pl
from jax.experimental.pallas import tpu as pltpu
from jax.sharding import PartitionSpec as P

HD = 256
ZN = 4

norm_eps = 1e-06
beta_first = 0.9
beta_second = 0.95
learn_rate = 0.01
decay_rate = 0.1
adam_eps = 1e-08
masked_score = -1e30

bf = jnp.bfloat16
fl = jnp.float32


def rms_scale(values, gain):
    inverse = lax.rsqrt(jnp.mean(values * values, axis=-1, keepdims=True) + norm_eps)
    return values * inverse * gain


def dot(left, right):
    return jnp.dot(left, right, preferred_element_type=fl)


def inner_rows(left, right):
    return lax.dot_general(left, right, (((0,), (0,)), ((), ())), preferred_element_type=fl)


def times_trans(left, right):
    return lax.dot_general(left, right, (((1,), (1,)), ((), ())), preferred_element_type=fl)


def slot_scores(query, keyval, length):
    slot = query.shape[0]
    heads = query.shape[1] // HD
    places = jnp.arange(slot)
    allowed = (places[None, :] <= places[:, None]) & (places[None, :] < length)
    raw = jnp.einsum(
        "qhd,kd->hqk",
        query.reshape(slot, heads, HD),
        keyval[:, :HD],
        preferred_element_type=fl,
    )
    return jnp.where(allowed[None], raw * HD ** (-0.5), masked_score)


def slot_forward(query, keyval, length):
    scores = slot_scores(query, keyval, length)
    top = jnp.max(scores, axis=-1, keepdims=True)
    expo = jnp.exp(scores - top)
    total = jnp.sum(expo, axis=-1, keepdims=True)
    probs = expo / total
    mixed = jnp.einsum(
        "hqk,kd->qhd", probs.astype(bf), keyval[:, HD:], preferred_element_type=fl
    )
    return mixed.reshape(query.shape), (top + jnp.log(total))[..., 0]


def slot_backward(query, keyval, length, logsum, grad_mixed):
    slot, width = query.shape
    heads = width // HD
    probs = jnp.exp(slot_scores(query, keyval, length) - logsum[..., None])
    grad_three = grad_mixed.reshape(slot, heads, HD)
    grad_value = jnp.einsum("hqk,qhd->kd", probs.astype(bf), grad_three, preferred_element_type=fl)
    grad_probs = jnp.einsum("qhd,kd->hqk", grad_three, keyval[:, HD:], preferred_element_type=fl)
    grad_scores = probs * (grad_probs - jnp.sum(grad_probs * probs, axis=-1, keepdims=True))
    grad_raw = (grad_scores * HD ** (-0.5)).astype(bf)
    grad_query = jnp.einsum("hqk,kd->qhd", grad_raw, keyval[:, :HD], preferred_element_type=fl)
    grad_key = jnp.einsum(
        "hqk,qhd->kd", grad_raw, query.reshape(slot, heads, HD), preferred_element_type=fl
    )
    return grad_query.reshape(slot, width), jnp.concatenate([grad_key, grad_value], axis=1)


def adamw(weight, grad, first, second, decay):
    first_new = beta_first * first + (1.0 - beta_first) * grad
    second_new = beta_second * second + (1.0 - beta_second) * grad * grad
    update = -learn_rate * (first_new / (jnp.sqrt(second_new) + adam_eps) + decay * weight)
    return (grad, first_new, second_new, update)


def swap(value, step):
    axis, bit = step
    return lax.ppermute(value, axis, [(i, i ^ bit) for i in range(lax.axis_size(axis))])


def offset(position, steps, axis):
    total = 0
    for i, (name, bit) in enumerate(steps):
        if name == axis and position >> i & 1:
            total ^= bit
    return total


def gather(value, steps):
    parts = value[None]
    for step in steps:
        parts = jnp.concatenate([parts, swap(parts, step)], axis=0)
    return parts


def reduce(parts, steps):
    for step in reversed(steps):
        half = parts.shape[0] // 2
        got = swap(parts[half:].astype(bf), step)
        parts = parts[:half].astype(fl) + got.astype(fl)
    return parts[0]


def take(array, index, axis=0):
    return lax.dynamic_index_in_dim(array, index, axis, keepdims=False)


def pick(array, me, steps, axis_name, axis=0):
    return jnp.stack(
        [take(array, me ^ offset(p, steps, axis_name), axis) for p in range(2 ** len(steps))]
    )


def place(parts, me, steps, axis_name, axis=0):
    count = parts.shape[0]
    block = parts.shape[1:]
    shape = block[:axis] + (count,) + block[axis:]
    out = jnp.zeros(shape, parts.dtype)
    for p in range(count):
        out = lax.dynamic_update_index_in_dim(
            out, parts[p], me ^ offset(p, steps, axis_name), axis
        )
    return out


def general(
    tokens,
    cotangent,
    lengths,
    w_query,
    w_keyval,
    w_output,
    w_gateup,
    w_down,
    norm_gains,
    first_query,
    first_keyval,
    first_output,
    first_gateup,
    first_down,
    first_gains,
    second_query,
    second_keyval,
    second_output,
    second_gateup,
    second_down,
    second_gains,
):
    dp = lax.axis_size("dp")
    tn = lax.axis_size("tensor")
    rn = dp // ZN
    me = lax.axis_index("dp")
    z, r = me // rn, me % rn
    t = lax.axis_index("tensor")
    z_steps = [("dp", 2 * rn), ("dp", rn)]
    r_steps = [("dp", 1 << i) for i in reversed(range(rn.bit_length() - 1))]
    t_steps = [("tensor", 1 << i) for i in reversed(range(tn.bit_length() - 1))]
    dp_steps = z_steps + r_steps
    group_steps = z_steps + t_steps

    model = tokens.shape[1]
    rows = model // dp
    slot = tokens.shape[0]
    quarter = slot // tn
    width = w_query.shape[1]
    kvt = w_keyval.shape[1] // tn
    ff = w_down.shape[0] // ZN

    gain_full = place(
        gather(norm_gains.astype(bf), dp_steps), me, dp_steps, "dp", axis=1
    ).reshape(2, model).astype(fl)
    own_keyval = lax.dynamic_slice_in_dim(w_keyval, t * kvt, kvt, 1)
    qkv_w = place(
        gather(jnp.concatenate([w_query, own_keyval], axis=1).astype(bf), dp_steps),
        me, dp_steps, "dp",
    ).reshape(model, width + kvt)
    output_w = place(
        gather(w_output.astype(bf), dp_steps), me, dp_steps, "dp", axis=1
    ).reshape(width, model)

    def zpos(k):
        return ("dp", k * rn)

    gateup_cols = w_gateup.astype(bf).reshape(2, rows, ZN, ff)
    down_rows = w_down.astype(bf).reshape(ZN, ff, rows)
    gateup_w = jnp.zeros((2, ZN, rn, rows, ff), bf)
    down_w = jnp.zeros((ff, ZN, rn, rows), bf)
    for k in range(ZN):
        block = take(gateup_cols, z ^ k, 2)
        if k:
            block = swap(block, zpos(k))
        block = place(gather(block, r_steps), r, r_steps, "dp", axis=1)
        gateup_w = lax.dynamic_update_index_in_dim(gateup_w, block, z ^ k, 1)
    for k in range(ZN):
        block = take(down_rows, z ^ k, 0)
        if k:
            block = swap(block, zpos(k))
        block = place(gather(block, r_steps), r, r_steps, "dp", axis=1)
        down_w = lax.dynamic_update_index_in_dim(down_w, block, z ^ k, 1)
    gateup_w = gateup_w.reshape(2, model, ff)
    down_w = down_w.reshape(ff, model)

    x = tokens.astype(fl)
    length = lengths[0]
    normed_one = rms_scale(x, gain_full[0]).astype(bf)
    projected = dot(normed_one, qkv_w).astype(bf)
    query = projected[:, :width]
    keyval = place(
        gather(projected[:, width:], t_steps), t, t_steps, "tensor", axis=1
    ).reshape(slot, tn * kvt)
    mixed, logsum = slot_forward(query, keyval, length)
    mixed = mixed.astype(bf)
    attn_part = dot(mixed, output_w).astype(bf).reshape(tn, quarter, model)
    attn = reduce(pick(attn_part, t, t_steps, "tensor"), t_steps)
    x_own = lax.dynamic_slice_in_dim(x, t * quarter, quarter, 0)
    resid = x_own + attn
    normed_two_own = rms_scale(resid, gain_full[1]).astype(bf)

    group = ZN * tn * quarter
    normed_two = gather(normed_two_own, group_steps).reshape(group, model)
    cot_own = lax.dynamic_slice_in_dim(cotangent, t * quarter, quarter, 0)
    valid = (t * quarter + jnp.arange(quarter) < length)[:, None]
    grad_own = jnp.where(valid, cot_own, jnp.zeros_like(cot_own))
    grad_low = gather(grad_own, group_steps).reshape(group, model)

    gate = dot(normed_two, gateup_w[0])
    upper = dot(normed_two, gateup_w[1])
    hidden = (jax.nn.gelu(gate, approximate=True) * upper).astype(bf)
    ff_part = dot(hidden, down_w).astype(bf).reshape(ZN * tn, quarter, model)
    out_own = resid + reduce(ff_part, group_steps)
    block_output = place(gather(out_own, t_steps), t, t_steps, "tensor").reshape(slot, model)

    grad_hidden = times_trans(grad_low, down_w)
    _, pull_gelu = jax.vjp(
        lambda left, right: jax.nn.gelu(left, approximate=True) * right, gate, upper
    )
    grad_gate, grad_up = pull_gelu(grad_hidden)
    grad_gate = grad_gate.astype(bf)
    grad_up = grad_up.astype(bf)
    grad_normed = (times_trans(grad_gate, gateup_w[0]) + times_trans(grad_up, gateup_w[1])).astype(bf)
    grad_normed_two = reduce(grad_normed.reshape(ZN * tn, quarter, model), group_steps)

    def columns(array, j):
        return take(array.reshape(group, ZN, rn, rows), r ^ j, 2).reshape(group, ZN * rows)

    def scatter_z(sums, axis):
        parts = []
        for k in range(ZN):
            block = take(sums, z ^ k, 0).astype(bf)
            parts.append(swap(block, zpos(k)) if k else block)
        shape = parts[0].shape
        out = jnp.zeros(shape[:axis] + (ZN,) + shape[axis:], bf)
        for k in range(ZN):
            out = lax.dynamic_update_index_in_dim(out, parts[k], z ^ k, axis)
        return out

    r_offsets = [offset(p, r_steps, "dp") for p in range(rn)]
    down_parts = jnp.stack(
        [
            inner_rows(hidden, columns(grad_low, j)).astype(bf).reshape(ff, ZN, rows)
            for j in r_offsets
        ]
    )
    down_sum = reduce(down_parts, r_steps)
    down_shard = scatter_z(jnp.moveaxis(down_sum, 1, 0), 0).reshape(ZN * ff, rows).astype(fl)

    shards_gu = []
    for grad in (grad_gate, grad_up):
        parts = jnp.stack(
            [
                inner_rows(columns(normed_two, j), grad).astype(bf).reshape(ZN, rows, ff)
                for j in r_offsets
            ]
        )
        sums = reduce(parts, r_steps)
        shards_gu.append(scatter_z(sums, 1).reshape(rows, ZN * ff).astype(fl))
    gateup_shard = jnp.stack(shards_gu)

    _, pull_second = jax.vjp(rms_scale, resid, gain_full[1])
    grad_resid_norm, grad_gain_two = pull_second(grad_normed_two)
    grad_resid = grad_own.astype(fl) + grad_resid_norm
    grad_attn = place(gather(grad_resid.astype(bf), t_steps), t, t_steps, "tensor").reshape(slot, model)

    output_grad = inner_rows(mixed, grad_attn).astype(bf)
    grad_mixed = times_trans(grad_attn, output_w).astype(bf)
    grad_query, grad_keyval = slot_backward(query, keyval, length, logsum, grad_mixed)
    keyval_parts = grad_keyval.astype(bf).reshape(slot, tn, kvt)
    keyval_low = reduce(pick(keyval_parts, t, t_steps, "tensor", axis=1), t_steps).astype(bf)
    grad_projected = jnp.concatenate([grad_query.astype(bf), keyval_low], axis=1)
    one_parts = times_trans(grad_projected, qkv_w).astype(bf).reshape(tn, quarter, model)
    grad_normed_one = reduce(pick(one_parts, t, t_steps, "tensor"), t_steps)
    qkv_grad = inner_rows(normed_one, grad_projected).astype(bf)
    _, pull_first = jax.vjp(rms_scale, x_own, gain_full[0])
    grad_x_norm, grad_gain_one = pull_first(grad_normed_one)
    input_own = grad_resid + grad_x_norm
    input_grad = place(gather(input_own, t_steps), t, t_steps, "tensor").reshape(slot, model)

    qkv_shard = reduce(
        pick(qkv_grad.reshape(dp, rows, width + kvt), me, dp_steps, "dp"), dp_steps
    )
    query_shard = qkv_shard[:, :width]
    keyval_shard = place(
        gather(qkv_shard[:, width:].astype(bf), t_steps), t, t_steps, "tensor", axis=1
    ).reshape(rows, tn * kvt).astype(fl)
    output_shard = reduce(
        pick(output_grad.reshape(width, dp, rows), me, dp_steps, "dp", axis=1), dp_steps
    )
    gains_grad = jnp.stack([grad_gain_one, grad_gain_two]).reshape(2, dp, rows)
    gains_parts = pick(gains_grad, me, dp_steps, "dp", axis=1)
    for step in reversed(dp_steps):
        half = gains_parts.shape[0] // 2
        gains_parts = gains_parts[:half] + swap(gains_parts[half:], step)
    gains_shard = gains_parts[0]
    for step in t_steps:
        gains_shard = gains_shard + swap(gains_shard, step)

    qa = adamw(w_query, query_shard, first_query, second_query, decay_rate)
    ka = adamw(w_keyval, keyval_shard, first_keyval, second_keyval, decay_rate)
    oa = adamw(w_output, output_shard, first_output, second_output, decay_rate)
    ga = adamw(w_gateup, gateup_shard, first_gateup, second_gateup, decay_rate)
    da = adamw(w_down, down_shard, first_down, second_down, decay_rate)
    na = adamw(norm_gains, gains_shard, first_gains, second_gains, 0.0)
    return (block_output, input_grad, *qa, *ka, *oa, *ga, *da, *na)


MESH = pl.DeviceIdType.MESH
ANY = pl.BlockSpec(memory_space=pl.ANY)
VMEM = pl.BlockSpec(memory_space=pltpu.VMEM)
LIMIT = 127 * 512 * 1024
WINDOW = 1
PIECES = 1


def position():
    me = lax.axis_index("dp")
    t = lax.axis_index("tensor")
    return me // 2, me % 2, t


def at_z(z, r, t, k):
    return ((z ^ k) * 2 + r, t)


def greet(partners):
    barrier = pltpu.get_barrier_semaphore()
    for device in partners:
        pl.semaphore_signal(barrier, inc=1, device_id=device, device_id_type=MESH)
    pl.semaphore_wait(barrier, len(partners))


class Copies:
    def __init__(self, send, recv):
        self.send, self.recv, self.made, self.gone = send, recv, {}, set()

    def start(self, name, src, dst, device, sent=None, got=None):
        i = len(self.made)
        make = lambda: pltpu.make_async_remote_copy(
            src_ref=src() if callable(src) else src,
            dst_ref=dst() if callable(dst) else dst,
            send_sem=self.send.at[i],
            recv_sem=self.recv.at[i],
            device_id=device,
            device_id_type=MESH,
        )
        self.made[name] = (make, sent, got)
        maybe(sent, lambda: make().start())

    def arrived(self, name):
        make, _, got = self.made[name]
        maybe(got, lambda: make().wait_recv())

    def left(self, name):
        if name not in self.gone:
            self.gone.add(name)
            make, sent, _ = self.made[name]
            maybe(sent, lambda: make().wait_send())

    def all_left(self, keep=lambda name: True):
        for name in self.made:
            if keep(name):
                self.left(name)


def maybe(condition, action):
    if condition is None:
        action()
    else:
        pl.when(condition)(action)


class Line:
    def __init__(self):
        self.z, self.r, self.t = position()

    def block(self, way, s):
        return lax.max(lax.min(self.z - way * s, 3), 0)

    def device(self, way):
        return (lax.max(lax.min(self.z + way, 3), 0) * 2 + self.r, self.t)

    def sent(self, way, s):
        if way > 0:
            return (self.z < 3) & (self.z >= s)
        return (self.z > 0) & (self.z + s <= 3)

    def got(self, way, s):
        return self.z >= 1 + s if way > 0 else self.z + 1 + s <= 3


WAYS = ((1, "u"), (-1, "d"))


def remote_params(number, limit=LIMIT):
    return pltpu.CompilerParams(
        collective_id=number, has_side_effects=True, vmem_limit_bytes=limit
    )


def block_rows(z, t, quarter):
    return pl.ds(pl.multiple_of((z * 4 + t) * quarter, quarter), quarter)


class TokenGather:
    count = 27

    def __init__(self, copies, own, out, tag):
        self.copies, self.own, self.out, self.tag = copies, own, out, tag
        self.line = Line()
        self.z, self.r, self.t = position()
        self.quarter = own.shape[0]

    def rows(self, b, j):
        return self.out.at[block_rows(b, self.t ^ j, self.quarter)]

    def send_z(self, s):
        for way, mark in WAYS:
            b = self.line.block(way, s)
            self.copies.start(
                f"{self.tag}z{mark}{s}",
                self.own if s == 0 else self.rows(b, 0),
                self.rows(b, 0),
                self.line.device(way),
                self.line.sent(way, s),
                self.line.got(way, s),
            )

    def over(self, name, src, b, j, step, got):
        self.copies.start(
            self.tag + name, src, self.rows(b, j), (self.z * 2 + self.r, self.t ^ step), got, got
        )

    def send_own(self):
        self.over("xo", self.own, self.z, 0, 2, None)
        self.over("co0", self.own, self.z, 0, 1, None)

    def take_z(self, s):
        for way, mark in WAYS:
            self.copies.arrived(f"{self.tag}z{mark}{s}")
        if s < 2:
            self.send_z(s + 1)
        for way, mark in WAYS:
            b, got = self.line.block(way, s + 1), self.line.got(way, s)
            self.over(f"x{mark}{s}", self.rows(b, 0), b, 0, 2, got)
            self.over(f"c{mark}{s}0", self.rows(b, 0), b, 0, 1, got)

    def take_own(self):
        self.copies.arrived(f"{self.tag}xo")
        self.over("co1", self.rows(self.z, 2), self.z, 2, 1, None)

    def take_x(self, s):
        for way, mark in WAYS:
            self.copies.arrived(f"{self.tag}x{mark}{s}")
            b = self.line.block(way, s + 1)
            self.over(f"c{mark}{s}1", self.rows(b, 2), b, 2, 1, self.line.got(way, s))

    def finish(self):
        for name in list(self.copies.made):
            if name.startswith(self.tag + "c"):
                self.copies.arrived(name)
        self.copies.all_left(lambda name: name.startswith(self.tag))


def partners_of(z, r, t, zs=(1, 2, 3), y=True, tensor=True):
    out = [at_z(z, r, t, k) for k in zs]
    if y:
        out.append((z * 2 + (r ^ 1), t))
    if tensor:
        out += [(z * 2 + r, t ^ 2), (z * 2 + r, t ^ 1)]
    return out


def rms_into(src, gain, dst, slab=16):
    @pl.loop(0, dst.shape[0] // slab)
    def _(i):
        rows = pl.ds(pl.multiple_of(i * slab, slab), slab)
        v = src[rows].astype(fl)
        inverse = lax.rsqrt(jnp.mean(v * v, axis=-1, keepdims=True) + norm_eps)
        dst[rows] = (v * inverse * gain).astype(bf)


def cast_into(src, dst, slab=16):
    @pl.loop(0, src.shape[0] // slab)
    def _(i):
        rows = pl.ds(pl.multiple_of(i * slab, slab), slab)
        dst[rows] = src[rows].astype(bf)


def probabilities(q, key, length, first):
    scores = times_trans(q, key) * HD ** (-0.5)
    row = first + lax.broadcasted_iota(jnp.int32, scores.shape, 0)
    col = lax.broadcasted_iota(jnp.int32, scores.shape, 1)
    scores = jnp.where((col <= row) & (col < length), scores, masked_score)
    expo = jnp.exp(scores - jnp.max(scores, axis=-1, keepdims=True))
    return expo / jnp.sum(expo, axis=-1, keepdims=True)


def forward_kernel(
    lengths, wq, wkv, wo, wgu, wd, gains, tokens, dy,
    gu_out, d_out, dy_out, nt_out, resid_out, one_out, q_out, kv_out, mixed_out, qkv_out, o_out, gain_out,
    wq_f, wkv_f, wo_f, gu_f, d_f, gu_b, d_b, x, qkv, o, gain, one, q, kv, mixed,
    part, recvc, sendx, recvx, resid, nt_own,
    send, recv, load, store,
):
    z, r, t = position()
    me = z * 2 + r
    rows = wq.shape[0]
    slot, model = tokens.shape
    quarter = dy.shape[0]
    width = wq.shape[1]
    kvt = qkv.shape[1] - width
    ff = d_out.shape[0]
    other = (z * 2 + (r ^ 1), t)
    x_peer, core_peer, far_peer = (me, t ^ 2), (me, t ^ 1), (me, t ^ 3)

    def d_block(k):
        return pl.ds(pl.multiple_of(((z ^ k) * 2 + r) * rows, rows), rows)

    def f_block(k):
        return pl.ds(pl.multiple_of((z ^ k) * ff, ff), ff)

    kv_cols = pl.ds(pl.multiple_of(t * kvt, kvt), kvt)
    loads = [
        pltpu.make_async_copy(wq, wq_f, load.at[0]),
        pltpu.make_async_copy(wkv.at[:, kv_cols], wkv_f, load.at[1]),
        pltpu.make_async_copy(wo, wo_f, load.at[2]),
        pltpu.make_async_copy(gains, gain.at[:, d_block(0)], load.at[3]),
        pltpu.make_async_copy(tokens, x, load.at[4]),
        pltpu.make_async_copy(wgu, gu_f, load.at[5]),
        pltpu.make_async_copy(wd, d_f, load.at[6]),
    ]
    for copy in loads:
        copy.start()
    stores = []

    def keep(src, dst):
        copy = pltpu.make_async_copy(src, dst, store.at[len(stores)])
        copy.start()
        stores.append(copy)

    keep(dy, dy_out.at[block_rows(z, t, quarter)])
    for copy in loads[:4]:
        copy.wait()

    @pl.loop(0, rows // 16)
    def _(i):
        own = pl.ds(pl.multiple_of(me * rows + i * 16, 16), 16)
        at = pl.ds(pl.multiple_of(i * 16, 16), 16)
        qkv[own, pl.ds(0, width)] = wq_f[at].astype(bf)
        qkv[own, pl.ds(width, kvt)] = wkv_f[at].astype(bf)

    @pl.loop(0, width // 16)
    def _(i):
        at = pl.ds(pl.multiple_of(i * 16, 16), 16)
        o[at, d_block(0)] = wo_f[at].astype(bf)

    greet(partners_of(z, r, t, zs=(1, 2, 3)) + [far_peer] + [((z ^ k) * 2 + (r ^ 1), t) for k in (1, 2, 3)])
    copies = Copies(send, recv)
    d = TokenGather(copies, dy, dy_out, "d")

    for k in range(4):
        for j in range(2):
            if k or j:
                copies.start(
                    f"g{k}{j}", gain.at[:, d_block(0)], gain.at[:, d_block(0)], ((z ^ k) * 2 + (r ^ j), t)
                )

    line = Line()

    def pack_send(tag, name, b, device, sent=None, got=None):
        at = pl.ds(pl.multiple_of((b * 2 + r) * rows, rows), rows)
        ref = qkv.at[at] if tag == "q" else o.at[:, at]
        copies.start(tag + name, ref, ref, device, sent, got)

    def pack_step(tag, s):
        for way, mark in WAYS:
            sent, got = line.sent(way, s), line.got(way, s)
            pack_send(tag, f"z{mark}{s}", line.block(way, s), line.device(way), sent, got)

    def pack_take(tag, s):
        for way, mark in WAYS:
            copies.arrived(f"{tag}z{mark}{s}")
        if s < 2:
            pack_step(tag, s + 1)
        for way, mark in WAYS:
            got = line.got(way, s)
            pack_send(tag, f"y{mark}{s}", line.block(way, s + 1), other, got, got)

    def pack_wait(tag):
        for name in ["o"] + [mark + str(s) for s in range(3) for _, mark in WAYS]:
            copies.arrived(tag + "y" + name)

    pack_step("q", 0)
    pack_send("q", "yo", z, other)
    d.send_own()

    for copy in loads[4:]:
        copy.wait()
    for m in range(2):
        cast_into(gu_f.at[m], gu_b.at[m])
    cast_into(d_f, d_b, 64)

    pieces = PIECES

    def owned(m, k, p):
        if m == 2:
            n = ff // pieces
            return d_b.at[pl.ds(pl.multiple_of((z ^ k) * ff + p * n, n), n)]
        n = rows // pieces
        return gu_b.at[m, p * n : (p + 1) * n, f_block(k)]

    def landed(m, k, p):
        if m == 2:
            n = ff // pieces
            return d_out.at[p * n : (p + 1) * n, d_block(k)]
        n = rows // pieces
        return gu_out.at[m, pl.ds(pl.multiple_of(((z ^ k) * 2 + r) * rows + p * n, n), n)]

    flows = [(m, k, p) for m in range(3) for k in (1, 3, 2) for p in range(pieces)]
    counts = [0, 0]

    def issue():
        if counts[0] < len(flows):
            m, k, p = flows[counts[0]]
            copies.start(f"wz{k}{m}{p}", owned(m, k, p), landed(m, 0, p), at_z(z, r, t, k))
            counts[0] += 1

    def forward(m, k, p):
        copies.start(f"wy{k}{m}{p}", owned(m, 0, p) if k == 0 else landed(m, k, p), landed(m, k, p), other)

    def pump(n, more=True):
        for _ in range(n):
            if counts[1] < counts[0]:
                m, k, p = flows[counts[1]]
                copies.arrived(f"wz{k}{m}{p}")
                forward(m, k, p)
                counts[1] += 1
            if more:
                issue()

    for _ in range(WINDOW):
        issue()
    for m in range(3):
        for p in range(pieces):
            keep(owned(m, 0, p), landed(m, 0, p))

    for k in range(4):
        for j in range(2):
            if k or j:
                copies.arrived(f"g{k}{j}")
    keep(gain, gain_out)
    rms_into(x, gain[0:1, :], one)
    keep(one, one_out)

    pack_take("q", 0)
    pack_take("q", 1)
    pack_step("o", 0)
    for _ in range(WINDOW):
        issue()
    pack_take("q", 2)
    pack_send("o", "yo", z, other)
    d.send_z(0)
    pack_wait("q")
    for p in range(pieces):
        forward(0, 0, p)
    keep(qkv, qkv_out)

    kv[:, kv_cols] = dot(one[...], qkv[:, width:]).astype(bf)
    for name, peer in (("k1", core_peer), ("k2", x_peer), ("k3", far_peer)):
        copies.start(name, kv.at[:, kv_cols], kv.at[:, kv_cols], peer)
    q[...] = dot(one[...], qkv[:, :width]).astype(bf)
    keep(q, q_out)
    pack_take("o", 0)
    for name in ("k1", "k2", "k3"):
        copies.arrived(name)
    keep(kv, kv_out)
    for p in range(pieces):
        forward(1, 0, p)
    length = lengths[0]
    step = 128
    for h in range(width // HD):
        for i in range(slot // step):
            at, upto = pl.ds(i * step, step), pl.ds(0, (i + 1) * step)
            probs = probabilities(q[at, h * HD : (h + 1) * HD], kv[upto, :HD], length, i * step)
            mixed[at, h * HD : (h + 1) * HD] = dot(probs.astype(bf), kv[upto, HD:]).astype(bf)
        if h == 0:
            pack_take("o", 1)
            pump(1)
    keep(mixed, mixed_out)
    pack_take("o", 2)
    pump(1)
    pack_wait("o")
    keep(o, o_out)
    for p in range(pieces):
        forward(2, 0, p)
    d.take_z(0)
    d.take_own()

    def part_of(j, store_part):
        at = pl.ds(pl.multiple_of((t ^ j) * quarter, quarter), quarter)
        for n in range(0, model, 512):
            store_part(dot(mixed[at], o[:, n : n + 512]), slice(n, n + 512))

    def into_part(i):
        def put(value, cols):
            part[i, :, cols] = value.astype(bf)

        return put

    part_of(3, into_part(0))
    part_of(1, into_part(1))
    copies.start("a1", part, recvc, core_peer)
    pump(1)
    copies.arrived("a1")

    def into_x(value, cols):
        sendx[:, cols] = (value + recvc[0, :, cols].astype(fl)).astype(bf)

    part_of(2, into_x)
    copies.start("a2", sendx, recvx, x_peer)

    def into_resid(value, cols):
        resid[:, cols] = value + recvc[1, :, cols].astype(fl)

    part_of(0, into_resid)
    d.take_z(1)
    d.take_x(0)
    copies.arrived("a2")
    first_row = t * quarter

    @pl.loop(0, quarter // 16)
    def _(i):
        at = pl.ds(pl.multiple_of(i * 16, 16), 16)
        mine = pl.ds(pl.multiple_of(first_row + i * 16, 16), 16)
        v = x[mine].astype(fl) + (resid[at] + recvx[at].astype(fl))
        resid[at] = v
        inverse = lax.rsqrt(jnp.mean(v * v, axis=-1, keepdims=True) + norm_eps)
        nt_own[at] = (v * inverse * gain[1:2, :]).astype(bf)

    keep(resid, resid_out)
    keep(nt_own, nt_out.at[block_rows(z, t, quarter)])
    n = TokenGather(copies, nt_own, nt_out, "n")
    n.send_z(0)
    n.send_own()
    pump(2)
    d.take_z(2)
    d.take_x(1)
    n.take_z(0)
    n.take_own()
    pump(2)
    d.take_x(2)
    n.take_z(1)
    n.take_x(0)
    pump(2)
    n.take_z(2)
    n.take_x(1)
    pump(2)
    n.take_x(2)
    pump(len(flows))
    n.finish()
    d.finish()
    for k in range(4):
        for m in range(3):
            for p in range(pieces):
                copies.arrived(f"wy{k}{m}{p}")
    copies.all_left(lambda name: name[0] not in "nd")
    for copy in stores:
        copy.wait()


def forward_part(lengths, wq, wkv, wo, wgu, wd, gains, tokens, dy):
    rows, width = wq.shape
    slot, model = tokens.shape
    quarter = dy.shape[0]
    kvt = wkv.shape[1] // 4
    ff = wd.shape[0] // ZN
    n = 7 + 26 + 21 * PIECES + 3 + 2 + 2 * TokenGather.count
    shape = jax.ShapeDtypeStruct
    return pl.pallas_call(
        forward_kernel,
        out_shape=(
            shape((2, model, ff), bf),
            shape((ff, model), bf),
            shape((16 * quarter, model), bf),
            shape((16 * quarter, model), bf),
            shape((quarter, model), fl),
            shape((slot, model), bf),
            shape((slot, width), bf),
            shape((slot, 4 * kvt), bf),
            shape((slot, width), bf),
            shape((model, width + kvt), bf),
            shape((width, model), bf),
            shape((8, model), fl),
        ),
        in_specs=[pl.BlockSpec(memory_space=pltpu.SMEM)] + [ANY] * 8,
        out_specs=(ANY,) * 12,
        scratch_shapes=[
            pltpu.VMEM((rows, width), fl),
            pltpu.VMEM((rows, kvt), fl),
            pltpu.VMEM((width, rows), fl),
            pltpu.VMEM(wgu.shape, fl),
            pltpu.VMEM(wd.shape, fl),
            pltpu.VMEM(wgu.shape, bf),
            pltpu.VMEM(wd.shape, bf),
            pltpu.VMEM((slot, model), bf),
            pltpu.VMEM((model, width + kvt), bf),
            pltpu.VMEM((width, model), bf),
            pltpu.VMEM((8, model), fl),
            pltpu.VMEM((slot, model), bf),
            pltpu.VMEM((slot, width), bf),
            pltpu.VMEM((slot, 4 * kvt), bf),
            pltpu.VMEM((slot, width), bf),
            pltpu.VMEM((2, quarter, model), bf),
            pltpu.VMEM((2, quarter, model), bf),
            pltpu.VMEM((quarter, model), bf),
            pltpu.VMEM((quarter, model), bf),
            pltpu.VMEM((quarter, model), fl),
            pltpu.VMEM((quarter, model), bf),
            pltpu.SemaphoreType.DMA((n,)),
            pltpu.SemaphoreType.DMA((n,)),
            pltpu.SemaphoreType.DMA((7,)),
            pltpu.SemaphoreType.DMA((10 + 3 * PIECES,)),
        ],
        compiler_params=remote_params(1),
        name="forward_part",
    )(lengths, wq, wkv, wo, wgu, wd, gains, tokens, dy)


ROOT = 0.7978845608028654
CUBE = 0.044715


def ff_kernel(
    nt_hbm, dy_hbm, gu_hbm, d_hbm, hgu_hbm, sums,
    wgu, wd, dots, xin, hgu, sendc, recvc, sendx, kept, recvx, recvz,
    send, recv, zsend, zrecv, load, wload, store,
):
    z, r, t = position()
    x, c = t // 2, t % 2
    me = z * 2 + r
    quarter = sums.shape[1]
    ff, model = wd.shape
    tile = 256
    wide = 1024

    loads = [pltpu.make_async_copy(gu_hbm.at[m], wgu.at[m], wload.at[m]) for m in range(2)]
    loads.append(pltpu.make_async_copy(d_hbm, wd, wload.at[2]))
    for copy in loads:
        copy.start()

    order = (3 * (1 - z // 2), (2 + 3 * z) % 5, 1 + z % 2, z)

    def rows(i, b):
        cc = c if i % 2 else c ^ 1
        xx = x if b else x ^ 1
        return block_rows(order[i // 2], xx * 2 + cc, quarter)

    def fetch(i):
        out = []
        for a, src in enumerate((nt_hbm, dy_hbm)):
            for b in range(2):
                copy = pltpu.make_async_copy(
                    src.at[rows(i, b)],
                    xin.at[i % 2, a, pl.ds(b * quarter, quarter)],
                    load.at[i % 2, a, b],
                )
                copy.start()
                out.append(copy)
        return out

    pending = fetch(0)
    greet(partners_of(z, r, t, zs=(1, 2), y=False))
    copies = Copies(send, recv)
    for copy in loads:
        copy.wait()

    middle = lax.min(lax.rem(z, 3), 1)

    def add_x(s, a, places):
        for place in places:
            pltpu.make_async_copy(recvz.at[place, a], recvz.at[place, a], zrecv.at[place, a]).wait()

        @pl.loop(0, model // tile)
        def _(n):
            cols = pl.ds(pl.multiple_of(n * tile, tile), tile)
            total = kept[s, a, :, cols].astype(fl) + recvx[s, a, :, cols].astype(fl)
            for place in places:
                total += recvz[place, a, :, cols].astype(fl)
            if s == 3:
                sums[a, :, cols] = total
            else:
                recvx[s, a, :, cols] = total.astype(bf)

    def z_copy(s, a):
        up = (order[s] + 4 - z) // 5
        there = z + 2 * up - 1
        same = 1 - lax.min((order[s] - there) * (order[s] - there), 1)
        place = order[s] + (1 - up) * same * (4 - order[s])
        return pltpu.make_async_remote_copy(
            src_ref=recvx.at[s, a],
            dst_ref=recvz.at[place, a],
            send_sem=zsend.at[s, a],
            recv_sem=zrecv.at[place, a],
            device_id=(there * 2 + r, t),
            device_id_type=MESH,
        )

    def take_x(s, a, mid):
        copies.arrived(f"x{s}{a}")
        if s == 3:
            low = lax.min(z, 1)
            add_x(s, a, (z, 4) if mid else (low * z + (1 - low) * 4,))
        else:
            add_x(s, a, (order[s],) if mid else ())
            z_copy(s, a).start()

    def take(at_ends, at_middle):
        for mid, parts in enumerate((at_ends, at_middle)):
            if parts:

                @pl.when(middle == mid)
                def _():
                    for s, a in parts:
                        take_x(s, a, bool(mid))

    rest = [(s, a) for s in range(4) for a in range(2)]
    takes = {
        3: (rest[:1], ()),
        4: (rest[1:2], ()),
        5: (rest[2:3], rest[:1]),
        6: (rest[3:4], rest[1:2]),
        7: (rest[4:], rest[2:]),
    }
    stores = {}
    for i in range(8):
        s, own = i // 2, i % 2
        for copy in pending:
            copy.wait()
        if i < 7:
            pending = fetch(i + 1)
        if i >= 2:
            for copy in stores[i - 2]:
                copy.wait()

        dots[0] = dot(xin[i % 2, 0], wgu[0])
        dots[1] = dot(xin[i % 2, 0], wgu[1])
        dots[2] = times_trans(xin[i % 2, 1], wd[...])

        @pl.loop(0, 2 * quarter // 16)
        def _(n):
            at = pl.ds(pl.multiple_of(n * 16, 16), 16)
            for half in range(0, ff, 512):
                cols = slice(half, half + 512)
                gate, upper, dh = dots[0, at, cols], dots[1, at, cols], dots[2, at, cols]
                square = gate * gate
                bend = jnp.tanh(ROOT * gate * (1.0 + CUBE * square))
                share = 0.5 * (1.0 + bend)
                gelu = gate * share
                slope = share + 0.5 * gate * (1.0 - bend * bend) * (ROOT * (1.0 + 3.0 * CUBE * square))
                hgu[i % 2, 0, at, cols] = (gelu * upper).astype(bf)
                hgu[i % 2, 1, at, cols] = (dh * upper * slope).astype(bf)
                hgu[i % 2, 2, at, cols] = (dh * gelu).astype(bf)

        stores[i] = []
        for m in range(3):
            for b in range(2):
                copy = pltpu.make_async_copy(
                    hgu.at[i % 2, m, pl.ds(b * quarter, quarter)],
                    hgu_hbm.at[m, rows(i, b)],
                    store.at[i % 2, m, b],
                )
                copy.start()
                stores[i].append(copy)

        if own:
            copies.arrived(f"c{s}")
            if s >= 2:
                for a in range(2):
                    copies.left(f"x{s - 2}{a}")
        elif s >= 1:
            copies.left(f"c{s - 1}")

        @pl.loop(0, model // wide)
        def _(n):
            cols = pl.ds(pl.multiple_of(n * wide, wide), wide)
            out = dot(hgu[i % 2, 0], wd[:, cols])
            back = times_trans(hgu[i % 2, 1], wgu[0, cols]) + times_trans(hgu[i % 2, 2], wgu[1, cols])
            for a, part in enumerate((out, back)):
                if own:
                    total = part + recvc[s % 2, a, :, cols].astype(fl)
                    sendx[s % 2, a, :, cols] = total[:quarter].astype(bf)
                    kept[s, a, :, cols] = total[quarter:].astype(bf)
                else:
                    sendc[a, :, cols] = part.astype(bf)

        if own:
            for a in range(2):
                copies.start(f"x{s}{a}", sendx.at[s % 2, a], recvx.at[s, a], (me, t ^ 2))
        else:
            copies.start(f"c{s}", sendc, recvc.at[s % 2], (me, t ^ 1))
        if i in takes:
            take(*takes[i])

    for i in (6, 7):
        for copy in stores[i]:
            copy.wait()
    for s in range(3):
        for a in range(2):
            z_copy(s, a).wait_send()
    copies.all_left()


def feed_forward(nt, dy, wgu, wd):
    group, model = nt.shape
    ff = wd.shape[0]
    quarter = group // 16
    return pl.pallas_call(
        ff_kernel,
        out_shape=(
            jax.ShapeDtypeStruct((3, group, ff), bf),
            jax.ShapeDtypeStruct((2, quarter, model), fl),
        ),
        in_specs=[ANY] * 4,
        out_specs=(ANY, VMEM),
        scratch_shapes=[
            pltpu.VMEM((2, model, ff), bf),
            pltpu.VMEM((ff, model), bf),
            pltpu.VMEM((3, 2 * quarter, ff), fl),
            pltpu.VMEM((2, 2, 2 * quarter, model), bf),
            pltpu.VMEM((2, 3, 2 * quarter, ff), bf),
            pltpu.VMEM((2, 2 * quarter, model), bf),
            pltpu.VMEM((2, 2, 2 * quarter, model), bf),
            pltpu.VMEM((2, 2, quarter, model), bf),
            pltpu.VMEM((4, 2, quarter, model), bf),
            pltpu.VMEM((4, 2, quarter, model), bf),
            pltpu.VMEM((5, 2, quarter, model), bf),
            pltpu.SemaphoreType.DMA((12,)),
            pltpu.SemaphoreType.DMA((12,)),
            pltpu.SemaphoreType.DMA((3, 2)),
            pltpu.SemaphoreType.DMA((5, 2)),
            pltpu.SemaphoreType.DMA((2, 2, 2)),
            pltpu.SemaphoreType.DMA((3,)),
            pltpu.SemaphoreType.DMA((2, 3, 2)),
        ],
        compiler_params=remote_params(3),
        name="feed_forward",
    )(nt, dy, wgu, wd)


def backward_kernel(
    lengths, nt_hbm, dy_hbm, hgu_hbm, sums, resid, dy_own, x_own, gain, one_hbm, q_hbm, kv_hbm, mixed_hbm, qkv_hbm, o_hbm,
    gu_out, d_out, qkv_grad, kv_grad, o_grad, block_out, input_out, gains_out,
    sendy_gu, sendy_d, recvy_gu, recvy_d, own_gu, own_d,
    a, d_resid, out_own, gacc, grecv, gmine, grecv_t,
    gp, dkv_send, dkv_recv, dkv_x, dkv_rx, part, precv, sendx, recvx,
    pk_send, po_send, pk_recv, po_recv, pk_own, po_own, pk_z, po_z,
    send, recv, zsend, zrecv, load, local,
):
    z, r, t = position()
    me = z * 2 + r
    quarter, model = resid.shape
    slot = 4 * quarter
    rows = model // 8
    ff = own_d.shape[1]
    kvt = dkv_x.shape[1]
    width = gp.shape[1] - kvt
    other = (z * 2 + (r ^ 1), t)
    x_peer, core_peer, far_peer = (me, t ^ 2), (me, t ^ 1), (me, t ^ 3)

    def d_block(k, j=0):
        return pl.ds(pl.multiple_of(((z ^ k) * 2 + (r ^ j)) * rows, rows), rows)

    def own_rows(j):
        return pl.ds(pl.multiple_of((t ^ j) * quarter, quarter), quarter)

    loads = [
        pltpu.make_async_copy(sums.at[1], d_resid, load.at[0]),
        pltpu.make_async_copy(sums.at[0], out_own, load.at[1]),
    ]
    for copy in loads:
        copy.start()
    greet(partners_of(z, r, t, zs=(1, 2, 3)) + [far_peer] + [((z ^ k) * 2 + (r ^ 1), t) for k in (1, 2, 3)])
    copies = Copies(send, recv)
    locals_ = []
    counter = list(range(8))

    def keep(src, dst):
        copy = pltpu.make_async_copy(src, dst, local.at[counter.pop(0)])
        copy.start()
        locals_.append(copy)
        return copy

    def norm_back(v, grad, row):
        inverse = lax.rsqrt(jnp.mean(v * v, axis=-1, keepdims=True) + norm_eps)
        scaled = v * inverse
        gacc[row : row + 1, :] += jnp.sum(grad * scaled, axis=0, keepdims=True)
        inner = grad * gain[row : row + 1, :]
        return inverse * (inner - scaled * jnp.mean(inner * scaled, axis=-1, keepdims=True))

    gacc[...] = jnp.zeros_like(gacc)
    for copy in loads:
        copy.wait()

    @pl.loop(0, quarter // 16)
    def _(i):
        at = pl.ds(pl.multiple_of(i * 16, 16), 16)
        mine = pl.ds(pl.multiple_of(t * quarter + i * 16, 16), 16)
        v = resid[at]
        total = dy_own[at].astype(fl) + norm_back(v, d_resid[at], 1)
        d_resid[at] = total
        a[mine] = total.astype(bf)
        out_own[at] += v

    copies.start("ax", a.at[own_rows(0)], a.at[own_rows(0)], x_peer)
    copies.start("ac", a.at[own_rows(0)], a.at[own_rows(0)], core_peer)
    keep(out_own, block_out.at[own_rows(0)])
    in_own = out_own
    copies.start("bx", out_own, block_out.at[own_rows(0)], x_peer)
    copies.start("bc", out_own, block_out.at[own_rows(0)], core_peer)

    end = 1 - lax.min(lax.rem(z, 3), 1)
    zorder = (3 - 2 * end, 2 + end, 1 + end, 0)

    def send_y(i):
        for m in range(2):
            copies.start(f"y{i}{m}", lambda m=m: sendy_gu.at[i, m], lambda m=m: recvy_gu.at[i, m], other)
        copies.start(f"y{i}2", lambda: sendy_d.at[i], lambda: recvy_d.at[i], other)

    flows = [(i, m) for i in range(3) for m in range(3)]
    taken = [0]

    def own_of(i, m):
        return own_d.at[i] if m == 2 else own_gu.at[i, m]

    def add_y(i, m):
        mine, theirs = own_of(i, m), (recvy_d.at[i] if m == 2 else recvy_gu.at[i, m])

        @pl.loop(0, mine.shape[0] // 64)
        def _(n):
            at = pl.ds(pl.multiple_of(n * 64, 64), 64)
            mine[at] = (mine[at].astype(fl) + theirs[at].astype(fl)).astype(bf)

    def place(m):
        cols = pl.ds(pl.multiple_of(z * ff, ff), ff)
        return d_out.at[cols] if m == 2 else gu_out.at[m, :, cols]

    def z_copy(i, m):
        k = zorder[i]
        return pltpu.make_async_remote_copy(
            src_ref=own_of(i, m),
            dst_ref=place(m),
            send_sem=zsend.at[i, m],
            recv_sem=zrecv.at[k - 1, m],
            device_id=at_z(z, r, t, k),
            device_id_type=MESH,
        )

    def pump(n):
        for _ in range(n):
            if taken[0] < len(flows):
                i, m = flows[taken[0]]
                copies.arrived(f"y{i}{m}")
                add_y(i, m)
                z_copy(i, m).start()
                taken[0] += 1

    def feed_forward_grads(first, last, pumps, hgu, lhs):
        loads = [pltpu.make_async_copy(hgu_hbm.at[m], hgu.at[m], load.at[m]) for m in range(3)]

        def fetch(i):
            cols = d_block(zorder[i // 2], 1 - i % 2)
            made = []
            for n, src in enumerate((nt_hbm, dy_hbm)):
                copy = pltpu.make_async_copy(src.at[:, cols], lhs.at[i % 2, n], load.at[3 + 2 * (i % 2) + n])
                copy.start()
                made.append(copy)
            return made

        pending = fetch(first)
        for m in (1, 2, 0):
            loads[m].start()
        for i in range(first, last):
            for copy in pending:
                copy.wait()
            if i < last - 1:
                pending = fetch(i + 1)
            to_gu, to_d = (own_gu, own_d) if i % 2 else (sendy_gu, sendy_d)
            for m, (h, n) in enumerate(((1, 0), (2, 0), (0, 1))):
                if i == first:
                    loads[h].wait()

                @pl.loop(0, ff // 512)
                def _(c):
                    cols = pl.ds(pl.multiple_of(c * 512, 512), 512)
                    grad = inner_rows(lhs[i % 2, n], hgu[h, :, cols])
                    if m < 2:
                        to_gu[i // 2, m, :, cols] = grad.astype(bf)
                    else:
                        to_d[i // 2, cols, :] = grad.T.astype(bf)

            if i % 2 == 0:
                send_y(i // 2)
            pump(pumps[i - first])

    group = nt_hbm.shape[0]
    scope = (pltpu.VMEM((3, group, ff), bf), pltpu.VMEM((2, 2, group, rows), bf))
    pl.run_scoped(functools.partial(feed_forward_grads, 0, 4, (0, 1, 0, 1)), *scope)

    copies.arrived("ax")
    copies.start("af", a.at[own_rows(2)], a.at[own_rows(2)], core_peer)
    copies.arrived("bx")
    copies.start("bf", block_out.at[own_rows(2)], block_out.at[own_rows(2)], core_peer)

    pack_order = (1, 3, 2, 0)

    def attention(q, kv, mixed, qkv, o, one, dm, dkv):
        loads = [
            pltpu.make_async_copy(src, dst, load.at[i])
            for i, (src, dst) in enumerate(
                ((o_hbm, o), (q_hbm, q), (kv_hbm, kv), (mixed_hbm, mixed), (qkv_hbm, qkv), (one_hbm, one))
            )
        ]
        for copy in loads:
            copy.start()
        copies.arrived("ac")
        copies.arrived("af")
        for copy in loads:
            copy.wait()
        dm[...] = times_trans(a[...], o[...]).astype(bf)
        length = lengths[0]
        step = 128
        dkv[...] = jnp.zeros_like(dkv)
        for h in range(width // HD):
            head = slice(h * HD, (h + 1) * HD)
            for i in range(slot // step):
                at, upto = pl.ds(i * step, step), pl.ds(0, (i + 1) * step)
                probs = probabilities(q[at, head], kv[upto, :HD], length, i * step)
                d_probs = times_trans(dm[at, head], kv[upto, HD:])
                d_scores = probs * (d_probs - jnp.sum(d_probs * probs, axis=-1, keepdims=True))
                d_raw = (d_scores * HD ** (-0.5)).astype(bf)
                gp[at, head] = dot(d_raw, kv[upto, :HD]).astype(bf)
                dkv[upto, :HD] += inner_rows(d_raw, q[at, head])
                dkv[upto, HD:] += inner_rows(probs.astype(bf), dm[at, head])
            pump(1)

        def kv_cols(j):
            return pl.ds(pl.multiple_of((t ^ j) * kvt, kvt), kvt)

        dkv_send[0] = dkv[:, kv_cols(1)].astype(bf)
        dkv_send[1] = dkv[:, kv_cols(3)].astype(bf)
        copies.start("kc", lambda: dkv_send, lambda: dkv_recv, core_peer)
        copies.arrived("kc")
        dkv_x[...] = (dkv[:, kv_cols(2)] + dkv_recv[1].astype(fl)).astype(bf)
        copies.start("kx", lambda: dkv_x, lambda: dkv_rx, x_peer)
        mine = dkv[:, kv_cols(0)] + dkv_recv[0].astype(fl)
        copies.arrived("kx")
        gp[:, width:] = (mine + dkv_rx[...].astype(fl)).astype(bf)

        def part_of(j, store_part):
            at = own_rows(j)
            for n in range(0, model, 512):
                store_part(times_trans(gp[at], qkv[n : n + 512]), slice(n, n + 512))

        def into_part(i):
            def put(value, cols):
                part[i, :, cols] = value.astype(bf)

            return put

        part_of(3, into_part(0))
        part_of(1, into_part(1))
        copies.start("pc", lambda: part, lambda: precv, core_peer)

        def pack_grads(k, j, to_k, to_o):
            cols = d_block(k, j)
            to_k[...] = inner_rows(one[:, cols], gp[...]).astype(to_k.dtype)
            to_o[...] = inner_rows(mixed[...], a[:, cols]).astype(to_o.dtype)

        for i, k in enumerate(pack_order):
            pack_grads(k, 1, pk_send.at[i], po_send.at[i])
            copies.start(f"yp{k}", lambda i=i: pk_send.at[i], lambda i=i: pk_recv.at[i], other)
            copies.start(f"yo{k}", lambda i=i: po_send.at[i], lambda i=i: po_recv.at[i], other)
        pump(1)

        copies.arrived("pc")

        def into_x(value, cols):
            sendx[:, cols] = (value + precv[0, :, cols].astype(fl)).astype(bf)

        part_of(2, into_x)
        copies.start("px", lambda: sendx, lambda: recvx, x_peer)

        copies.left("bx")
        copies.left("bc")
        locals_.pop(0).wait()

        def into_own(value, cols):
            in_own[:, cols] = value + precv[1, :, cols].astype(fl)

        part_of(0, into_own)
        for i, k in enumerate(pack_order):
            pack_grads(k, 0, pk_own.at[i], po_own.at[i])
        copies.arrived("px")

    pl.run_scoped(
        attention,
        pltpu.VMEM((slot, width), bf),
        pltpu.VMEM((slot, 2 * HD), bf),
        pltpu.VMEM((slot, width), bf),
        pltpu.VMEM((model, width + kvt), bf),
        pltpu.VMEM((width, model), bf),
        pltpu.VMEM((slot, model), bf),
        pltpu.VMEM((slot, width), bf),
        pltpu.VMEM((slot, 2 * HD), fl),
    )
    pl.run_scoped(functools.partial(feed_forward_grads, 4, 8, (1, 0, 0, 0)), *scope)

    @pl.loop(0, quarter // 16)
    def _(i):
        at = pl.ds(pl.multiple_of(i * 16, 16), 16)
        grad = in_own[at] + recvx[at].astype(fl)
        in_own[at] = d_resid[at] + norm_back(x_own[at].astype(fl), grad, 0)

    keep(in_own, input_out.at[own_rows(0)])
    copies.start("ix", in_own, input_out.at[own_rows(0)], x_peer)
    copies.start("ic", in_own, input_out.at[own_rows(0)], core_peer)

    for k in range(4):
        for j in range(2):
            if k or j:
                copies.start(
                    f"g{k}{j}", gacc.at[:, d_block(k, j)], grecv.at[2 * k + j], ((z ^ k) * 2 + (r ^ j), t)
                )
    pump(6 - taken[0])

    def add_pack(i):
        k = pack_order[i]
        copies.arrived(f"yp{k}")
        copies.arrived(f"yo{k}")
        for mine, theirs in ((pk_own.at[i], pk_recv.at[i]), (po_own.at[i], po_recv.at[i])):
            mine[...] = (mine[...].astype(fl) + theirs[...].astype(fl)).astype(mine.dtype)

    def send_pack(i, k):
        copies.start(f"zp{i}", pk_own.at[i], pk_z.at[i], at_z(z, r, t, k))
        copies.start(f"zo{i}", po_own.at[i], po_z.at[i], at_z(z, r, t, k))

    def pack_arrived(i):
        copies.arrived(f"zp{i}")
        copies.arrived(f"zo{i}")

    add_pack(0)
    send_pack(0, 1)
    add_pack(1)
    send_pack(1, 1)
    add_pack(2)
    pump(1)
    pack_arrived(1)
    pk_own[2] = (pk_own[2].astype(fl) + pk_z[1].astype(fl)).astype(bf)
    po_own[2] = (po_own[2].astype(fl) + po_z[1].astype(fl)).astype(bf)
    send_pack(2, 2)
    pump(9)
    add_pack(3)
    total = gacc[:, d_block(0)]
    for k in range(4):
        for j in range(2):
            if k or j:
                copies.arrived(f"g{k}{j}")
                total += grecv[2 * k + j]
    gmine[...] = total
    for j, peer in ((1, core_peer), (2, x_peer), (3, far_peer)):
        copies.start(f"gt{j}", gmine, grecv_t.at[j], peer)
    copies.arrived("ix")
    copies.start("if", input_out.at[own_rows(2)], input_out.at[own_rows(2)], core_peer)

    for m in range(3):
        copies.arrived(f"y3{m}")
        add_y(3, m)
        keep(own_of(3, m), place(m))
    pk_sum = pk_own[3].astype(fl)
    po_sum = po_own[3].astype(fl)
    for i in (0, 2):
        pack_arrived(i)
        pk_sum += pk_z[i].astype(fl)
        po_sum += po_z[i].astype(fl)
    qkv_grad[...] = pk_sum
    o_grad[...] = po_sum
    mine = pl.ds(pl.multiple_of(t * kvt, kvt), kvt)
    kv_grad[:, mine] = pk_sum[:, width:]
    for j, peer in ((1, core_peer), (2, x_peer), (3, far_peer)):
        copies.start(f"kg{j}", kv_grad.at[:, mine], kv_grad.at[:, mine], peer)
    total = gmine[...]
    for j in (1, 2, 3):
        copies.arrived(f"gt{j}")
        total += grecv_t[j]
    gains_out[...] = total
    for name in ("ic", "if", "bc", "bf", "kg1", "kg2", "kg3"):
        copies.arrived(name)
    for m in range(3):
        for i in range(3):
            pltpu.make_async_copy(place(m), place(m), zrecv.at[i, m]).wait()
            z_copy(i, m).wait_send()
    copies.all_left()
    for copy in locals_:
        copy.wait()


def backward_part(lengths, nt, dy, hgu, sums, resid, dy_own, x_own, gain, one, q, kv, mixed, qkv, o):
    group, model = nt.shape
    ff = hgu.shape[2]
    rows = model // 8
    quarter = resid.shape[0]
    slot, width = q.shape
    kvt = qkv.shape[1] - width
    n = 2 + 2 + 2 + 12 + 2 + 8 + 2 + 3 + 7 + 6 + 3 + 3
    shape = jax.ShapeDtypeStruct
    buf = pltpu.VMEM
    return pl.pallas_call(
        backward_kernel,
        out_shape=(
            shape((2, rows, ZN * ff), bf),
            shape((ZN * ff, rows), bf),
            shape((rows, width + kvt), fl),
            shape((rows, 4 * kvt), fl),
            shape((width, rows), fl),
            shape((slot, model), fl),
            shape((slot, model), fl),
            shape((8, rows), fl),
        ),
        in_specs=[pl.BlockSpec(memory_space=pltpu.SMEM)] + [ANY] * 4 + [VMEM] * 4 + [ANY] * 6,
        out_specs=(ANY, ANY, VMEM, VMEM, VMEM, ANY, ANY, VMEM),
        scratch_shapes=[
            buf((4, 2, rows, ff), bf), buf((4, ff, rows), bf),
            buf((4, 2, rows, ff), bf), buf((4, ff, rows), bf),
            buf((4, 2, rows, ff), bf), buf((4, ff, rows), bf),
            buf((slot, model), bf), buf((quarter, model), fl), buf((quarter, model), fl),
            buf((8, model), fl), buf((8, 8, rows), fl), buf((8, rows), fl), buf((4, 8, rows), fl),
            buf((slot, width + kvt), bf), buf((2, slot, kvt), bf), buf((2, slot, kvt), bf),
            buf((slot, kvt), bf), buf((slot, kvt), bf),
            buf((2, quarter, model), bf), buf((2, quarter, model), bf),
            buf((quarter, model), bf), buf((quarter, model), bf),
            buf((4, rows, width + kvt), bf), buf((4, width, rows), bf),
            buf((4, rows, width + kvt), bf), buf((4, width, rows), bf),
            buf((4, rows, width + kvt), bf), buf((4, width, rows), bf),
            buf((3, rows, width + kvt), bf), buf((3, width, rows), bf),
            pltpu.SemaphoreType.DMA((n,)),
            pltpu.SemaphoreType.DMA((n,)),
            pltpu.SemaphoreType.DMA((3, 3)),
            pltpu.SemaphoreType.DMA((3, 3)),
            pltpu.SemaphoreType.DMA((7,)),
            pltpu.SemaphoreType.DMA((8,)),
        ],
        compiler_params=remote_params(4),
        name="backward_part",
    )(lengths, nt, dy, hgu, sums, resid, dy_own, x_own, gain, one, q, kv, mixed, qkv, o)


def fast(
    tokens,
    cotangent,
    lengths,
    w_query,
    w_keyval,
    w_output,
    w_gateup,
    w_down,
    norm_gains,
    first_query,
    first_keyval,
    first_output,
    first_gateup,
    first_down,
    first_gains,
    second_query,
    second_keyval,
    second_output,
    second_gateup,
    second_down,
    second_gains,
):
    t = lax.axis_index("tensor")
    quarter = tokens.shape[0] // lax.axis_size("tensor")
    length = lengths[0]

    cot_own = lax.dynamic_slice_in_dim(cotangent, t * quarter, quarter, 0)
    valid = (t * quarter + jnp.arange(quarter) < length)[:, None]
    grad_own = jnp.where(valid, cot_own, jnp.zeros_like(cot_own))
    gains_low = jnp.pad(norm_gains.astype(bf).astype(fl), ((0, 6), (0, 0)))
    (
        gateup, down, dy, normed_two, resid, normed_one, query, keyval, mixed, qkv_w, output_w, gain_full,
    ) = forward_part(lengths, w_query, w_keyval, w_output, w_gateup, w_down, gains_low, tokens, grad_own)
    x_own = lax.dynamic_slice_in_dim(tokens, t * quarter, quarter, 0)

    hgu, sums = feed_forward(normed_two, dy, gateup, down)
    (
        gateup_grad, down_grad, qkv_grad, keyval_shard, output_shard, block_output, input_grad, gains_grad,
    ) = backward_part(
        lengths, normed_two, dy, hgu, sums, resid, grad_own, x_own, gain_full,
        normed_one, query, keyval, mixed, qkv_w, output_w,
    )
    query_shard = qkv_grad[:, : w_query.shape[1]]
    gateup_shard = gateup_grad.astype(fl)
    down_shard = down_grad.astype(fl)
    gains_shard = gains_grad[:2]

    qa = adamw(w_query, query_shard, first_query, second_query, decay_rate)
    ka = adamw(w_keyval, keyval_shard, first_keyval, second_keyval, decay_rate)
    oa = adamw(w_output, output_shard, first_output, second_output, decay_rate)
    ga = adamw(w_gateup, gateup_shard, first_gateup, second_gateup, decay_rate)
    da = adamw(w_down, down_shard, first_down, second_down, decay_rate)
    na = adamw(norm_gains, gains_shard, first_gains, second_gains, 0.0)
    return (block_output, input_grad, *qa, *ka, *oa, *ga, *da, *na)


def solution(mesh):
    query = P("dp", "tensor")
    keyval = P("dp", None)
    output = P("tensor", "dp")
    gateup = P(None, "dp", "tensor")
    gains = P(None, "dp")
    weights = (query, keyval, output, gateup, output, gains)
    return jax.shard_map(
        fast if mesh.shape["dp"] == 2 * ZN and mesh.shape["tensor"] == 4 else general,
        mesh=mesh,
        in_specs=(P("dp", None), P("dp", None), P("dp")) + weights * 3,
        out_specs=(P("dp", None), P("dp", None)) + tuple(w for w in weights for _ in range(4)),
        check_vma=False,
    )
```

```python
import functools

import jax
import jax.numpy as jnp
from jax import lax
from jax.experimental import pallas as pl
from jax.experimental.pallas import tpu as pltpu
from jax.sharding import PartitionSpec as P

HD = 256
ZN = 4

norm_eps = 1e-06
beta_first = 0.9
beta_second = 0.95
learn_rate = 0.01
decay_rate = 0.1
adam_eps = 1e-08
masked_score = -1e30

bf = jnp.bfloat16
fl = jnp.float32


def rms_scale(values, gain):
    inverse = lax.rsqrt(jnp.mean(values * values, axis=-1, keepdims=True) + norm_eps)
    return values * inverse * gain


def dot(left, right):
    return jnp.dot(left, right, preferred_element_type=fl)


def inner_rows(left, right):
    return lax.dot_general(left, right, (((0,), (0,)), ((), ())), preferred_element_type=fl)


def times_trans(left, right):
    return lax.dot_general(left, right, (((1,), (1,)), ((), ())), preferred_element_type=fl)


def slot_scores(query, keyval, length):
    slot = query.shape[0]
    heads = query.shape[1] // HD
    places = jnp.arange(slot)
    allowed = (places[None, :] <= places[:, None]) & (places[None, :] < length)
    raw = jnp.einsum(
        "qhd,kd->hqk",
        query.reshape(slot, heads, HD),
        keyval[:, :HD],
        preferred_element_type=fl,
    )
    return jnp.where(allowed[None], raw * HD ** (-0.5), masked_score)


def slot_forward(query, keyval, length):
    scores = slot_scores(query, keyval, length)
    top = jnp.max(scores, axis=-1, keepdims=True)
    expo = jnp.exp(scores - top)
    total = jnp.sum(expo, axis=-1, keepdims=True)
    probs = expo / total
    mixed = jnp.einsum(
        "hqk,kd->qhd", probs.astype(bf), keyval[:, HD:], preferred_element_type=fl
    )
    return mixed.reshape(query.shape), (top + jnp.log(total))[..., 0]


def slot_backward(query, keyval, length, logsum, grad_mixed):
    slot, width = query.shape
    heads = width // HD
    probs = jnp.exp(slot_scores(query, keyval, length) - logsum[..., None])
    grad_three = grad_mixed.reshape(slot, heads, HD)
    grad_value = jnp.einsum("hqk,qhd->kd", probs.astype(bf), grad_three, preferred_element_type=fl)
    grad_probs = jnp.einsum("qhd,kd->hqk", grad_three, keyval[:, HD:], preferred_element_type=fl)
    grad_scores = probs * (grad_probs - jnp.sum(grad_probs * probs, axis=-1, keepdims=True))
    grad_raw = (grad_scores * HD ** (-0.5)).astype(bf)
    grad_query = jnp.einsum("hqk,kd->qhd", grad_raw, keyval[:, :HD], preferred_element_type=fl)
    grad_key = jnp.einsum(
        "hqk,qhd->kd", grad_raw, query.reshape(slot, heads, HD), preferred_element_type=fl
    )
    return grad_query.reshape(slot, width), jnp.concatenate([grad_key, grad_value], axis=1)


def adamw(weight, grad, first, second, decay):
    first_new = beta_first * first + (1.0 - beta_first) * grad
    second_new = beta_second * second + (1.0 - beta_second) * grad * grad
    update = -learn_rate * (first_new / (jnp.sqrt(second_new) + adam_eps) + decay * weight)
    return (grad, first_new, second_new, update)


def swap(value, step):
    axis, bit = step
    return lax.ppermute(value, axis, [(i, i ^ bit) for i in range(lax.axis_size(axis))])


def offset(position, steps, axis):
    total = 0
    for i, (name, bit) in enumerate(steps):
        if name == axis and position >> i & 1:
            total ^= bit
    return total


def gather(value, steps):
    parts = value[None]
    for step in steps:
        parts = jnp.concatenate([parts, swap(parts, step)], axis=0)
    return parts


def reduce(parts, steps):
    for step in reversed(steps):
        half = parts.shape[0] // 2
        got = swap(parts[half:].astype(bf), step)
        parts = parts[:half].astype(fl) + got.astype(fl)
    return parts[0]


def take(array, index, axis=0):
    return lax.dynamic_index_in_dim(array, index, axis, keepdims=False)


def pick(array, me, steps, axis_name, axis=0):
    return jnp.stack(
        [take(array, me ^ offset(p, steps, axis_name), axis) for p in range(2 ** len(steps))]
    )


def place(parts, me, steps, axis_name, axis=0):
    count = parts.shape[0]
    block = parts.shape[1:]
    shape = block[:axis] + (count,) + block[axis:]
    out = jnp.zeros(shape, parts.dtype)
    for p in range(count):
        out = lax.dynamic_update_index_in_dim(
            out, parts[p], me ^ offset(p, steps, axis_name), axis
        )
    return out


def general(
    tokens,
    cotangent,
    lengths,
    w_query,
    w_keyval,
    w_output,
    w_gateup,
    w_down,
    norm_gains,
    first_query,
    first_keyval,
    first_output,
    first_gateup,
    first_down,
    first_gains,
    second_query,
    second_keyval,
    second_output,
    second_gateup,
    second_down,
    second_gains,
):
    dp = lax.axis_size("dp")
    tn = lax.axis_size("tensor")
    rn = dp // ZN
    me = lax.axis_index("dp")
    z, r = me // rn, me % rn
    t = lax.axis_index("tensor")
    z_steps = [("dp", 2 * rn), ("dp", rn)]
    r_steps = [("dp", 1 << i) for i in reversed(range(rn.bit_length() - 1))]
    t_steps = [("tensor", 1 << i) for i in reversed(range(tn.bit_length() - 1))]
    dp_steps = z_steps + r_steps
    group_steps = z_steps + t_steps

    model = tokens.shape[1]
    rows = model // dp
    slot = tokens.shape[0]
    quarter = slot // tn
    width = w_query.shape[1]
    kvt = w_keyval.shape[1] // tn
    ff = w_down.shape[0] // ZN

    gain_full = place(
        gather(norm_gains.astype(bf), dp_steps), me, dp_steps, "dp", axis=1
    ).reshape(2, model).astype(fl)
    own_keyval = lax.dynamic_slice_in_dim(w_keyval, t * kvt, kvt, 1)
    qkv_w = place(
        gather(jnp.concatenate([w_query, own_keyval], axis=1).astype(bf), dp_steps),
        me, dp_steps, "dp",
    ).reshape(model, width + kvt)
    output_w = place(
        gather(w_output.astype(bf), dp_steps), me, dp_steps, "dp", axis=1
    ).reshape(width, model)

    def zpos(k):
        return ("dp", k * rn)

    gateup_cols = w_gateup.astype(bf).reshape(2, rows, ZN, ff)
    down_rows = w_down.astype(bf).reshape(ZN, ff, rows)
    gateup_w = jnp.zeros((2, ZN, rn, rows, ff), bf)
    down_w = jnp.zeros((ff, ZN, rn, rows), bf)
    for k in range(ZN):
        block = take(gateup_cols, z ^ k, 2)
        if k:
            block = swap(block, zpos(k))
        block = place(gather(block, r_steps), r, r_steps, "dp", axis=1)
        gateup_w = lax.dynamic_update_index_in_dim(gateup_w, block, z ^ k, 1)
    for k in range(ZN):
        block = take(down_rows, z ^ k, 0)
        if k:
            block = swap(block, zpos(k))
        block = place(gather(block, r_steps), r, r_steps, "dp", axis=1)
        down_w = lax.dynamic_update_index_in_dim(down_w, block, z ^ k, 1)
    gateup_w = gateup_w.reshape(2, model, ff)
    down_w = down_w.reshape(ff, model)

    x = tokens.astype(fl)
    length = lengths[0]
    normed_one = rms_scale(x, gain_full[0]).astype(bf)
    projected = dot(normed_one, qkv_w).astype(bf)
    query = projected[:, :width]
    keyval = place(
        gather(projected[:, width:], t_steps), t, t_steps, "tensor", axis=1
    ).reshape(slot, tn * kvt)
    mixed, logsum = slot_forward(query, keyval, length)
    mixed = mixed.astype(bf)
    attn_part = dot(mixed, output_w).astype(bf).reshape(tn, quarter, model)
    attn = reduce(pick(attn_part, t, t_steps, "tensor"), t_steps)
    x_own = lax.dynamic_slice_in_dim(x, t * quarter, quarter, 0)
    resid = x_own + attn
    normed_two_own = rms_scale(resid, gain_full[1]).astype(bf)

    group = ZN * tn * quarter
    normed_two = gather(normed_two_own, group_steps).reshape(group, model)
    cot_own = lax.dynamic_slice_in_dim(cotangent, t * quarter, quarter, 0)
    valid = (t * quarter + jnp.arange(quarter) < length)[:, None]
    grad_own = jnp.where(valid, cot_own, jnp.zeros_like(cot_own))
    grad_low = gather(grad_own, group_steps).reshape(group, model)

    gate = dot(normed_two, gateup_w[0])
    upper = dot(normed_two, gateup_w[1])
    hidden = (jax.nn.gelu(gate, approximate=True) * upper).astype(bf)
    ff_part = dot(hidden, down_w).astype(bf).reshape(ZN * tn, quarter, model)
    out_own = resid + reduce(ff_part, group_steps)
    block_output = place(gather(out_own, t_steps), t, t_steps, "tensor").reshape(slot, model)

    grad_hidden = times_trans(grad_low, down_w)
    _, pull_gelu = jax.vjp(
        lambda left, right: jax.nn.gelu(left, approximate=True) * right, gate, upper
    )
    grad_gate, grad_up = pull_gelu(grad_hidden)
    grad_gate = grad_gate.astype(bf)
    grad_up = grad_up.astype(bf)
    grad_normed = (times_trans(grad_gate, gateup_w[0]) + times_trans(grad_up, gateup_w[1])).astype(bf)
    grad_normed_two = reduce(grad_normed.reshape(ZN * tn, quarter, model), group_steps)

    def columns(array, j):
        return take(array.reshape(group, ZN, rn, rows), r ^ j, 2).reshape(group, ZN * rows)

    def scatter_z(sums, axis):
        parts = []
        for k in range(ZN):
            block = take(sums, z ^ k, 0).astype(bf)
            parts.append(swap(block, zpos(k)) if k else block)
        shape = parts[0].shape
        out = jnp.zeros(shape[:axis] + (ZN,) + shape[axis:], bf)
        for k in range(ZN):
            out = lax.dynamic_update_index_in_dim(out, parts[k], z ^ k, axis)
        return out

    r_offsets = [offset(p, r_steps, "dp") for p in range(rn)]
    down_parts = jnp.stack(
        [
            inner_rows(hidden, columns(grad_low, j)).astype(bf).reshape(ff, ZN, rows)
            for j in r_offsets
        ]
    )
    down_sum = reduce(down_parts, r_steps)
    down_shard = scatter_z(jnp.moveaxis(down_sum, 1, 0), 0).reshape(ZN * ff, rows).astype(fl)

    shards_gu = []
    for grad in (grad_gate, grad_up):
        parts = jnp.stack(
            [
                inner_rows(columns(normed_two, j), grad).astype(bf).reshape(ZN, rows, ff)
                for j in r_offsets
            ]
        )
        sums = reduce(parts, r_steps)
        shards_gu.append(scatter_z(sums, 1).reshape(rows, ZN * ff).astype(fl))
    gateup_shard = jnp.stack(shards_gu)

    _, pull_second = jax.vjp(rms_scale, resid, gain_full[1])
    grad_resid_norm, grad_gain_two = pull_second(grad_normed_two)
    grad_resid = grad_own.astype(fl) + grad_resid_norm
    grad_attn = place(gather(grad_resid.astype(bf), t_steps), t, t_steps, "tensor").reshape(slot, model)

    output_grad = inner_rows(mixed, grad_attn).astype(bf)
    grad_mixed = times_trans(grad_attn, output_w).astype(bf)
    grad_query, grad_keyval = slot_backward(query, keyval, length, logsum, grad_mixed)
    keyval_parts = grad_keyval.astype(bf).reshape(slot, tn, kvt)
    keyval_low = reduce(pick(keyval_parts, t, t_steps, "tensor", axis=1), t_steps).astype(bf)
    grad_projected = jnp.concatenate([grad_query.astype(bf), keyval_low], axis=1)
    one_parts = times_trans(grad_projected, qkv_w).astype(bf).reshape(tn, quarter, model)
    grad_normed_one = reduce(pick(one_parts, t, t_steps, "tensor"), t_steps)
    qkv_grad = inner_rows(normed_one, grad_projected).astype(bf)
    _, pull_first = jax.vjp(rms_scale, x_own, gain_full[0])
    grad_x_norm, grad_gain_one = pull_first(grad_normed_one)
    input_own = grad_resid + grad_x_norm
    input_grad = place(gather(input_own, t_steps), t, t_steps, "tensor").reshape(slot, model)

    qkv_shard = reduce(
        pick(qkv_grad.reshape(dp, rows, width + kvt), me, dp_steps, "dp"), dp_steps
    )
    query_shard = qkv_shard[:, :width]
    keyval_shard = place(
        gather(qkv_shard[:, width:].astype(bf), t_steps), t, t_steps, "tensor", axis=1
    ).reshape(rows, tn * kvt).astype(fl)
    output_shard = reduce(
        pick(output_grad.reshape(width, dp, rows), me, dp_steps, "dp", axis=1), dp_steps
    )
    gains_grad = jnp.stack([grad_gain_one, grad_gain_two]).reshape(2, dp, rows)
    gains_parts = pick(gains_grad, me, dp_steps, "dp", axis=1)
    for step in reversed(dp_steps):
        half = gains_parts.shape[0] // 2
        gains_parts = gains_parts[:half] + swap(gains_parts[half:], step)
    gains_shard = gains_parts[0]
    for step in t_steps:
        gains_shard = gains_shard + swap(gains_shard, step)

    qa = adamw(w_query, query_shard, first_query, second_query, decay_rate)
    ka = adamw(w_keyval, keyval_shard, first_keyval, second_keyval, decay_rate)
    oa = adamw(w_output, output_shard, first_output, second_output, decay_rate)
    ga = adamw(w_gateup, gateup_shard, first_gateup, second_gateup, decay_rate)
    da = adamw(w_down, down_shard, first_down, second_down, decay_rate)
    na = adamw(norm_gains, gains_shard, first_gains, second_gains, 0.0)
    return (block_output, input_grad, *qa, *ka, *oa, *ga, *da, *na)


MESH = pl.DeviceIdType.MESH
ANY = pl.BlockSpec(memory_space=pl.ANY)
VMEM = pl.BlockSpec(memory_space=pltpu.VMEM)
LIMIT = 127 * 512 * 1024
WINDOW = 1
PIECES = 1


def position():
    me = lax.axis_index("dp")
    t = lax.axis_index("tensor")
    return me // 2, me % 2, t


def at_z(z, r, t, k):
    return ((z ^ k) * 2 + r, t)


def greet(partners):
    barrier = pltpu.get_barrier_semaphore()
    for device in partners:
        pl.semaphore_signal(barrier, inc=1, device_id=device, device_id_type=MESH)
    pl.semaphore_wait(barrier, len(partners))


class Copies:
    def __init__(self, send, recv):
        self.send, self.recv, self.made, self.gone = send, recv, {}, set()

    def start(self, name, src, dst, device, sent=None, got=None):
        i = len(self.made)
        make = lambda: pltpu.make_async_remote_copy(
            src_ref=src() if callable(src) else src,
            dst_ref=dst() if callable(dst) else dst,
            send_sem=self.send.at[i],
            recv_sem=self.recv.at[i],
            device_id=device,
            device_id_type=MESH,
        )
        self.made[name] = (make, sent, got)
        maybe(sent, lambda: make().start())

    def arrived(self, name):
        make, _, got = self.made[name]
        maybe(got, lambda: make().wait_recv())

    def left(self, name):
        if name not in self.gone:
            self.gone.add(name)
            make, sent, _ = self.made[name]
            maybe(sent, lambda: make().wait_send())

    def all_left(self, keep=lambda name: True):
        for name in self.made:
            if keep(name):
                self.left(name)


def maybe(condition, action):
    if condition is None:
        action()
    else:
        pl.when(condition)(action)


class Line:
    def __init__(self):
        self.z, self.r, self.t = position()

    def block(self, way, s):
        return lax.max(lax.min(self.z - way * s, 3), 0)

    def device(self, way):
        return (lax.max(lax.min(self.z + way, 3), 0) * 2 + self.r, self.t)

    def sent(self, way, s):
        if way > 0:
            return (self.z < 3) & (self.z >= s)
        return (self.z > 0) & (self.z + s <= 3)

    def got(self, way, s):
        return self.z >= 1 + s if way > 0 else self.z + 1 + s <= 3


WAYS = ((1, "u"), (-1, "d"))


def remote_params(number, limit=LIMIT):
    return pltpu.CompilerParams(
        collective_id=number, has_side_effects=True, vmem_limit_bytes=limit
    )


def block_rows(z, t, quarter):
    return pl.ds(pl.multiple_of((z * 4 + t) * quarter, quarter), quarter)


class TokenGather:
    count = 27

    def __init__(self, copies, own, out, tag):
        self.copies, self.own, self.out, self.tag = copies, own, out, tag
        self.line = Line()
        self.z, self.r, self.t = position()
        self.quarter = own.shape[0]

    def rows(self, b, j):
        return self.out.at[block_rows(b, self.t ^ j, self.quarter)]

    def send_z(self, s):
        for way, mark in WAYS:
            b = self.line.block(way, s)
            self.copies.start(
                f"{self.tag}z{mark}{s}",
                self.own if s == 0 else self.rows(b, 0),
                self.rows(b, 0),
                self.line.device(way),
                self.line.sent(way, s),
                self.line.got(way, s),
            )

    def over(self, name, src, b, j, step, got):
        self.copies.start(
            self.tag + name, src, self.rows(b, j), (self.z * 2 + self.r, self.t ^ step), got, got
        )

    def send_own(self):
        self.over("xo", self.own, self.z, 0, 2, None)
        self.over("co0", self.own, self.z, 0, 1, None)

    def take_z(self, s):
        for way, mark in WAYS:
            self.copies.arrived(f"{self.tag}z{mark}{s}")
        if s < 2:
            self.send_z(s + 1)
        for way, mark in WAYS:
            b, got = self.line.block(way, s + 1), self.line.got(way, s)
            self.over(f"x{mark}{s}", self.rows(b, 0), b, 0, 2, got)
            self.over(f"c{mark}{s}0", self.rows(b, 0), b, 0, 1, got)

    def take_own(self):
        self.copies.arrived(f"{self.tag}xo")
        self.over("co1", self.rows(self.z, 2), self.z, 2, 1, None)

    def take_x(self, s):
        for way, mark in WAYS:
            self.copies.arrived(f"{self.tag}x{mark}{s}")
            b = self.line.block(way, s + 1)
            self.over(f"c{mark}{s}1", self.rows(b, 2), b, 2, 1, self.line.got(way, s))

    def finish(self):
        for name in list(self.copies.made):
            if name.startswith(self.tag + "c"):
                self.copies.arrived(name)
        self.copies.all_left(lambda name: name.startswith(self.tag))


def partners_of(z, r, t, zs=(1, 2, 3), y=True, tensor=True):
    out = [at_z(z, r, t, k) for k in zs]
    if y:
        out.append((z * 2 + (r ^ 1), t))
    if tensor:
        out += [(z * 2 + r, t ^ 2), (z * 2 + r, t ^ 1)]
    return out


def rms_into(src, gain, dst, slab=16):
    @pl.loop(0, dst.shape[0] // slab)
    def _(i):
        rows = pl.ds(pl.multiple_of(i * slab, slab), slab)
        v = src[rows].astype(fl)
        inverse = lax.rsqrt(jnp.mean(v * v, axis=-1, keepdims=True) + norm_eps)
        dst[rows] = (v * inverse * gain).astype(bf)


def cast_into(src, dst, slab=16):
    @pl.loop(0, src.shape[0] // slab)
    def _(i):
        rows = pl.ds(pl.multiple_of(i * slab, slab), slab)
        dst[rows] = src[rows].astype(bf)


def probabilities(q, key, length, first):
    scores = times_trans(q, key) * HD ** (-0.5)
    row = first + lax.broadcasted_iota(jnp.int32, scores.shape, 0)
    col = lax.broadcasted_iota(jnp.int32, scores.shape, 1)
    scores = jnp.where((col <= row) & (col < length), scores, masked_score)
    expo = jnp.exp(scores - jnp.max(scores, axis=-1, keepdims=True))
    return expo / jnp.sum(expo, axis=-1, keepdims=True)


def forward_kernel(
    lengths, wq, wkv, wo, wgu, wd, gains, tokens, cotangent,
    gu_out, d_out, dy_out, nt_out, resid_out, one_out, q_out, kv_out, mixed_out, qkv_out, o_out, gain_out,
    wq_f, wkv_f, wo_f, gu_f, d_f, gu_b, d_b, x, qkv, o, gain, one, q, kv, mixed,
    part, recvc, sendx, recvx, resid, nt_own, dy,
    send, recv, load, store,
):
    z, r, t = position()
    me = z * 2 + r
    rows = wq.shape[0]
    slot, model = tokens.shape
    quarter = slot // 4
    width = wq.shape[1]
    kvt = qkv.shape[1] - width
    ff = d_out.shape[0]
    other = (z * 2 + (r ^ 1), t)
    x_peer, core_peer, far_peer = (me, t ^ 2), (me, t ^ 1), (me, t ^ 3)

    def d_block(k):
        return pl.ds(pl.multiple_of(((z ^ k) * 2 + r) * rows, rows), rows)

    def f_block(k):
        return pl.ds(pl.multiple_of((z ^ k) * ff, ff), ff)

    kv_cols = pl.ds(pl.multiple_of(t * kvt, kvt), kvt)
    loads = [
        pltpu.make_async_copy(wq, wq_f, load.at[0]),
        pltpu.make_async_copy(wkv.at[:, kv_cols], wkv_f, load.at[1]),
        pltpu.make_async_copy(wo, wo_f, load.at[2]),
        pltpu.make_async_copy(gains, gain.at[:, d_block(0)], load.at[3]),
        pltpu.make_async_copy(
            cotangent.at[pl.ds(pl.multiple_of(t * quarter, quarter), quarter)], dy, load.at[7]
        ),
        pltpu.make_async_copy(tokens, x, load.at[4]),
        pltpu.make_async_copy(wgu, gu_f, load.at[5]),
        pltpu.make_async_copy(wd, d_f, load.at[6]),
    ]
    for copy in loads:
        copy.start()
    stores = []

    def keep(src, dst):
        copy = pltpu.make_async_copy(src, dst, store.at[len(stores)])
        copy.start()
        stores.append(copy)

    for copy in loads[:5]:
        copy.wait()
    length = lengths[0]

    @pl.loop(0, quarter // 16)
    def _(i):
        at = pl.ds(pl.multiple_of(i * 16, 16), 16)
        row = t * quarter + i * 16 + lax.broadcasted_iota(jnp.int32, (16, model), 0)
        dy[at] = jnp.where(row < length, dy[at].astype(fl), 0.0).astype(bf)

    keep(dy, dy_out.at[block_rows(z, t, quarter)])

    @pl.loop(0, rows // 16)
    def _(i):
        own = pl.ds(pl.multiple_of(me * rows + i * 16, 16), 16)
        at = pl.ds(pl.multiple_of(i * 16, 16), 16)
        qkv[own, pl.ds(0, width)] = wq_f[at].astype(bf)
        qkv[own, pl.ds(width, kvt)] = wkv_f[at].astype(bf)

    @pl.loop(0, width // 16)
    def _(i):
        at = pl.ds(pl.multiple_of(i * 16, 16), 16)
        o[at, d_block(0)] = wo_f[at].astype(bf)

    greet(partners_of(z, r, t, zs=(1, 2, 3)) + [far_peer] + [((z ^ k) * 2 + (r ^ 1), t) for k in (1, 2, 3)])
    copies = Copies(send, recv)
    d = TokenGather(copies, dy, dy_out, "d")

    for k in range(4):
        for j in range(2):
            if k or j:
                copies.start(
                    f"g{k}{j}", gain.at[:, d_block(0)], gain.at[:, d_block(0)], ((z ^ k) * 2 + (r ^ j), t)
                )

    line = Line()

    def pack_send(tag, name, b, device, sent=None, got=None):
        at = pl.ds(pl.multiple_of((b * 2 + r) * rows, rows), rows)
        ref = qkv.at[at] if tag == "q" else o.at[:, at]
        copies.start(tag + name, ref, ref, device, sent, got)

    def pack_step(tag, s):
        for way, mark in WAYS:
            sent, got = line.sent(way, s), line.got(way, s)
            pack_send(tag, f"z{mark}{s}", line.block(way, s), line.device(way), sent, got)

    def pack_take(tag, s):
        for way, mark in WAYS:
            copies.arrived(f"{tag}z{mark}{s}")
        if s < 2:
            pack_step(tag, s + 1)
        for way, mark in WAYS:
            got = line.got(way, s)
            pack_send(tag, f"y{mark}{s}", line.block(way, s + 1), other, got, got)

    def pack_wait(tag):
        for name in ["o"] + [mark + str(s) for s in range(3) for _, mark in WAYS]:
            copies.arrived(tag + "y" + name)

    pack_step("q", 0)
    pack_send("q", "yo", z, other)
    d.send_own()

    for copy in loads[5:]:
        copy.wait()
    for m in range(2):
        cast_into(gu_f.at[m], gu_b.at[m])
    cast_into(d_f, d_b, 64)

    pieces = PIECES

    def owned(m, k, p):
        if m == 2:
            n = ff // pieces
            return d_b.at[pl.ds(pl.multiple_of((z ^ k) * ff + p * n, n), n)]
        n = rows // pieces
        return gu_b.at[m, p * n : (p + 1) * n, f_block(k)]

    def landed(m, k, p):
        if m == 2:
            n = ff // pieces
            return d_out.at[p * n : (p + 1) * n, d_block(k)]
        n = rows // pieces
        return gu_out.at[m, pl.ds(pl.multiple_of(((z ^ k) * 2 + r) * rows + p * n, n), n)]

    flows = [(m, k, p) for m in range(3) for k in (1, 3, 2) for p in range(pieces)]
    counts = [0, 0]

    def issue():
        if counts[0] < len(flows):
            m, k, p = flows[counts[0]]
            copies.start(f"wz{k}{m}{p}", owned(m, k, p), landed(m, 0, p), at_z(z, r, t, k))
            counts[0] += 1

    def forward(m, k, p):
        copies.start(f"wy{k}{m}{p}", owned(m, 0, p) if k == 0 else landed(m, k, p), landed(m, k, p), other)

    def pump(n, more=True):
        for _ in range(n):
            if counts[1] < counts[0]:
                m, k, p = flows[counts[1]]
                copies.arrived(f"wz{k}{m}{p}")
                forward(m, k, p)
                counts[1] += 1
            if more:
                issue()

    for _ in range(WINDOW):
        issue()
    for m in range(3):
        for p in range(pieces):
            keep(owned(m, 0, p), landed(m, 0, p))

    for k in range(4):
        for j in range(2):
            if k or j:
                copies.arrived(f"g{k}{j}")
    keep(gain, gain_out)
    rms_into(x, gain[0:1, :], one)
    keep(one, one_out)

    pack_take("q", 0)
    pack_take("q", 1)
    pack_step("o", 0)
    for _ in range(WINDOW):
        issue()
    pack_take("q", 2)
    pack_send("o", "yo", z, other)
    d.send_z(0)
    pack_wait("q")
    for p in range(pieces):
        forward(0, 0, p)
    keep(qkv, qkv_out)

    kv[:, kv_cols] = dot(one[...], qkv[:, width:]).astype(bf)
    for name, peer in (("k1", core_peer), ("k2", x_peer), ("k3", far_peer)):
        copies.start(name, kv.at[:, kv_cols], kv.at[:, kv_cols], peer)
    q[...] = dot(one[...], qkv[:, :width]).astype(bf)
    keep(q, q_out)
    pack_take("o", 0)
    for name in ("k1", "k2", "k3"):
        copies.arrived(name)
    keep(kv, kv_out)
    for p in range(pieces):
        forward(1, 0, p)
    step = 128
    for h in range(width // HD):
        for i in range(slot // step):
            at, upto = pl.ds(i * step, step), pl.ds(0, (i + 1) * step)
            probs = probabilities(q[at, h * HD : (h + 1) * HD], kv[upto, :HD], length, i * step)
            mixed[at, h * HD : (h + 1) * HD] = dot(probs.astype(bf), kv[upto, HD:]).astype(bf)
        if h == 0:
            pack_take("o", 1)
            pump(1)
    keep(mixed, mixed_out)
    pack_take("o", 2)
    pump(1)
    pack_wait("o")
    keep(o, o_out)
    for p in range(pieces):
        forward(2, 0, p)
    d.take_z(0)
    d.take_own()

    def part_of(j, store_part):
        at = pl.ds(pl.multiple_of((t ^ j) * quarter, quarter), quarter)
        for n in range(0, model, 512):
            store_part(dot(mixed[at], o[:, n : n + 512]), slice(n, n + 512))

    def into_part(i):
        def put(value, cols):
            part[i, :, cols] = value.astype(bf)

        return put

    part_of(3, into_part(0))
    part_of(1, into_part(1))
    copies.start("a1", part, recvc, core_peer)
    pump(1)
    copies.arrived("a1")

    def into_x(value, cols):
        sendx[:, cols] = (value + recvc[0, :, cols].astype(fl)).astype(bf)

    part_of(2, into_x)
    copies.start("a2", sendx, recvx, x_peer)

    def into_resid(value, cols):
        resid[:, cols] = value + recvc[1, :, cols].astype(fl)

    part_of(0, into_resid)
    d.take_z(1)
    d.take_x(0)
    copies.arrived("a2")
    first_row = t * quarter

    @pl.loop(0, quarter // 16)
    def _(i):
        at = pl.ds(pl.multiple_of(i * 16, 16), 16)
        mine = pl.ds(pl.multiple_of(first_row + i * 16, 16), 16)
        v = x[mine].astype(fl) + (resid[at] + recvx[at].astype(fl))
        resid[at] = v
        inverse = lax.rsqrt(jnp.mean(v * v, axis=-1, keepdims=True) + norm_eps)
        nt_own[at] = (v * inverse * gain[1:2, :]).astype(bf)

    keep(resid, resid_out)
    keep(nt_own, nt_out.at[block_rows(z, t, quarter)])
    n = TokenGather(copies, nt_own, nt_out, "n")
    n.send_z(0)
    n.send_own()
    pump(2)
    d.take_z(2)
    d.take_x(1)
    n.take_z(0)
    n.take_own()
    pump(2)
    d.take_x(2)
    n.take_z(1)
    n.take_x(0)
    pump(2)
    n.take_z(2)
    n.take_x(1)
    pump(2)
    n.take_x(2)
    pump(len(flows))
    n.finish()
    d.finish()
    for k in range(4):
        for m in range(3):
            for p in range(pieces):
                copies.arrived(f"wy{k}{m}{p}")
    copies.all_left(lambda name: name[0] not in "nd")
    for copy in stores:
        copy.wait()


def forward_part(lengths, wq, wkv, wo, wgu, wd, gains, tokens, cotangent):
    rows, width = wq.shape
    slot, model = tokens.shape
    quarter = slot // 4
    kvt = wkv.shape[1] // 4
    ff = wd.shape[0] // ZN
    n = 7 + 26 + 21 * PIECES + 3 + 2 + 2 * TokenGather.count
    shape = jax.ShapeDtypeStruct
    return pl.pallas_call(
        forward_kernel,
        out_shape=(
            shape((2, model, ff), bf),
            shape((ff, model), bf),
            shape((16 * quarter, model), bf),
            shape((16 * quarter, model), bf),
            shape((quarter, model), fl),
            shape((slot, model), bf),
            shape((slot, width), bf),
            shape((slot, 4 * kvt), bf),
            shape((slot, width), bf),
            shape((model, width + kvt), bf),
            shape((width, model), bf),
            shape((8, model), fl),
        ),
        in_specs=[pl.BlockSpec(memory_space=pltpu.SMEM)] + [ANY] * 8,
        out_specs=(ANY,) * 12,
        scratch_shapes=[
            pltpu.VMEM((rows, width), fl),
            pltpu.VMEM((rows, kvt), fl),
            pltpu.VMEM((width, rows), fl),
            pltpu.VMEM(wgu.shape, fl),
            pltpu.VMEM(wd.shape, fl),
            pltpu.VMEM(wgu.shape, bf),
            pltpu.VMEM(wd.shape, bf),
            pltpu.VMEM((slot, model), bf),
            pltpu.VMEM((model, width + kvt), bf),
            pltpu.VMEM((width, model), bf),
            pltpu.VMEM((8, model), fl),
            pltpu.VMEM((slot, model), bf),
            pltpu.VMEM((slot, width), bf),
            pltpu.VMEM((slot, 4 * kvt), bf),
            pltpu.VMEM((slot, width), bf),
            pltpu.VMEM((2, quarter, model), bf),
            pltpu.VMEM((2, quarter, model), bf),
            pltpu.VMEM((quarter, model), bf),
            pltpu.VMEM((quarter, model), bf),
            pltpu.VMEM((quarter, model), fl),
            pltpu.VMEM((quarter, model), bf),
            pltpu.VMEM((quarter, model), bf),
            pltpu.SemaphoreType.DMA((n,)),
            pltpu.SemaphoreType.DMA((n,)),
            pltpu.SemaphoreType.DMA((8,)),
            pltpu.SemaphoreType.DMA((10 + 3 * PIECES,)),
        ],
        compiler_params=remote_params(1),
        name="forward_part",
    )(lengths, wq, wkv, wo, wgu, wd, gains, tokens, cotangent)


ROOT = 0.7978845608028654
CUBE = 0.044715


def z_order(z):
    end = 1 - lax.min(lax.rem(z, 3), 1)
    return (3 - 2 * end, 2 + end, 1 + end, 0)


def block_grads(h, lhs, to_gu, to_d):
    for m, (which, n) in enumerate(((1, 0), (2, 0), (0, 1))):

        @pl.loop(0, h.shape[2] // 512)
        def _(c):
            cols = pl.ds(pl.multiple_of(c * 512, 512), 512)
            grad = inner_rows(lhs[n], h[which, :, cols])
            if m < 2:
                to_gu[m, :, cols] = grad.astype(bf)
            else:
                to_d[cols, :] = grad.T.astype(bf)


def add_to(mine, theirs):
    @pl.loop(0, mine.shape[0] // 64)
    def _(n):
        at = pl.ds(pl.multiple_of(n * 64, 64), 64)
        mine[at] = (mine[at].astype(fl) + theirs[at].astype(fl)).astype(bf)


def ff_kernel(
    nt_hbm, dy_hbm, gu_hbm, d_hbm, hgu_hbm, sums, first_gu, first_d,
    sendc, recvc, sendx, kept, recvx, recvz, recvy_gu, recvy_d,
    send, recv, zsend, zrecv, load, wload, store,
):
    z, r, t = position()
    x, c = t // 2, t % 2
    me = z * 2 + r
    quarter = sums.shape[1]
    other, x_peer, core_peer = (z * 2 + (r ^ 1), t), (me, t ^ 2), (me, t ^ 1)
    drows = recvy_d.shape[1]
    ff, model = d_hbm.shape
    tile = 256
    wide = 1024

    order = (3 * (1 - z // 2), (2 + 3 * z) % 5, 1 + z % 2, z)

    def rows(i, b):
        cc = c if i % 2 else c ^ 1
        xx = x if b else x ^ 1
        return block_rows(order[i // 2], xx * 2 + cc, quarter)

    greet(partners_of(z, r, t, zs=(1, 2)))
    copies = Copies(send, recv)

    middle = lax.min(lax.rem(z, 3), 1)

    def add_x(s, a, places):
        for place in places:
            pltpu.make_async_copy(recvz.at[place, a], recvz.at[place, a], zrecv.at[place, a]).wait()

        @pl.loop(0, model // tile)
        def _(n):
            cols = pl.ds(pl.multiple_of(n * tile, tile), tile)
            total = kept[s, a, :, cols].astype(fl) + recvx[s, a, :, cols].astype(fl)
            for place in places:
                total += recvz[place, a, :, cols].astype(fl)
            if s == 3:
                sums[a, :, cols] = total
            else:
                recvx[s, a, :, cols] = total.astype(bf)

    def z_copy(s, a):
        up = (order[s] + 4 - z) // 5
        there = z + 2 * up - 1
        same = 1 - lax.min((order[s] - there) * (order[s] - there), 1)
        place = order[s] + (1 - up) * same * (4 - order[s])
        return pltpu.make_async_remote_copy(
            src_ref=recvx.at[s, a],
            dst_ref=recvz.at[place, a],
            send_sem=zsend.at[s, a],
            recv_sem=zrecv.at[place, a],
            device_id=(there * 2 + r, t),
            device_id_type=MESH,
        )

    def take_x(s, a, mid):
        copies.arrived(f"x{s}{a}")
        if s == 3:
            low = lax.min(z, 1)
            add_x(s, a, (z, 4) if mid else (low * z + (1 - low) * 4,))
        else:
            add_x(s, a, (order[s],) if mid else ())
            z_copy(s, a).start()

    def take(at_ends, at_middle):
        for mid, parts in enumerate((at_ends, at_middle)):
            if parts:

                @pl.when(middle == mid)
                def _():
                    for s, a in parts:
                        take_x(s, a, bool(mid))

    rest = [(s, a) for s in range(4) for a in range(2)]
    takes = {
        3: (rest[:1], ()),
        4: (rest[1:2], ()),
        5: (rest[2:3], rest[:1]),
        6: (rest[3:4], rest[1:2]),
        7: (rest[4:5], rest[2:4]),
    }
    def layers(wgu, wd, dots, xin, hgu):
        loads = [pltpu.make_async_copy(gu_hbm.at[m], wgu.at[m], wload.at[m]) for m in range(2)]
        loads.append(pltpu.make_async_copy(d_hbm, wd, wload.at[2]))
        for copy in loads:
            copy.start()


        def fetch(i):
            out = []
            for a, src in enumerate((nt_hbm, dy_hbm)):
                for b in range(2):
                    copy = pltpu.make_async_copy(
                        src.at[rows(i, b)],
                        xin.at[i % 2, a, pl.ds(b * quarter, quarter)],
                        load.at[i % 2, a, b],
                    )
                    copy.start()
                    out.append(copy)
            return out

        pending = fetch(0)
        for copy in loads:
            copy.wait()


        stores = {}
        for i in range(8):
            s, own = i // 2, i % 2
            for copy in pending:
                copy.wait()
            if i < 7:
                pending = fetch(i + 1)
            if i >= 2:
                for copy in stores[i - 2]:
                    copy.wait()

            dots[0] = dot(xin[i % 2, 0], wgu[0])
            dots[1] = dot(xin[i % 2, 0], wgu[1])
            dots[2] = times_trans(xin[i % 2, 1], wd[...])

            @pl.loop(0, 2 * quarter // 16)
            def _(n):
                at = pl.ds(pl.multiple_of(n * 16, 16), 16)
                for half in range(0, ff, 512):
                    cols = slice(half, half + 512)
                    gate, upper, dh = dots[0, at, cols], dots[1, at, cols], dots[2, at, cols]
                    square = gate * gate
                    bend = jnp.tanh(ROOT * gate * (1.0 + CUBE * square))
                    share = 0.5 * (1.0 + bend)
                    gelu = gate * share
                    slope = share + 0.5 * gate * (1.0 - bend * bend) * (ROOT * (1.0 + 3.0 * CUBE * square))
                    hgu[i % 2, 0, at, cols] = (gelu * upper).astype(bf)
                    hgu[i % 2, 1, at, cols] = (dh * upper * slope).astype(bf)
                    hgu[i % 2, 2, at, cols] = (dh * gelu).astype(bf)

            stores[i] = []
            for m in range(3):
                for b in range(2):
                    copy = pltpu.make_async_copy(
                        hgu.at[i % 2, m, pl.ds(b * quarter, quarter)],
                        hgu_hbm.at[m, rows(i, b)],
                        store.at[i % 2, m, b],
                    )
                    copy.start()
                    stores[i].append(copy)

            if own:
                copies.arrived(f"c{s}")
                if s >= 2:
                    for a in range(2):
                        copies.left(f"x{s - 2}{a}")
            elif s >= 1:
                copies.left(f"c{s - 1}")

            @pl.loop(0, model // wide)
            def _(n):
                cols = pl.ds(pl.multiple_of(n * wide, wide), wide)
                out = dot(hgu[i % 2, 0], wd[:, cols])
                back = times_trans(hgu[i % 2, 1], wgu[0, cols]) + times_trans(hgu[i % 2, 2], wgu[1, cols])
                for a, part in enumerate((out, back)):
                    if own:
                        total = part + recvc[s % 2, a, :, cols].astype(fl)
                        sendx[s % 2, a, :, cols] = total[:quarter].astype(bf)
                        kept[s, a, :, cols] = total[quarter:].astype(bf)
                    else:
                        sendc[a, :, cols] = part.astype(bf)

            if own:
                for a in range(2):
                    copies.start(
                        f"x{s}{a}",
                        lambda s=s, a=a: sendx.at[s % 2, a],
                        lambda s=s, a=a: recvx.at[s, a],
                        x_peer,
                    )
            else:
                copies.start(f"c{s}", lambda: sendc, lambda s=s: recvc.at[s % 2], core_peer)
            if i in takes:
                take(*takes[i])

        for i in (6, 7):
            for copy in stores[i]:
                copy.wait()

    pl.run_scoped(
        layers,
        pltpu.VMEM((2, model, ff), bf),
        pltpu.VMEM((ff, model), bf),
        pltpu.VMEM((3, 2 * quarter, ff), fl),
        pltpu.VMEM((2, 2, 2 * quarter, model), bf),
        pltpu.VMEM((2, 3, 2 * quarter, ff), bf),
    )

    first = z_order(z)[0]

    def first_grads(h, lhs, to_gu, to_d, own_gu, own_d):
        loads = [pltpu.make_async_copy(hgu_hbm.at[m], h.at[m], wload.at[m]) for m in range(3)]

        def fetch(j):
            block = pl.multiple_of(((z ^ first) * 2 + (r ^ j)) * drows, drows)
            made = []
            for n, src in enumerate((nt_hbm, dy_hbm)):
                copy = pltpu.make_async_copy(src.at[:, pl.ds(block, drows)], lhs.at[n], load.at[0, 0, n])
                copy.start()
                made.append(copy)
            return made

        pending = fetch(1)
        for m in (1, 2, 0):
            loads[m].start()
        for m in (1, 2, 0):
            loads[m].wait()
        for copy in pending:
            copy.wait()
        block_grads(h, lhs, to_gu, to_d)
        for m in range(2):
            copies.start(f"y{m}", lambda m=m: to_gu.at[m], lambda m=m: recvy_gu.at[m], other)
        copies.start("y2", lambda: to_d, lambda: recvy_d, other)
        pending = fetch(0)
        take(rest[5:6], rest[4:6])
        for copy in pending:
            copy.wait()
        block_grads(h, lhs, own_gu, own_d)
        take(rest[6:], rest[6:])
        for m in range(3):
            copies.arrived(f"y{m}")
            mine, theirs = (own_d, recvy_d) if m == 2 else (own_gu.at[m], recvy_gu.at[m])
            add_to(mine, theirs)
            copy = pltpu.make_async_copy(mine, first_d if m == 2 else first_gu.at[m], wload.at[m])
            copy.start()
        for m in range(3):
            mine = own_d if m == 2 else own_gu.at[m]
            pltpu.make_async_copy(mine, first_d if m == 2 else first_gu.at[m], wload.at[m]).wait()
            copies.left(f"y{m}")

    group = nt_hbm.shape[0]
    pl.run_scoped(
        first_grads,
        pltpu.VMEM((3, group, ff), bf),
        pltpu.VMEM((2, group, drows), bf),
        pltpu.VMEM((2, drows, ff), bf),
        pltpu.VMEM((ff, drows), bf),
        pltpu.VMEM((2, drows, ff), bf),
        pltpu.VMEM((ff, drows), bf),
    )
    for s in range(3):
        for a in range(2):
            z_copy(s, a).wait_send()
    copies.all_left()


def feed_forward(nt, dy, wgu, wd):
    group, model = nt.shape
    ff = wd.shape[0]
    quarter = group // 16
    rows = model // 8
    return pl.pallas_call(
        ff_kernel,
        out_shape=(
            jax.ShapeDtypeStruct((3, group, ff), bf),
            jax.ShapeDtypeStruct((2, quarter, model), fl),
            jax.ShapeDtypeStruct((2, rows, ff), bf),
            jax.ShapeDtypeStruct((ff, rows), bf),
        ),
        in_specs=[ANY] * 4,
        out_specs=(ANY, VMEM, ANY, ANY),
        scratch_shapes=[
            pltpu.VMEM((2, 2 * quarter, model), bf),
            pltpu.VMEM((2, 2, 2 * quarter, model), bf),
            pltpu.VMEM((2, 2, quarter, model), bf),
            pltpu.VMEM((4, 2, quarter, model), bf),
            pltpu.VMEM((4, 2, quarter, model), bf),
            pltpu.VMEM((5, 2, quarter, model), bf),
            pltpu.VMEM((2, rows, ff), bf),
            pltpu.VMEM((ff, rows), bf),
            pltpu.SemaphoreType.DMA((15,)),
            pltpu.SemaphoreType.DMA((15,)),
            pltpu.SemaphoreType.DMA((3, 2)),
            pltpu.SemaphoreType.DMA((5, 2)),
            pltpu.SemaphoreType.DMA((2, 2, 2)),
            pltpu.SemaphoreType.DMA((3,)),
            pltpu.SemaphoreType.DMA((2, 3, 2)),
        ],
        compiler_params=remote_params(3),
        name="feed_forward",
    )(nt, dy, wgu, wd)


def backward_kernel(
    lengths, nt_hbm, dy_hbm, hgu_hbm, sums, first_gu, first_d, tokens, resid, gain, one_hbm, q_hbm, kv_hbm, mixed_hbm, qkv_hbm, o_hbm,
    gu_out, d_out, qkv_grad, kv_grad, o_grad, block_out, input_out, gains_out,
    sendy_gu, sendy_d, recvy_gu, recvy_d, own_gu, own_d,
    a, dy_own, x_own, d_resid, out_own, gacc, grecv, gmine, grecv_t,
    gp, dkv_send, dkv_recv, dkv_x, dkv_rx, part, precv, sendx, recvx,
    pk_send, po_send, pk_recv, po_recv, pk_own, po_own, pk_z, po_z,
    send, recv, zsend, zrecv, load, local,
):
    z, r, t = position()
    me = z * 2 + r
    quarter, model = resid.shape
    slot = 4 * quarter
    rows = model // 8
    ff = own_d.shape[1]
    kvt = dkv_x.shape[1]
    width = gp.shape[1] - kvt
    other = (z * 2 + (r ^ 1), t)
    x_peer, core_peer, far_peer = (me, t ^ 2), (me, t ^ 1), (me, t ^ 3)

    def d_block(k, j=0):
        return pl.ds(pl.multiple_of(((z ^ k) * 2 + (r ^ j)) * rows, rows), rows)

    def own_rows(j):
        return pl.ds(pl.multiple_of((t ^ j) * quarter, quarter), quarter)

    loads = [
        pltpu.make_async_copy(sums.at[1], d_resid, load.at[0]),
        pltpu.make_async_copy(sums.at[0], out_own, load.at[1]),
        pltpu.make_async_copy(dy_hbm.at[block_rows(z, t, quarter)], dy_own, load.at[2]),
        pltpu.make_async_copy(tokens.at[own_rows(0)], x_own, load.at[3]),
    ]
    for copy in loads:
        copy.start()
    greet(partners_of(z, r, t, zs=(1, 2, 3)) + [far_peer] + [((z ^ k) * 2 + (r ^ 1), t) for k in (1, 2, 3)])
    copies = Copies(send, recv)
    locals_ = []
    counter = list(range(8))

    def keep(src, dst):
        copy = pltpu.make_async_copy(src, dst, local.at[counter.pop(0)])
        copy.start()
        locals_.append(copy)
        return copy

    def norm_back(v, grad, row):
        inverse = lax.rsqrt(jnp.mean(v * v, axis=-1, keepdims=True) + norm_eps)
        scaled = v * inverse
        gacc[row : row + 1, :] += jnp.sum(grad * scaled, axis=0, keepdims=True)
        inner = grad * gain[row : row + 1, :]
        return inverse * (inner - scaled * jnp.mean(inner * scaled, axis=-1, keepdims=True))

    gacc[...] = jnp.zeros_like(gacc)
    for copy in loads:
        copy.wait()

    @pl.loop(0, quarter // 16)
    def _(i):
        at = pl.ds(pl.multiple_of(i * 16, 16), 16)
        mine = pl.ds(pl.multiple_of(t * quarter + i * 16, 16), 16)
        v = resid[at]
        total = dy_own[at].astype(fl) + norm_back(v, d_resid[at], 1)
        d_resid[at] = total
        a[mine] = total.astype(bf)
        out_own[at] += v

    copies.start("ax", a.at[own_rows(0)], a.at[own_rows(0)], x_peer)
    copies.start("ac", a.at[own_rows(0)], a.at[own_rows(0)], core_peer)
    keep(out_own, block_out.at[own_rows(0)])
    in_own = out_own
    copies.start("bx", out_own, block_out.at[own_rows(0)], x_peer)
    copies.start("bc", out_own, block_out.at[own_rows(0)], core_peer)

    zorder = z_order(z)

    def send_y(i):
        for m in range(2):
            copies.start(f"y{i}{m}", lambda m=m: sendy_gu.at[i - 1, m], lambda m=m: recvy_gu.at[i - 1, m], other)
        copies.start(f"y{i}2", lambda: sendy_d.at[i - 1], lambda: recvy_d.at[i - 1], other)

    flows = [(i, m) for i in (1, 2) for m in range(3)]
    taken = [0]

    def own_of(i, m):
        if i == 0:
            return first_d if m == 2 else first_gu.at[m]
        return own_d.at[i - 1] if m == 2 else own_gu.at[i - 1, m]

    def add_y(i, m):
        add_to(own_of(i, m), recvy_d.at[i - 1] if m == 2 else recvy_gu.at[i - 1, m])

    def place(m):
        cols = pl.ds(pl.multiple_of(z * ff, ff), ff)
        return d_out.at[cols] if m == 2 else gu_out.at[m, :, cols]

    def z_copy(i, m):
        k = zorder[i]
        return pltpu.make_async_remote_copy(
            src_ref=own_of(i, m),
            dst_ref=place(m),
            send_sem=zsend.at[i, m],
            recv_sem=zrecv.at[k - 1, m],
            device_id=at_z(z, r, t, k),
            device_id_type=MESH,
        )

    def pump(n):
        for _ in range(n):
            if taken[0] < len(flows):
                i, m = flows[taken[0]]
                copies.arrived(f"y{i}{m}")
                add_y(i, m)
                z_copy(i, m).start()
                taken[0] += 1

    def feed_forward_grads(first, last, pumps, hgu, lhs):
        loads = [pltpu.make_async_copy(hgu_hbm.at[m], hgu.at[m], load.at[m]) for m in range(3)]

        def fetch(i):
            cols = d_block(zorder[i // 2], 1 - i % 2)
            made = []
            for n, src in enumerate((nt_hbm, dy_hbm)):
                copy = pltpu.make_async_copy(src.at[:, cols], lhs.at[i % 2, n], load.at[3 + 2 * (i % 2) + n])
                copy.start()
                made.append(copy)
            return made

        pending = fetch(first)
        for m in (1, 2, 0):
            loads[m].start()
        for i in range(first, last):
            for copy in pending:
                copy.wait()
            if i < last - 1:
                pending = fetch(i + 1)
            if i == first:
                for m in range(3):
                    loads[m].wait()
            to_gu, to_d = (own_gu, own_d) if i % 2 else (sendy_gu, sendy_d)
            block_grads(hgu, lhs.at[i % 2], to_gu.at[i // 2 - 1], to_d.at[i // 2 - 1])
            if i in (2, 6):
                send_y(i // 2)
            pump(pumps[i - first])

    for m in range(3):
        z_copy(0, m).start()
    group = nt_hbm.shape[0]
    scope = (pltpu.VMEM((3, group, ff), bf), pltpu.VMEM((2, 2, group, rows), bf))
    pl.run_scoped(functools.partial(feed_forward_grads, 2, 5, (0, 1, 0)), *scope)

    copies.arrived("ax")
    copies.start("af", a.at[own_rows(2)], a.at[own_rows(2)], core_peer)
    copies.arrived("bx")
    copies.start("bf", block_out.at[own_rows(2)], block_out.at[own_rows(2)], core_peer)

    pack_order = (1, 3, 2, 0)
    at_zs = [at_z(z, r, t, k) for k in range(4)]
    packs = {"p": (pk_own, pk_recv, pk_z), "o": (po_own, po_recv, po_z)}

    def add_pack(tag, i):
        own, theirs, _ = packs[tag]
        copies.arrived(f"y{tag}{i}")
        own[i] = (own[i].astype(fl) + theirs[i].astype(fl)).astype(bf)

    def send_pack(tag, i, k):
        copies.start(f"z{tag}{i}", lambda: packs[tag][0].at[i], lambda: packs[tag][2].at[i], at_zs[k])

    def pack_first(tag, i):
        add_pack(tag, i)
        send_pack(tag, i, 1)

    def pack_second(tag):
        own, _, came = packs[tag]
        add_pack(tag, 2)
        copies.arrived(f"z{tag}1")
        own[2] = (own[2].astype(fl) + came[1].astype(fl)).astype(bf)
        send_pack(tag, 2, 2)
        add_pack(tag, 3)


    def attention(q, kv, mixed, qkv, o, one, dm, dkv):
        loads = [
            pltpu.make_async_copy(src, dst, load.at[i])
            for i, (src, dst) in enumerate(
                ((o_hbm, o), (q_hbm, q), (kv_hbm, kv), (mixed_hbm, mixed), (qkv_hbm, qkv), (one_hbm, one))
            )
        ]
        for copy in loads:
            copy.start()
        copies.arrived("ac")
        copies.arrived("af")
        for copy in loads:
            copy.wait()
        for i, k in enumerate(pack_order):
            po_send[i] = inner_rows(mixed[...], a[:, d_block(k, 1)]).astype(bf)
            copies.start(f"yo{i}", lambda i=i: po_send.at[i], lambda i=i: po_recv.at[i], other)
        send_y(2)
        for i, k in enumerate(pack_order):
            po_own[i] = inner_rows(mixed[...], a[:, d_block(k, 0)]).astype(bf)
        dm[...] = times_trans(a[...], o[...]).astype(bf)
        length = lengths[0]
        step = 128
        dkv[...] = jnp.zeros_like(dkv)
        for h in range(width // HD):
            head = slice(h * HD, (h + 1) * HD)
            for i in range(slot // step):
                at, upto = pl.ds(i * step, step), pl.ds(0, (i + 1) * step)
                probs = probabilities(q[at, head], kv[upto, :HD], length, i * step)
                d_probs = times_trans(dm[at, head], kv[upto, HD:])
                d_scores = probs * (d_probs - jnp.sum(d_probs * probs, axis=-1, keepdims=True))
                d_raw = (d_scores * HD ** (-0.5)).astype(bf)
                gp[at, head] = dot(d_raw, kv[upto, :HD]).astype(bf)
                dkv[upto, :HD] += inner_rows(d_raw, q[at, head])
                dkv[upto, HD:] += inner_rows(probs.astype(bf), dm[at, head])
            pump(1)

        def kv_cols(j):
            return pl.ds(pl.multiple_of((t ^ j) * kvt, kvt), kvt)

        dkv_send[0] = dkv[:, kv_cols(1)].astype(bf)
        dkv_send[1] = dkv[:, kv_cols(3)].astype(bf)
        copies.start("kc", lambda: dkv_send, lambda: dkv_recv, core_peer)
        copies.arrived("kc")
        dkv_x[...] = (dkv[:, kv_cols(2)] + dkv_recv[1].astype(fl)).astype(bf)
        copies.start("kx", lambda: dkv_x, lambda: dkv_rx, x_peer)
        pack_first("o", 0)
        pack_first("o", 1)
        mine = dkv[:, kv_cols(0)] + dkv_recv[0].astype(fl)
        copies.arrived("kx")
        gp[:, width:] = (mine + dkv_rx[...].astype(fl)).astype(bf)

        def part_of(j, store_part):
            at = own_rows(j)
            for n in range(0, model, 512):
                store_part(times_trans(gp[at], qkv[n : n + 512]), slice(n, n + 512))

        def into_part(i):
            def put(value, cols):
                part[i, :, cols] = value.astype(bf)

            return put

        part_of(3, into_part(0))
        part_of(1, into_part(1))
        copies.start("pc", lambda: part, lambda: precv, core_peer)

        for i, k in enumerate(pack_order):
            pk_send[i] = inner_rows(one[:, d_block(k, 1)], gp[...]).astype(bf)
            copies.start(f"yp{i}", lambda i=i: pk_send.at[i], lambda i=i: pk_recv.at[i], other)

        copies.arrived("pc")

        def into_x(value, cols):
            sendx[:, cols] = (value + precv[0, :, cols].astype(fl)).astype(bf)

        part_of(2, into_x)
        copies.start("px", lambda: sendx, lambda: recvx, x_peer)

        copies.left("bx")
        copies.left("bc")
        locals_.pop(0).wait()

        def into_own(value, cols):
            in_own[:, cols] = value + precv[1, :, cols].astype(fl)

        part_of(0, into_own)
        for i, k in enumerate(pack_order):
            pk_own[i] = inner_rows(one[:, d_block(k, 0)], gp[...]).astype(bf)
        copies.arrived("px")

    pl.run_scoped(
        attention,
        pltpu.VMEM((slot, width), bf),
        pltpu.VMEM((slot, 2 * HD), bf),
        pltpu.VMEM((slot, width), bf),
        pltpu.VMEM((model, width + kvt), bf),
        pltpu.VMEM((width, model), bf),
        pltpu.VMEM((slot, model), bf),
        pltpu.VMEM((slot, width), bf),
        pltpu.VMEM((slot, 2 * HD), fl),
    )
    pl.run_scoped(functools.partial(feed_forward_grads, 5, 8, (1, 1, 1)), *scope)

    @pl.loop(0, quarter // 16)
    def _(i):
        at = pl.ds(pl.multiple_of(i * 16, 16), 16)
        grad = in_own[at] + recvx[at].astype(fl)
        in_own[at] = d_resid[at] + norm_back(x_own[at].astype(fl), grad, 0)

    keep(in_own, input_out.at[own_rows(0)])
    copies.start("ix", in_own, input_out.at[own_rows(0)], x_peer)
    copies.start("ic", in_own, input_out.at[own_rows(0)], core_peer)

    for k in range(4):
        for j in range(2):
            if k or j:
                copies.start(
                    f"g{k}{j}", gacc.at[:, d_block(k, j)], grecv.at[2 * k + j], ((z ^ k) * 2 + (r ^ j), t)
                )
    pump(len(flows))

    pack_second("o")
    pack_first("p", 0)
    pack_first("p", 1)
    pack_second("p")
    total = gacc[:, d_block(0)]
    for k in range(4):
        for j in range(2):
            if k or j:
                copies.arrived(f"g{k}{j}")
                total += grecv[2 * k + j]
    gmine[...] = total
    for j, peer in ((1, core_peer), (2, x_peer), (3, far_peer)):
        copies.start(f"gt{j}", gmine, grecv_t.at[j], peer)
    copies.arrived("ix")
    copies.start("if", input_out.at[own_rows(2)], input_out.at[own_rows(2)], core_peer)

    for m in range(3):
        copies.arrived(f"y3{m}")
        add_y(3, m)
        keep(own_of(3, m), place(m))
    pk_sum = pk_own[3].astype(fl)
    po_sum = po_own[3].astype(fl)
    for i in (0, 2):
        copies.arrived(f"zp{i}")
        copies.arrived(f"zo{i}")
        pk_sum += pk_z[i].astype(fl)
        po_sum += po_z[i].astype(fl)
    qkv_grad[...] = pk_sum
    o_grad[...] = po_sum
    mine = pl.ds(pl.multiple_of(t * kvt, kvt), kvt)
    kv_grad[:, mine] = pk_sum[:, width:]
    for j, peer in ((1, core_peer), (2, x_peer), (3, far_peer)):
        copies.start(f"kg{j}", kv_grad.at[:, mine], kv_grad.at[:, mine], peer)
    total = gmine[...]
    for j in (1, 2, 3):
        copies.arrived(f"gt{j}")
        total += grecv_t[j]
    gains_out[...] = total
    for name in ("ic", "if", "bc", "bf", "kg1", "kg2", "kg3"):
        copies.arrived(name)
    for m in range(3):
        for i in range(3):
            pltpu.make_async_copy(place(m), place(m), zrecv.at[i, m]).wait()
            z_copy(i, m).wait_send()
    copies.all_left()
    for copy in locals_:
        copy.wait()


def backward_part(lengths, nt, dy, hgu, sums, first_gu, first_d, tokens, resid, gain, one, q, kv, mixed, qkv, o):
    group, model = nt.shape
    ff = hgu.shape[2]
    rows = model // 8
    quarter = resid.shape[0]
    slot, width = q.shape
    kvt = qkv.shape[1] - width
    n = 2 + 2 + 2 + 12 + 2 + 8 + 2 + 3 + 7 + 6 + 3 + 3
    shape = jax.ShapeDtypeStruct
    buf = pltpu.VMEM
    return pl.pallas_call(
        backward_kernel,
        out_shape=(
            shape((2, rows, ZN * ff), bf),
            shape((ZN * ff, rows), bf),
            shape((rows, width + kvt), fl),
            shape((rows, 4 * kvt), fl),
            shape((width, rows), fl),
            shape((slot, model), fl),
            shape((slot, model), fl),
            shape((8, rows), fl),
        ),
        in_specs=[pl.BlockSpec(memory_space=pltpu.SMEM)] + [ANY] * 7 + [VMEM] * 2 + [ANY] * 6,
        out_specs=(ANY, ANY, VMEM, VMEM, VMEM, ANY, ANY, VMEM),
        scratch_shapes=[
            buf((3, 2, rows, ff), bf), buf((3, ff, rows), bf),
            buf((3, 2, rows, ff), bf), buf((3, ff, rows), bf),
            buf((3, 2, rows, ff), bf), buf((3, ff, rows), bf),
            buf((slot, model), bf), buf((quarter, model), bf), buf((quarter, model), bf), buf((quarter, model), fl), buf((quarter, model), fl),
            buf((8, model), fl), buf((8, 8, rows), fl), buf((8, rows), fl), buf((4, 8, rows), fl),
            buf((slot, width + kvt), bf), buf((2, slot, kvt), bf), buf((2, slot, kvt), bf),
            buf((slot, kvt), bf), buf((slot, kvt), bf),
            buf((2, quarter, model), bf), buf((2, quarter, model), bf),
            buf((quarter, model), bf), buf((quarter, model), bf),
            buf((4, rows, width + kvt), bf), buf((4, width, rows), bf),
            buf((4, rows, width + kvt), bf), buf((4, width, rows), bf),
            buf((4, rows, width + kvt), bf), buf((4, width, rows), bf),
            buf((3, rows, width + kvt), bf), buf((3, width, rows), bf),
            pltpu.SemaphoreType.DMA((n,)),
            pltpu.SemaphoreType.DMA((n,)),
            pltpu.SemaphoreType.DMA((3, 3)),
            pltpu.SemaphoreType.DMA((3, 3)),
            pltpu.SemaphoreType.DMA((7,)),
            pltpu.SemaphoreType.DMA((8,)),
        ],
        compiler_params=remote_params(4),
        name="backward_part",
    )(lengths, nt, dy, hgu, sums, first_gu, first_d, tokens, resid, gain, one, q, kv, mixed, qkv, o)


def fast(
    tokens,
    cotangent,
    lengths,
    w_query,
    w_keyval,
    w_output,
    w_gateup,
    w_down,
    norm_gains,
    first_query,
    first_keyval,
    first_output,
    first_gateup,
    first_down,
    first_gains,
    second_query,
    second_keyval,
    second_output,
    second_gateup,
    second_down,
    second_gains,
):
    gains_low = jnp.pad(norm_gains.astype(bf).astype(fl), ((0, 6), (0, 0)))
    (
        gateup, down, dy, normed_two, resid, normed_one, query, keyval, mixed, qkv_w, output_w, gain_full,
    ) = forward_part(lengths, w_query, w_keyval, w_output, w_gateup, w_down, gains_low, tokens, cotangent)

    hgu, sums, first_gu, first_d = feed_forward(normed_two, dy, gateup, down)
    (
        gateup_grad, down_grad, qkv_grad, keyval_shard, output_shard, block_output, input_grad, gains_grad,
    ) = backward_part(
        lengths, normed_two, dy, hgu, sums, first_gu, first_d, tokens, resid, gain_full,
        normed_one, query, keyval, mixed, qkv_w, output_w,
    )
    query_shard = qkv_grad[:, : w_query.shape[1]]
    gateup_shard = gateup_grad.astype(fl)
    down_shard = down_grad.astype(fl)
    gains_shard = gains_grad[:2]

    qa = adamw(w_query, query_shard, first_query, second_query, decay_rate)
    ka = adamw(w_keyval, keyval_shard, first_keyval, second_keyval, decay_rate)
    oa = adamw(w_output, output_shard, first_output, second_output, decay_rate)
    ga = adamw(w_gateup, gateup_shard, first_gateup, second_gateup, decay_rate)
    da = adamw(w_down, down_shard, first_down, second_down, decay_rate)
    na = adamw(norm_gains, gains_shard, first_gains, second_gains, 0.0)
    return (block_output, input_grad, *qa, *ka, *oa, *ga, *da, *na)


def solution(mesh):
    query = P("dp", "tensor")
    keyval = P("dp", None)
    output = P("tensor", "dp")
    gateup = P(None, "dp", "tensor")
    gains = P(None, "dp")
    weights = (query, keyval, output, gateup, output, gains)
    return jax.shard_map(
        fast if mesh.shape["dp"] == 2 * ZN and mesh.shape["tensor"] == 4 else general,
        mesh=mesh,
        in_specs=(P("dp", None), P("dp", None), P("dp")) + weights * 3,
        out_specs=(P("dp", None), P("dp", None)) + tuple(w for w in weights for _ in range(4)),
        check_vma=False,
    )
```

```python
import functools

import jax
import jax.numpy as jnp
from jax import lax
from jax.experimental import pallas as pl
from jax.experimental.pallas import tpu as pltpu
from jax.sharding import PartitionSpec as P

HD = 256
ZN = 4

norm_eps = 1e-06
beta_first = 0.9
beta_second = 0.95
learn_rate = 0.01
decay_rate = 0.1
adam_eps = 1e-08
masked_score = -1e30

bf = jnp.bfloat16
fl = jnp.float32


def rms_scale(values, gain):
    inverse = lax.rsqrt(jnp.mean(values * values, axis=-1, keepdims=True) + norm_eps)
    return values * inverse * gain


def dot(left, right):
    return jnp.dot(left, right, preferred_element_type=fl)


def inner_rows(left, right):
    return lax.dot_general(left, right, (((0,), (0,)), ((), ())), preferred_element_type=fl)


def times_trans(left, right):
    return lax.dot_general(left, right, (((1,), (1,)), ((), ())), preferred_element_type=fl)


def slot_scores(query, keyval, length):
    slot = query.shape[0]
    heads = query.shape[1] // HD
    places = jnp.arange(slot)
    allowed = (places[None, :] <= places[:, None]) & (places[None, :] < length)
    raw = jnp.einsum(
        "qhd,kd->hqk",
        query.reshape(slot, heads, HD),
        keyval[:, :HD],
        preferred_element_type=fl,
    )
    return jnp.where(allowed[None], raw * HD ** (-0.5), masked_score)


def slot_forward(query, keyval, length):
    scores = slot_scores(query, keyval, length)
    top = jnp.max(scores, axis=-1, keepdims=True)
    expo = jnp.exp(scores - top)
    total = jnp.sum(expo, axis=-1, keepdims=True)
    probs = expo / total
    mixed = jnp.einsum(
        "hqk,kd->qhd", probs.astype(bf), keyval[:, HD:], preferred_element_type=fl
    )
    return mixed.reshape(query.shape), (top + jnp.log(total))[..., 0]


def slot_backward(query, keyval, length, logsum, grad_mixed):
    slot, width = query.shape
    heads = width // HD
    probs = jnp.exp(slot_scores(query, keyval, length) - logsum[..., None])
    grad_three = grad_mixed.reshape(slot, heads, HD)
    grad_value = jnp.einsum("hqk,qhd->kd", probs.astype(bf), grad_three, preferred_element_type=fl)
    grad_probs = jnp.einsum("qhd,kd->hqk", grad_three, keyval[:, HD:], preferred_element_type=fl)
    grad_scores = probs * (grad_probs - jnp.sum(grad_probs * probs, axis=-1, keepdims=True))
    grad_raw = (grad_scores * HD ** (-0.5)).astype(bf)
    grad_query = jnp.einsum("hqk,kd->qhd", grad_raw, keyval[:, :HD], preferred_element_type=fl)
    grad_key = jnp.einsum(
        "hqk,qhd->kd", grad_raw, query.reshape(slot, heads, HD), preferred_element_type=fl
    )
    return grad_query.reshape(slot, width), jnp.concatenate([grad_key, grad_value], axis=1)


def adamw(weight, grad, first, second, decay):
    first_new = beta_first * first + (1.0 - beta_first) * grad
    second_new = beta_second * second + (1.0 - beta_second) * grad * grad
    update = -learn_rate * (first_new / (jnp.sqrt(second_new) + adam_eps) + decay * weight)
    return (grad, first_new, second_new, update)


def swap(value, step):
    axis, bit = step
    return lax.ppermute(value, axis, [(i, i ^ bit) for i in range(lax.axis_size(axis))])


def offset(position, steps, axis):
    total = 0
    for i, (name, bit) in enumerate(steps):
        if name == axis and position >> i & 1:
            total ^= bit
    return total


def gather(value, steps):
    parts = value[None]
    for step in steps:
        parts = jnp.concatenate([parts, swap(parts, step)], axis=0)
    return parts


def reduce(parts, steps):
    for step in reversed(steps):
        half = parts.shape[0] // 2
        got = swap(parts[half:].astype(bf), step)
        parts = parts[:half].astype(fl) + got.astype(fl)
    return parts[0]


def take(array, index, axis=0):
    return lax.dynamic_index_in_dim(array, index, axis, keepdims=False)


def pick(array, me, steps, axis_name, axis=0):
    return jnp.stack(
        [take(array, me ^ offset(p, steps, axis_name), axis) for p in range(2 ** len(steps))]
    )


def place(parts, me, steps, axis_name, axis=0):
    count = parts.shape[0]
    block = parts.shape[1:]
    shape = block[:axis] + (count,) + block[axis:]
    out = jnp.zeros(shape, parts.dtype)
    for p in range(count):
        out = lax.dynamic_update_index_in_dim(
            out, parts[p], me ^ offset(p, steps, axis_name), axis
        )
    return out


def general(
    tokens,
    cotangent,
    lengths,
    w_query,
    w_keyval,
    w_output,
    w_gateup,
    w_down,
    norm_gains,
    first_query,
    first_keyval,
    first_output,
    first_gateup,
    first_down,
    first_gains,
    second_query,
    second_keyval,
    second_output,
    second_gateup,
    second_down,
    second_gains,
):
    dp = lax.axis_size("dp")
    tn = lax.axis_size("tensor")
    rn = dp // ZN
    me = lax.axis_index("dp")
    z, r = me // rn, me % rn
    t = lax.axis_index("tensor")
    z_steps = [("dp", 2 * rn), ("dp", rn)]
    r_steps = [("dp", 1 << i) for i in reversed(range(rn.bit_length() - 1))]
    t_steps = [("tensor", 1 << i) for i in reversed(range(tn.bit_length() - 1))]
    dp_steps = z_steps + r_steps
    group_steps = z_steps + t_steps

    model = tokens.shape[1]
    rows = model // dp
    slot = tokens.shape[0]
    quarter = slot // tn
    width = w_query.shape[1]
    kvt = w_keyval.shape[1] // tn
    ff = w_down.shape[0] // ZN

    gain_full = place(
        gather(norm_gains.astype(bf), dp_steps), me, dp_steps, "dp", axis=1
    ).reshape(2, model).astype(fl)
    own_keyval = lax.dynamic_slice_in_dim(w_keyval, t * kvt, kvt, 1)
    qkv_w = place(
        gather(jnp.concatenate([w_query, own_keyval], axis=1).astype(bf), dp_steps),
        me, dp_steps, "dp",
    ).reshape(model, width + kvt)
    output_w = place(
        gather(w_output.astype(bf), dp_steps), me, dp_steps, "dp", axis=1
    ).reshape(width, model)

    def zpos(k):
        return ("dp", k * rn)

    gateup_cols = w_gateup.astype(bf).reshape(2, rows, ZN, ff)
    down_rows = w_down.astype(bf).reshape(ZN, ff, rows)
    gateup_w = jnp.zeros((2, ZN, rn, rows, ff), bf)
    down_w = jnp.zeros((ff, ZN, rn, rows), bf)
    for k in range(ZN):
        block = take(gateup_cols, z ^ k, 2)
        if k:
            block = swap(block, zpos(k))
        block = place(gather(block, r_steps), r, r_steps, "dp", axis=1)
        gateup_w = lax.dynamic_update_index_in_dim(gateup_w, block, z ^ k, 1)
    for k in range(ZN):
        block = take(down_rows, z ^ k, 0)
        if k:
            block = swap(block, zpos(k))
        block = place(gather(block, r_steps), r, r_steps, "dp", axis=1)
        down_w = lax.dynamic_update_index_in_dim(down_w, block, z ^ k, 1)
    gateup_w = gateup_w.reshape(2, model, ff)
    down_w = down_w.reshape(ff, model)

    x = tokens.astype(fl)
    length = lengths[0]
    normed_one = rms_scale(x, gain_full[0]).astype(bf)
    projected = dot(normed_one, qkv_w).astype(bf)
    query = projected[:, :width]
    keyval = place(
        gather(projected[:, width:], t_steps), t, t_steps, "tensor", axis=1
    ).reshape(slot, tn * kvt)
    mixed, logsum = slot_forward(query, keyval, length)
    mixed = mixed.astype(bf)
    attn_part = dot(mixed, output_w).astype(bf).reshape(tn, quarter, model)
    attn = reduce(pick(attn_part, t, t_steps, "tensor"), t_steps)
    x_own = lax.dynamic_slice_in_dim(x, t * quarter, quarter, 0)
    resid = x_own + attn
    normed_two_own = rms_scale(resid, gain_full[1]).astype(bf)

    group = ZN * tn * quarter
    normed_two = gather(normed_two_own, group_steps).reshape(group, model)
    cot_own = lax.dynamic_slice_in_dim(cotangent, t * quarter, quarter, 0)
    valid = (t * quarter + jnp.arange(quarter) < length)[:, None]
    grad_own = jnp.where(valid, cot_own, jnp.zeros_like(cot_own))
    grad_low = gather(grad_own, group_steps).reshape(group, model)

    gate = dot(normed_two, gateup_w[0])
    upper = dot(normed_two, gateup_w[1])
    hidden = (jax.nn.gelu(gate, approximate=True) * upper).astype(bf)
    ff_part = dot(hidden, down_w).astype(bf).reshape(ZN * tn, quarter, model)
    out_own = resid + reduce(ff_part, group_steps)
    block_output = place(gather(out_own, t_steps), t, t_steps, "tensor").reshape(slot, model)

    grad_hidden = times_trans(grad_low, down_w)
    _, pull_gelu = jax.vjp(
        lambda left, right: jax.nn.gelu(left, approximate=True) * right, gate, upper
    )
    grad_gate, grad_up = pull_gelu(grad_hidden)
    grad_gate = grad_gate.astype(bf)
    grad_up = grad_up.astype(bf)
    grad_normed = (times_trans(grad_gate, gateup_w[0]) + times_trans(grad_up, gateup_w[1])).astype(bf)
    grad_normed_two = reduce(grad_normed.reshape(ZN * tn, quarter, model), group_steps)

    def columns(array, j):
        return take(array.reshape(group, ZN, rn, rows), r ^ j, 2).reshape(group, ZN * rows)

    def scatter_z(sums, axis):
        parts = []
        for k in range(ZN):
            block = take(sums, z ^ k, 0).astype(bf)
            parts.append(swap(block, zpos(k)) if k else block)
        shape = parts[0].shape
        out = jnp.zeros(shape[:axis] + (ZN,) + shape[axis:], bf)
        for k in range(ZN):
            out = lax.dynamic_update_index_in_dim(out, parts[k], z ^ k, axis)
        return out

    r_offsets = [offset(p, r_steps, "dp") for p in range(rn)]
    down_parts = jnp.stack(
        [
            inner_rows(hidden, columns(grad_low, j)).astype(bf).reshape(ff, ZN, rows)
            for j in r_offsets
        ]
    )
    down_sum = reduce(down_parts, r_steps)
    down_shard = scatter_z(jnp.moveaxis(down_sum, 1, 0), 0).reshape(ZN * ff, rows).astype(fl)

    shards_gu = []
    for grad in (grad_gate, grad_up):
        parts = jnp.stack(
            [
                inner_rows(columns(normed_two, j), grad).astype(bf).reshape(ZN, rows, ff)
                for j in r_offsets
            ]
        )
        sums = reduce(parts, r_steps)
        shards_gu.append(scatter_z(sums, 1).reshape(rows, ZN * ff).astype(fl))
    gateup_shard = jnp.stack(shards_gu)

    _, pull_second = jax.vjp(rms_scale, resid, gain_full[1])
    grad_resid_norm, grad_gain_two = pull_second(grad_normed_two)
    grad_resid = grad_own.astype(fl) + grad_resid_norm
    grad_attn = place(gather(grad_resid.astype(bf), t_steps), t, t_steps, "tensor").reshape(slot, model)

    output_grad = inner_rows(mixed, grad_attn).astype(bf)
    grad_mixed = times_trans(grad_attn, output_w).astype(bf)
    grad_query, grad_keyval = slot_backward(query, keyval, length, logsum, grad_mixed)
    keyval_parts = grad_keyval.astype(bf).reshape(slot, tn, kvt)
    keyval_low = reduce(pick(keyval_parts, t, t_steps, "tensor", axis=1), t_steps).astype(bf)
    grad_projected = jnp.concatenate([grad_query.astype(bf), keyval_low], axis=1)
    one_parts = times_trans(grad_projected, qkv_w).astype(bf).reshape(tn, quarter, model)
    grad_normed_one = reduce(pick(one_parts, t, t_steps, "tensor"), t_steps)
    qkv_grad = inner_rows(normed_one, grad_projected).astype(bf)
    _, pull_first = jax.vjp(rms_scale, x_own, gain_full[0])
    grad_x_norm, grad_gain_one = pull_first(grad_normed_one)
    input_own = grad_resid + grad_x_norm
    input_grad = place(gather(input_own, t_steps), t, t_steps, "tensor").reshape(slot, model)

    qkv_shard = reduce(
        pick(qkv_grad.reshape(dp, rows, width + kvt), me, dp_steps, "dp"), dp_steps
    )
    query_shard = qkv_shard[:, :width]
    keyval_shard = place(
        gather(qkv_shard[:, width:].astype(bf), t_steps), t, t_steps, "tensor", axis=1
    ).reshape(rows, tn * kvt).astype(fl)
    output_shard = reduce(
        pick(output_grad.reshape(width, dp, rows), me, dp_steps, "dp", axis=1), dp_steps
    )
    gains_grad = jnp.stack([grad_gain_one, grad_gain_two]).reshape(2, dp, rows)
    gains_parts = pick(gains_grad, me, dp_steps, "dp", axis=1)
    for step in reversed(dp_steps):
        half = gains_parts.shape[0] // 2
        gains_parts = gains_parts[:half] + swap(gains_parts[half:], step)
    gains_shard = gains_parts[0]
    for step in t_steps:
        gains_shard = gains_shard + swap(gains_shard, step)

    qa = adamw(w_query, query_shard, first_query, second_query, decay_rate)
    ka = adamw(w_keyval, keyval_shard, first_keyval, second_keyval, decay_rate)
    oa = adamw(w_output, output_shard, first_output, second_output, decay_rate)
    ga = adamw(w_gateup, gateup_shard, first_gateup, second_gateup, decay_rate)
    da = adamw(w_down, down_shard, first_down, second_down, decay_rate)
    na = adamw(norm_gains, gains_shard, first_gains, second_gains, 0.0)
    return (block_output, input_grad, *qa, *ka, *oa, *ga, *da, *na)


MESH = pl.DeviceIdType.MESH
ANY = pl.BlockSpec(memory_space=pl.ANY)
VMEM = pl.BlockSpec(memory_space=pltpu.VMEM)
LIMIT = 127 * 512 * 1024
WINDOW = 1
PIECES = 1


def position():
    me = lax.axis_index("dp")
    t = lax.axis_index("tensor")
    return me // 2, me % 2, t


def at_z(z, r, t, k):
    return ((z ^ k) * 2 + r, t)


def greet(partners):
    barrier = pltpu.get_barrier_semaphore()
    for device in partners:
        pl.semaphore_signal(barrier, inc=1, device_id=device, device_id_type=MESH)
    pl.semaphore_wait(barrier, len(partners))


class Copies:
    def __init__(self, send, recv):
        self.send, self.recv, self.made, self.gone = send, recv, {}, set()

    def start(self, name, src, dst, device, sent=None, got=None):
        i = len(self.made)
        make = lambda: pltpu.make_async_remote_copy(
            src_ref=src() if callable(src) else src,
            dst_ref=dst() if callable(dst) else dst,
            send_sem=self.send.at[i],
            recv_sem=self.recv.at[i],
            device_id=device,
            device_id_type=MESH,
        )
        self.made[name] = (make, sent, got)
        maybe(sent, lambda: make().start())

    def arrived(self, name):
        make, _, got = self.made[name]
        maybe(got, lambda: make().wait_recv())

    def left(self, name):
        if name not in self.gone:
            self.gone.add(name)
            make, sent, _ = self.made[name]
            maybe(sent, lambda: make().wait_send())

    def all_left(self, keep=lambda name: True):
        for name in self.made:
            if keep(name):
                self.left(name)


def maybe(condition, action):
    if condition is None:
        action()
    else:
        pl.when(condition)(action)


class Line:
    def __init__(self):
        self.z, self.r, self.t = position()

    def block(self, way, s):
        return lax.max(lax.min(self.z - way * s, 3), 0)

    def device(self, way):
        return (lax.max(lax.min(self.z + way, 3), 0) * 2 + self.r, self.t)

    def sent(self, way, s):
        if way > 0:
            return (self.z < 3) & (self.z >= s)
        return (self.z > 0) & (self.z + s <= 3)

    def got(self, way, s):
        return self.z >= 1 + s if way > 0 else self.z + 1 + s <= 3


WAYS = ((1, "u"), (-1, "d"))


def remote_params(number, limit=LIMIT):
    return pltpu.CompilerParams(
        collective_id=number, has_side_effects=True, vmem_limit_bytes=limit
    )


def block_rows(z, t, quarter):
    return pl.ds(pl.multiple_of((z * 4 + t) * quarter, quarter), quarter)


class TokenGather:
    count = 27

    def __init__(self, copies, own, out, tag):
        self.copies, self.own, self.out, self.tag = copies, own, out, tag
        self.line = Line()
        self.z, self.r, self.t = position()
        self.quarter = own.shape[0]

    def rows(self, b, j):
        return self.out.at[block_rows(b, self.t ^ j, self.quarter)]

    def send_z(self, s):
        for way, mark in WAYS:
            b = self.line.block(way, s)
            self.copies.start(
                f"{self.tag}z{mark}{s}",
                self.own if s == 0 else self.rows(b, 0),
                self.rows(b, 0),
                self.line.device(way),
                self.line.sent(way, s),
                self.line.got(way, s),
            )

    def over(self, name, src, b, j, step, got):
        self.copies.start(
            self.tag + name, src, self.rows(b, j), (self.z * 2 + self.r, self.t ^ step), got, got
        )

    def send_own(self):
        self.over("xo", self.own, self.z, 0, 2, None)
        self.over("co0", self.own, self.z, 0, 1, None)

    def take_z(self, s):
        for way, mark in WAYS:
            self.copies.arrived(f"{self.tag}z{mark}{s}")
        if s < 2:
            self.send_z(s + 1)
        for way, mark in WAYS:
            b, got = self.line.block(way, s + 1), self.line.got(way, s)
            self.over(f"x{mark}{s}", self.rows(b, 0), b, 0, 2, got)
            self.over(f"c{mark}{s}0", self.rows(b, 0), b, 0, 1, got)

    def take_own(self):
        self.copies.arrived(f"{self.tag}xo")
        self.over("co1", self.rows(self.z, 2), self.z, 2, 1, None)

    def take_x(self, s):
        for way, mark in WAYS:
            self.copies.arrived(f"{self.tag}x{mark}{s}")
            b = self.line.block(way, s + 1)
            self.over(f"c{mark}{s}1", self.rows(b, 2), b, 2, 1, self.line.got(way, s))

    def finish(self):
        for name in list(self.copies.made):
            if name.startswith(self.tag + "c"):
                self.copies.arrived(name)
        self.copies.all_left(lambda name: name.startswith(self.tag))


def partners_of(z, r, t, zs=(1, 2, 3), y=True, tensor=True):
    out = [at_z(z, r, t, k) for k in zs]
    if y:
        out.append((z * 2 + (r ^ 1), t))
    if tensor:
        out += [(z * 2 + r, t ^ 2), (z * 2 + r, t ^ 1)]
    return out


def rms_into(src, gain, dst, slab=16):
    @pl.loop(0, dst.shape[0] // slab)
    def _(i):
        rows = pl.ds(pl.multiple_of(i * slab, slab), slab)
        v = src[rows].astype(fl)
        inverse = lax.rsqrt(jnp.mean(v * v, axis=-1, keepdims=True) + norm_eps)
        dst[rows] = (v * inverse * gain).astype(bf)


def cast_into(src, dst, slab=16):
    @pl.loop(0, src.shape[0] // slab)
    def _(i):
        rows = pl.ds(pl.multiple_of(i * slab, slab), slab)
        dst[rows] = src[rows].astype(bf)


def probabilities(q, key, length, first):
    scores = times_trans(q, key) * HD ** (-0.5)
    row = first + lax.broadcasted_iota(jnp.int32, scores.shape, 0)
    col = lax.broadcasted_iota(jnp.int32, scores.shape, 1)
    scores = jnp.where((col <= row) & (col < length), scores, masked_score)
    expo = jnp.exp(scores - jnp.max(scores, axis=-1, keepdims=True))
    return expo / jnp.sum(expo, axis=-1, keepdims=True)


def forward_kernel(
    lengths, wq, wkv, wo, wgu, wd, gains, tokens, cotangent,
    gu_out, d_out, dy_out, nt_out, resid_out, one_out, q_out, kv_out, mixed_out, qkv_out, o_out, gain_out,
    wq_f, wkv_f, wo_f, gu_f, d_f, gu_b, d_b, x, qkv, o, gain, one, q, kv, mixed,
    part, recvc, sendx, recvx, resid, nt_own, dy,
    send, recv, load, store,
):
    z, r, t = position()
    me = z * 2 + r
    rows = wq.shape[0]
    slot, model = tokens.shape
    quarter = slot // 4
    width = wq.shape[1]
    kvt = qkv.shape[1] - width
    ff = d_out.shape[0]
    other = (z * 2 + (r ^ 1), t)
    x_peer, core_peer, far_peer = (me, t ^ 2), (me, t ^ 1), (me, t ^ 3)

    def d_block(k):
        return pl.ds(pl.multiple_of(((z ^ k) * 2 + r) * rows, rows), rows)

    def f_block(k):
        return pl.ds(pl.multiple_of((z ^ k) * ff, ff), ff)

    kv_cols = pl.ds(pl.multiple_of(t * kvt, kvt), kvt)
    loads = [
        pltpu.make_async_copy(wq, wq_f, load.at[0]),
        pltpu.make_async_copy(wkv.at[:, kv_cols], wkv_f, load.at[1]),
        pltpu.make_async_copy(wo, wo_f, load.at[2]),
        pltpu.make_async_copy(gains, gain.at[:, d_block(0)], load.at[3]),
        pltpu.make_async_copy(
            cotangent.at[pl.ds(pl.multiple_of(t * quarter, quarter), quarter)], dy, load.at[7]
        ),
        pltpu.make_async_copy(tokens, x, load.at[4]),
        pltpu.make_async_copy(wgu, gu_f, load.at[5]),
        pltpu.make_async_copy(wd, d_f, load.at[6]),
    ]
    for copy in loads:
        copy.start()
    stores = []

    def keep(src, dst):
        copy = pltpu.make_async_copy(src, dst, store.at[len(stores)])
        copy.start()
        stores.append(copy)

    for copy in loads[:5]:
        copy.wait()
    length = lengths[0]

    @pl.loop(0, quarter // 16)
    def _(i):
        at = pl.ds(pl.multiple_of(i * 16, 16), 16)
        row = t * quarter + i * 16 + lax.broadcasted_iota(jnp.int32, (16, model), 0)
        dy[at] = jnp.where(row < length, dy[at].astype(fl), 0.0).astype(bf)

    keep(dy, dy_out.at[block_rows(z, t, quarter)])

    @pl.loop(0, rows // 16)
    def _(i):
        own = pl.ds(pl.multiple_of(me * rows + i * 16, 16), 16)
        at = pl.ds(pl.multiple_of(i * 16, 16), 16)
        qkv[own, pl.ds(0, width)] = wq_f[at].astype(bf)
        qkv[own, pl.ds(width, kvt)] = wkv_f[at].astype(bf)

    @pl.loop(0, width // 16)
    def _(i):
        at = pl.ds(pl.multiple_of(i * 16, 16), 16)
        o[at, d_block(0)] = wo_f[at].astype(bf)

    greet(partners_of(z, r, t, zs=(1, 2, 3)) + [far_peer] + [((z ^ k) * 2 + (r ^ 1), t) for k in (1, 2, 3)])
    copies = Copies(send, recv)
    d = TokenGather(copies, dy, dy_out, "d")

    for k in range(4):
        for j in range(2):
            if k or j:
                copies.start(
                    f"g{k}{j}", gain.at[:, d_block(0)], gain.at[:, d_block(0)], ((z ^ k) * 2 + (r ^ j), t)
                )

    line = Line()

    def pack_send(tag, name, b, device, sent=None, got=None):
        at = pl.ds(pl.multiple_of((b * 2 + r) * rows, rows), rows)
        ref = qkv.at[at] if tag == "q" else o.at[:, at]
        copies.start(tag + name, ref, ref, device, sent, got)

    def pack_step(tag, s):
        for way, mark in WAYS:
            sent, got = line.sent(way, s), line.got(way, s)
            pack_send(tag, f"z{mark}{s}", line.block(way, s), line.device(way), sent, got)

    def pack_take(tag, s):
        for way, mark in WAYS:
            copies.arrived(f"{tag}z{mark}{s}")
        if s < 2:
            pack_step(tag, s + 1)
        for way, mark in WAYS:
            got = line.got(way, s)
            pack_send(tag, f"y{mark}{s}", line.block(way, s + 1), other, got, got)

    def pack_wait(tag):
        for name in ["o"] + [mark + str(s) for s in range(3) for _, mark in WAYS]:
            copies.arrived(tag + "y" + name)

    pack_step("q", 0)
    pack_send("q", "yo", z, other)
    d.send_own()

    for copy in loads[5:]:
        copy.wait()
    for m in range(2):
        cast_into(gu_f.at[m], gu_b.at[m])
    cast_into(d_f, d_b, 64)

    pieces = PIECES

    def owned(m, k, p):
        if m == 2:
            n = ff // pieces
            return d_b.at[pl.ds(pl.multiple_of((z ^ k) * ff + p * n, n), n)]
        n = rows // pieces
        return gu_b.at[m, p * n : (p + 1) * n, f_block(k)]

    def landed(m, k, p):
        if m == 2:
            n = ff // pieces
            return d_out.at[p * n : (p + 1) * n, d_block(k)]
        n = rows // pieces
        return gu_out.at[m, pl.ds(pl.multiple_of(((z ^ k) * 2 + r) * rows + p * n, n), n)]

    flows = [(m, k, p) for m in range(3) for k in (1, 3, 2) for p in range(pieces)]
    counts = [0, 0]

    def issue():
        if counts[0] < len(flows):
            m, k, p = flows[counts[0]]
            copies.start(f"wz{k}{m}{p}", owned(m, k, p), landed(m, 0, p), at_z(z, r, t, k))
            counts[0] += 1

    def forward(m, k, p):
        copies.start(f"wy{k}{m}{p}", owned(m, 0, p) if k == 0 else landed(m, k, p), landed(m, k, p), other)

    def pump(n, more=True):
        for _ in range(n):
            if counts[1] < counts[0]:
                m, k, p = flows[counts[1]]
                copies.arrived(f"wz{k}{m}{p}")
                forward(m, k, p)
                counts[1] += 1
            if more:
                issue()

    for _ in range(WINDOW):
        issue()
    for m in range(3):
        for p in range(pieces):
            keep(owned(m, 0, p), landed(m, 0, p))

    for k in range(4):
        for j in range(2):
            if k or j:
                copies.arrived(f"g{k}{j}")
    keep(gain, gain_out)
    rms_into(x, gain[0:1, :], one)
    keep(one, one_out)

    pack_take("q", 0)
    pack_take("q", 1)
    d.send_z(0)
    pack_step("o", 0)
    for _ in range(WINDOW):
        issue()
    pack_take("q", 2)
    pack_send("o", "yo", z, other)
    pack_wait("q")
    for p in range(pieces):
        forward(0, 0, p)
    keep(qkv, qkv_out)

    kv[:, kv_cols] = dot(one[...], qkv[:, width:]).astype(bf)
    for name, peer in (("k1", core_peer), ("k2", x_peer), ("k3", far_peer)):
        copies.start(name, kv.at[:, kv_cols], kv.at[:, kv_cols], peer)
    q[...] = dot(one[...], qkv[:, :width]).astype(bf)
    keep(q, q_out)
    pack_take("o", 0)
    for name in ("k1", "k2", "k3"):
        copies.arrived(name)
    keep(kv, kv_out)
    for p in range(pieces):
        forward(1, 0, p)
    step = 128
    for h in range(width // HD):
        for i in range(slot // step):
            at, upto = pl.ds(i * step, step), pl.ds(0, (i + 1) * step)
            probs = probabilities(q[at, h * HD : (h + 1) * HD], kv[upto, :HD], length, i * step)
            mixed[at, h * HD : (h + 1) * HD] = dot(probs.astype(bf), kv[upto, HD:]).astype(bf)
        if h == 0:
            pack_take("o", 1)
            pump(1)
    keep(mixed, mixed_out)
    pack_take("o", 2)
    pump(1)
    pack_wait("o")
    keep(o, o_out)
    for p in range(pieces):
        forward(2, 0, p)
    d.take_z(0)
    d.take_own()

    def part_of(j, store_part):
        at = pl.ds(pl.multiple_of((t ^ j) * quarter, quarter), quarter)
        for n in range(0, model, 512):
            store_part(dot(mixed[at], o[:, n : n + 512]), slice(n, n + 512))

    def into_part(i):
        def put(value, cols):
            part[i, :, cols] = value.astype(bf)

        return put

    part_of(3, into_part(0))
    part_of(1, into_part(1))
    copies.start("a1", part, recvc, core_peer)
    pump(1)
    copies.arrived("a1")

    def into_x(value, cols):
        sendx[:, cols] = (value + recvc[0, :, cols].astype(fl)).astype(bf)

    part_of(2, into_x)
    copies.start("a2", sendx, recvx, x_peer)

    def into_resid(value, cols):
        resid[:, cols] = value + recvc[1, :, cols].astype(fl)

    part_of(0, into_resid)
    d.take_z(1)
    d.take_x(0)
    copies.arrived("a2")
    first_row = t * quarter

    @pl.loop(0, quarter // 16)
    def _(i):
        at = pl.ds(pl.multiple_of(i * 16, 16), 16)
        mine = pl.ds(pl.multiple_of(first_row + i * 16, 16), 16)
        v = x[mine].astype(fl) + (resid[at] + recvx[at].astype(fl))
        resid[at] = v
        inverse = lax.rsqrt(jnp.mean(v * v, axis=-1, keepdims=True) + norm_eps)
        nt_own[at] = (v * inverse * gain[1:2, :]).astype(bf)

    keep(resid, resid_out)
    keep(nt_own, nt_out.at[block_rows(z, t, quarter)])
    n = TokenGather(copies, nt_own, nt_out, "n")
    n.send_z(0)
    n.send_own()
    pump(2)
    d.take_z(2)
    d.take_x(1)
    n.take_z(0)
    n.take_own()
    pump(2)
    d.take_x(2)
    n.take_z(1)
    n.take_x(0)
    pump(2)
    n.take_z(2)
    n.take_x(1)
    pump(2)
    n.take_x(2)
    pump(len(flows))
    n.finish()
    d.finish()
    for k in range(4):
        for m in range(3):
            for p in range(pieces):
                copies.arrived(f"wy{k}{m}{p}")
    copies.all_left(lambda name: name[0] not in "nd")
    for copy in stores:
        copy.wait()


def forward_part(lengths, wq, wkv, wo, wgu, wd, gains, tokens, cotangent):
    rows, width = wq.shape
    slot, model = tokens.shape
    quarter = slot // 4
    kvt = wkv.shape[1] // 4
    ff = wd.shape[0] // ZN
    n = 7 + 26 + 21 * PIECES + 3 + 2 + 2 * TokenGather.count
    shape = jax.ShapeDtypeStruct
    return pl.pallas_call(
        forward_kernel,
        out_shape=(
            shape((2, model, ff), bf),
            shape((ff, model), bf),
            shape((16 * quarter, model), bf),
            shape((16 * quarter, model), bf),
            shape((quarter, model), fl),
            shape((slot, model), bf),
            shape((slot, width), bf),
            shape((slot, 4 * kvt), bf),
            shape((slot, width), bf),
            shape((model, width + kvt), bf),
            shape((width, model), bf),
            shape((8, model), fl),
        ),
        in_specs=[pl.BlockSpec(memory_space=pltpu.SMEM)] + [ANY] * 8,
        out_specs=(ANY,) * 12,
        scratch_shapes=[
            pltpu.VMEM((rows, width), fl),
            pltpu.VMEM((rows, kvt), fl),
            pltpu.VMEM((width, rows), fl),
            pltpu.VMEM(wgu.shape, fl),
            pltpu.VMEM(wd.shape, fl),
            pltpu.VMEM(wgu.shape, bf),
            pltpu.VMEM(wd.shape, bf),
            pltpu.VMEM((slot, model), bf),
            pltpu.VMEM((model, width + kvt), bf),
            pltpu.VMEM((width, model), bf),
            pltpu.VMEM((8, model), fl),
            pltpu.VMEM((slot, model), bf),
            pltpu.VMEM((slot, width), bf),
            pltpu.VMEM((slot, 4 * kvt), bf),
            pltpu.VMEM((slot, width), bf),
            pltpu.VMEM((2, quarter, model), bf),
            pltpu.VMEM((2, quarter, model), bf),
            pltpu.VMEM((quarter, model), bf),
            pltpu.VMEM((quarter, model), bf),
            pltpu.VMEM((quarter, model), fl),
            pltpu.VMEM((quarter, model), bf),
            pltpu.VMEM((quarter, model), bf),
            pltpu.SemaphoreType.DMA((n,)),
            pltpu.SemaphoreType.DMA((n,)),
            pltpu.SemaphoreType.DMA((8,)),
            pltpu.SemaphoreType.DMA((10 + 3 * PIECES,)),
        ],
        compiler_params=remote_params(1),
        name="forward_part",
    )(lengths, wq, wkv, wo, wgu, wd, gains, tokens, cotangent)


ROOT = 0.7978845608028654
CUBE = 0.044715


def z_order(z):
    end = 1 - lax.min(lax.rem(z, 3), 1)
    return (3 - 2 * end, 2 + end, 1 + end, 0)


def block_grads(h, lhs, to_gu, to_d):
    for m, (which, n) in enumerate(((1, 0), (2, 0), (0, 1))):

        @pl.loop(0, h.shape[2] // 512)
        def _(c):
            cols = pl.ds(pl.multiple_of(c * 512, 512), 512)
            grad = inner_rows(lhs[n], h[which, :, cols])
            if m < 2:
                to_gu[m, :, cols] = grad.astype(bf)
            else:
                to_d[cols, :] = grad.T.astype(bf)


def add_to(mine, theirs):
    @pl.loop(0, mine.shape[0] // 64)
    def _(n):
        at = pl.ds(pl.multiple_of(n * 64, 64), 64)
        mine[at] = (mine[at].astype(fl) + theirs[at].astype(fl)).astype(bf)


def ff_kernel(
    nt_hbm, dy_hbm, gu_hbm, d_hbm, hgu_hbm, sums, first_gu, first_d,
    sendc, recvc, sendx, kept, recvx, recvz, recvy_gu, recvy_d,
    send, recv, zsend, zrecv, load, wload, store,
):
    z, r, t = position()
    x, c = t // 2, t % 2
    me = z * 2 + r
    quarter = sums.shape[1]
    other, x_peer, core_peer = (z * 2 + (r ^ 1), t), (me, t ^ 2), (me, t ^ 1)
    drows = recvy_d.shape[1]
    ff, model = d_hbm.shape
    tile = 256
    wide = 1024

    order = (3 * (1 - z // 2), (2 + 3 * z) % 5, 1 + z % 2, z)

    def rows(i, b):
        cc = c if i % 2 else c ^ 1
        xx = x if b else x ^ 1
        return block_rows(order[i // 2], xx * 2 + cc, quarter)

    greet(partners_of(z, r, t, zs=(1, 2)))
    copies = Copies(send, recv)

    middle = lax.min(lax.rem(z, 3), 1)

    def add_x(s, a, places):
        for place in places:
            pltpu.make_async_copy(recvz.at[place, a], recvz.at[place, a], zrecv.at[place, a]).wait()

        @pl.loop(0, model // tile)
        def _(n):
            cols = pl.ds(pl.multiple_of(n * tile, tile), tile)
            total = kept[s, a, :, cols].astype(fl) + recvx[s, a, :, cols].astype(fl)
            for place in places:
                total += recvz[place, a, :, cols].astype(fl)
            if s == 3:
                sums[a, :, cols] = total
            else:
                recvx[s, a, :, cols] = total.astype(bf)

    def z_copy(s, a):
        up = (order[s] + 4 - z) // 5
        there = z + 2 * up - 1
        same = 1 - lax.min((order[s] - there) * (order[s] - there), 1)
        place = order[s] + (1 - up) * same * (4 - order[s])
        return pltpu.make_async_remote_copy(
            src_ref=recvx.at[s, a],
            dst_ref=recvz.at[place, a],
            send_sem=zsend.at[s, a],
            recv_sem=zrecv.at[place, a],
            device_id=(there * 2 + r, t),
            device_id_type=MESH,
        )

    def take_x(s, a, mid):
        copies.arrived(f"x{s}{a}")
        if s == 3:
            low = lax.min(z, 1)
            add_x(s, a, (z, 4) if mid else (low * z + (1 - low) * 4,))
        else:
            add_x(s, a, (order[s],) if mid else ())
            z_copy(s, a).start()

    def take(at_ends, at_middle):
        for mid, parts in enumerate((at_ends, at_middle)):
            if parts:

                @pl.when(middle == mid)
                def _():
                    for s, a in parts:
                        take_x(s, a, bool(mid))

    rest = [(s, a) for s in range(4) for a in range(2)]
    takes = {
        3: (rest[:1], ()),
        4: (rest[1:2], ()),
        5: (rest[2:3], rest[:1]),
        6: (rest[3:4], rest[1:2]),
    }
    def layers(wgu, wd, dots, xin, hgu):
        loads = [pltpu.make_async_copy(gu_hbm.at[m], wgu.at[m], wload.at[m]) for m in range(2)]
        loads.append(pltpu.make_async_copy(d_hbm, wd, wload.at[2]))
        for copy in loads:
            copy.start()


        def fetch(i):
            out = []
            for a, src in enumerate((nt_hbm, dy_hbm)):
                for b in range(2):
                    copy = pltpu.make_async_copy(
                        src.at[rows(i, b)],
                        xin.at[i % 2, a, pl.ds(b * quarter, quarter)],
                        load.at[i % 2, a, b],
                    )
                    copy.start()
                    out.append(copy)
            return out

        pending = fetch(0)


        stores = {}
        for i in range(8):
            s, own = i // 2, i % 2
            for copy in pending:
                copy.wait()
            if i < 7:
                pending = fetch(i + 1)
            if i >= 2:
                for copy in stores[i - 2]:
                    copy.wait()

            if i == 0:
                loads[0].wait()
            dots[0] = dot(xin[i % 2, 0], wgu[0])
            if i == 0:
                loads[1].wait()
            dots[1] = dot(xin[i % 2, 0], wgu[1])
            if i == 0:
                loads[2].wait()
            dots[2] = times_trans(xin[i % 2, 1], wd[...])

            @pl.loop(0, 2 * quarter // 16)
            def _(n):
                at = pl.ds(pl.multiple_of(n * 16, 16), 16)
                for half in range(0, ff, 512):
                    cols = slice(half, half + 512)
                    gate, upper, dh = dots[0, at, cols], dots[1, at, cols], dots[2, at, cols]
                    square = gate * gate
                    bend = jnp.tanh(ROOT * gate * (1.0 + CUBE * square))
                    share = 0.5 * (1.0 + bend)
                    gelu = gate * share
                    slope = share + 0.5 * gate * (1.0 - bend * bend) * (ROOT * (1.0 + 3.0 * CUBE * square))
                    hgu[i % 2, 0, at, cols] = (gelu * upper).astype(bf)
                    hgu[i % 2, 1, at, cols] = (dh * upper * slope).astype(bf)
                    hgu[i % 2, 2, at, cols] = (dh * gelu).astype(bf)

            stores[i] = []
            for m in range(3):
                for b in range(2):
                    copy = pltpu.make_async_copy(
                        hgu.at[i % 2, m, pl.ds(b * quarter, quarter)],
                        hgu_hbm.at[m, rows(i, b)],
                        store.at[i % 2, m, b],
                    )
                    copy.start()
                    stores[i].append(copy)

            if own:
                copies.arrived(f"c{s}")
                if s >= 2:
                    for a in range(2):
                        copies.left(f"x{s - 2}{a}")
            elif s >= 1:
                copies.left(f"c{s - 1}")

            @pl.loop(0, model // wide)
            def _(n):
                cols = pl.ds(pl.multiple_of(n * wide, wide), wide)
                out = dot(hgu[i % 2, 0], wd[:, cols])
                back = times_trans(hgu[i % 2, 1], wgu[0, cols]) + times_trans(hgu[i % 2, 2], wgu[1, cols])
                for a, part in enumerate((out, back)):
                    if own:
                        total = part + recvc[s % 2, a, :, cols].astype(fl)
                        sendx[s % 2, a, :, cols] = total[:quarter].astype(bf)
                        kept[s, a, :, cols] = total[quarter:].astype(bf)
                    else:
                        sendc[a, :, cols] = part.astype(bf)

            if own:
                for a in range(2):
                    copies.start(
                        f"x{s}{a}",
                        lambda s=s, a=a: sendx.at[s % 2, a],
                        lambda s=s, a=a: recvx.at[s, a],
                        x_peer,
                    )
            else:
                copies.start(f"c{s}", lambda: sendc, lambda s=s: recvc.at[s % 2], core_peer)
            if i in takes:
                take(*takes[i])

        for i in (6, 7):
            for copy in stores[i]:
                copy.wait()

    pl.run_scoped(
        layers,
        pltpu.VMEM((2, model, ff), bf),
        pltpu.VMEM((ff, model), bf),
        pltpu.VMEM((3, 2 * quarter, ff), fl),
        pltpu.VMEM((2, 2, 2 * quarter, model), bf),
        pltpu.VMEM((2, 3, 2 * quarter, ff), bf),
    )

    first = z_order(z)[0]

    def first_grads(h, lhs, to_gu, to_d, own_gu, own_d):
        loads = [pltpu.make_async_copy(hgu_hbm.at[m], h.at[m], wload.at[m]) for m in range(3)]

        def fetch(j):
            block = pl.multiple_of(((z ^ first) * 2 + (r ^ j)) * drows, drows)
            made = []
            for n, src in enumerate((nt_hbm, dy_hbm)):
                copy = pltpu.make_async_copy(src.at[:, pl.ds(block, drows)], lhs.at[n], load.at[0, 0, n])
                copy.start()
                made.append(copy)
            return made

        pending = fetch(1)
        for m in (1, 2, 0):
            loads[m].start()
        take(rest[4:5], rest[2:4])
        for m in (1, 2, 0):
            loads[m].wait()
        for copy in pending:
            copy.wait()
        block_grads(h, lhs, to_gu, to_d)
        for m in range(2):
            copies.start(f"y{m}", lambda m=m: to_gu.at[m], lambda m=m: recvy_gu.at[m], other)
        copies.start("y2", lambda: to_d, lambda: recvy_d, other)
        pending = fetch(0)
        take(rest[5:6], rest[4:6])
        for copy in pending:
            copy.wait()
        block_grads(h, lhs, own_gu, own_d)
        take(rest[6:], rest[6:])
        for m in range(3):
            copies.arrived(f"y{m}")
            mine, theirs = (own_d, recvy_d) if m == 2 else (own_gu.at[m], recvy_gu.at[m])
            add_to(mine, theirs)
            copy = pltpu.make_async_copy(mine, first_d if m == 2 else first_gu.at[m], wload.at[m])
            copy.start()
        for m in range(3):
            mine = own_d if m == 2 else own_gu.at[m]
            pltpu.make_async_copy(mine, first_d if m == 2 else first_gu.at[m], wload.at[m]).wait()
            copies.left(f"y{m}")

    group = nt_hbm.shape[0]
    pl.run_scoped(
        first_grads,
        pltpu.VMEM((3, group, ff), bf),
        pltpu.VMEM((2, group, drows), bf),
        pltpu.VMEM((2, drows, ff), bf),
        pltpu.VMEM((ff, drows), bf),
        pltpu.VMEM((2, drows, ff), bf),
        pltpu.VMEM((ff, drows), bf),
    )
    for s in range(3):
        for a in range(2):
            z_copy(s, a).wait_send()
    copies.all_left()


def feed_forward(nt, dy, wgu, wd):
    group, model = nt.shape
    ff = wd.shape[0]
    quarter = group // 16
    rows = model // 8
    return pl.pallas_call(
        ff_kernel,
        out_shape=(
            jax.ShapeDtypeStruct((3, group, ff), bf),
            jax.ShapeDtypeStruct((2, quarter, model), fl),
            jax.ShapeDtypeStruct((2, rows, ff), bf),
            jax.ShapeDtypeStruct((ff, rows), bf),
        ),
        in_specs=[ANY] * 4,
        out_specs=(ANY, VMEM, ANY, ANY),
        scratch_shapes=[
            pltpu.VMEM((2, 2 * quarter, model), bf),
            pltpu.VMEM((2, 2, 2 * quarter, model), bf),
            pltpu.VMEM((2, 2, quarter, model), bf),
            pltpu.VMEM((4, 2, quarter, model), bf),
            pltpu.VMEM((4, 2, quarter, model), bf),
            pltpu.VMEM((5, 2, quarter, model), bf),
            pltpu.VMEM((2, rows, ff), bf),
            pltpu.VMEM((ff, rows), bf),
            pltpu.SemaphoreType.DMA((15,)),
            pltpu.SemaphoreType.DMA((15,)),
            pltpu.SemaphoreType.DMA((3, 2)),
            pltpu.SemaphoreType.DMA((5, 2)),
            pltpu.SemaphoreType.DMA((2, 2, 2)),
            pltpu.SemaphoreType.DMA((3,)),
            pltpu.SemaphoreType.DMA((2, 3, 2)),
        ],
        compiler_params=remote_params(3),
        name="feed_forward",
    )(nt, dy, wgu, wd)


def backward_kernel(
    lengths, nt_hbm, dy_hbm, hgu_hbm, sums, first_gu, first_d, tokens, resid, gain, one_hbm, q_hbm, kv_hbm, mixed_hbm, qkv_hbm, o_hbm,
    gu_out, d_out, qkv_grad, kv_grad, o_grad, block_out, input_out, gains_out,
    sendy_gu, sendy_d, recvy_gu, recvy_d, own_gu, own_d,
    a, dy_own, x_own, d_resid, out_own, gacc, grecv, gmine, grecv_t,
    gp, dkv_send, dkv_recv, dkv_x, dkv_rx, part, precv, sendx, recvx,
    pk_send, po_send, pk_recv, po_recv, pk_own, po_own, pk_z, po_z,
    send, recv, zsend, zrecv, load, local,
):
    z, r, t = position()
    me = z * 2 + r
    quarter, model = resid.shape
    slot = 4 * quarter
    rows = model // 8
    ff = own_d.shape[1]
    kvt = dkv_x.shape[1]
    width = gp.shape[1] - kvt
    other = (z * 2 + (r ^ 1), t)
    x_peer, core_peer, far_peer = (me, t ^ 2), (me, t ^ 1), (me, t ^ 3)

    def d_block(k, j=0):
        return pl.ds(pl.multiple_of(((z ^ k) * 2 + (r ^ j)) * rows, rows), rows)

    def own_rows(j):
        return pl.ds(pl.multiple_of((t ^ j) * quarter, quarter), quarter)

    first_loads = [
        pltpu.make_async_copy(sums.at[1], d_resid, load.at[7]),
        pltpu.make_async_copy(sums.at[0], out_own, load.at[8]),
        pltpu.make_async_copy(dy_hbm.at[block_rows(z, t, quarter)], dy_own, load.at[9]),
        pltpu.make_async_copy(tokens.at[own_rows(0)], x_own, load.at[10]),
    ]
    for copy in first_loads:
        copy.start()
    greet(partners_of(z, r, t, zs=(1, 2, 3)) + [far_peer] + [((z ^ k) * 2 + (r ^ 1), t) for k in (1, 2, 3)])
    copies = Copies(send, recv)
    locals_ = []
    counter = list(range(7))

    def keep(src, dst):
        copy = pltpu.make_async_copy(src, dst, local.at[counter.pop(0)])
        copy.start()
        locals_.append(copy)
        return copy

    def norm_back(v, grad, row):
        inverse = lax.rsqrt(jnp.mean(v * v, axis=-1, keepdims=True) + norm_eps)
        scaled = v * inverse
        gacc[row : row + 1, :] += jnp.sum(grad * scaled, axis=0, keepdims=True)
        inner = grad * gain[row : row + 1, :]
        return inverse * (inner - scaled * jnp.mean(inner * scaled, axis=-1, keepdims=True))

    gacc[...] = jnp.zeros_like(gacc)
    in_own = out_own

    zorder = z_order(z)

    def send_y(i):
        for m in range(2):
            copies.start(f"y{i}{m}", lambda m=m: sendy_gu.at[i - 1, m], lambda m=m: recvy_gu.at[i - 1, m], other)
        copies.start(f"y{i}2", lambda: sendy_d.at[i - 1], lambda: recvy_d.at[i - 1], other)

    flows = [(i, m) for i in (1, 2) for m in range(3)]
    taken = [0]

    def own_of(i, m):
        if i == 0:
            return first_d if m == 2 else first_gu.at[m]
        return own_d.at[i - 1] if m == 2 else own_gu.at[i - 1, m]

    def add_y(i, m):
        add_to(own_of(i, m), recvy_d.at[i - 1] if m == 2 else recvy_gu.at[i - 1, m])

    def place(m):
        cols = pl.ds(pl.multiple_of(z * ff, ff), ff)
        return d_out.at[cols] if m == 2 else gu_out.at[m, :, cols]

    def z_copy(i, m):
        k = zorder[i]
        return pltpu.make_async_remote_copy(
            src_ref=own_of(i, m),
            dst_ref=place(m),
            send_sem=zsend.at[i, m],
            recv_sem=zrecv.at[k - 1, m],
            device_id=at_z(z, r, t, k),
            device_id_type=MESH,
        )

    def pump(n):
        for _ in range(n):
            if taken[0] < len(flows):
                i, m = flows[taken[0]]
                copies.arrived(f"y{i}{m}")
                add_y(i, m)
                z_copy(i, m).start()
                taken[0] += 1

    def block_copy():
        return pltpu.make_async_copy(out_own, block_out.at[own_rows(0)], local.at[7])

    def second_norm():
        for copy in first_loads:
            copy.wait()

        @pl.loop(0, quarter // 16)
        def _(i):
            at = pl.ds(pl.multiple_of(i * 16, 16), 16)
            mine = pl.ds(pl.multiple_of(t * quarter + i * 16, 16), 16)
            v = resid[at]
            total = dy_own[at].astype(fl) + norm_back(v, d_resid[at], 1)
            d_resid[at] = total
            a[mine] = total.astype(bf)
            out_own[at] += v

        copies.start("ax", lambda: a.at[own_rows(0)], lambda: a.at[own_rows(0)], x_peer)
        copies.start("ac", lambda: a.at[own_rows(0)], lambda: a.at[own_rows(0)], core_peer)
        block_copy().start()
        copies.start("bx", lambda: out_own, lambda: block_out.at[own_rows(0)], x_peer)
        copies.start("bc", lambda: out_own, lambda: block_out.at[own_rows(0)], core_peer)

    def feed_forward_grads(first, last, pumps, hgu, lhs):
        loads = [pltpu.make_async_copy(hgu_hbm.at[m], hgu.at[m], load.at[m]) for m in range(3)]

        def fetch(i):
            cols = d_block(zorder[i // 2], 1 - i % 2)
            made = []
            for n, src in enumerate((nt_hbm, dy_hbm)):
                copy = pltpu.make_async_copy(src.at[:, cols], lhs.at[i % 2, n], load.at[3 + 2 * (i % 2) + n])
                copy.start()
                made.append(copy)
            return made

        pending = fetch(first)
        for m in (1, 2, 0):
            loads[m].start()
        if first == 2:
            second_norm()
        for i in range(first, last):
            for copy in pending:
                copy.wait()
            if i < last - 1:
                pending = fetch(i + 1)
            if i == first:
                for m in range(3):
                    loads[m].wait()
            to_gu, to_d = (own_gu, own_d) if i % 2 else (sendy_gu, sendy_d)
            block_grads(hgu, lhs.at[i % 2], to_gu.at[i // 2 - 1], to_d.at[i // 2 - 1])
            if i in (2, 6):
                send_y(i // 2)
            pump(pumps[i - first])

    for m in range(3):
        z_copy(0, m).start()
    group = nt_hbm.shape[0]
    scope = (pltpu.VMEM((3, group, ff), bf), pltpu.VMEM((2, 2, group, rows), bf))
    pl.run_scoped(functools.partial(feed_forward_grads, 2, 5, (0, 1, 0)), *scope)

    copies.arrived("ax")
    copies.start("af", a.at[own_rows(2)], a.at[own_rows(2)], core_peer)
    copies.arrived("bx")
    copies.start("bf", block_out.at[own_rows(2)], block_out.at[own_rows(2)], core_peer)

    pack_order = (1, 3, 2, 0)
    at_zs = [at_z(z, r, t, k) for k in range(4)]
    packs = {"p": (pk_own, pk_recv, pk_z), "o": (po_own, po_recv, po_z)}

    def add_pack(tag, i):
        own, theirs, _ = packs[tag]
        copies.arrived(f"y{tag}{i}")
        own[i] = (own[i].astype(fl) + theirs[i].astype(fl)).astype(bf)

    def send_pack(tag, i, k):
        copies.start(f"z{tag}{i}", lambda: packs[tag][0].at[i], lambda: packs[tag][2].at[i], at_zs[k])

    def pack_first(tag, i):
        add_pack(tag, i)
        send_pack(tag, i, 1)

    def pack_second(tag):
        own, _, came = packs[tag]
        add_pack(tag, 2)
        copies.arrived(f"z{tag}1")
        own[2] = (own[2].astype(fl) + came[1].astype(fl)).astype(bf)
        send_pack(tag, 2, 2)
        add_pack(tag, 3)


    def attention(q, kv, mixed, qkv, o, one, dm, dkv):
        loads = [
            pltpu.make_async_copy(src, dst, load.at[i])
            for i, (src, dst) in enumerate(
                ((o_hbm, o), (q_hbm, q), (kv_hbm, kv), (mixed_hbm, mixed), (qkv_hbm, qkv), (one_hbm, one))
            )
        ]
        for copy in loads:
            copy.start()
        copies.arrived("ac")
        copies.arrived("af")
        for copy in loads:
            copy.wait()
        for i, k in enumerate(pack_order):
            po_send[i] = inner_rows(mixed[...], a[:, d_block(k, 1)]).astype(bf)
            copies.start(f"yo{i}", lambda i=i: po_send.at[i], lambda i=i: po_recv.at[i], other)
        send_y(2)
        for i, k in enumerate(pack_order):
            po_own[i] = inner_rows(mixed[...], a[:, d_block(k, 0)]).astype(bf)
        dm[...] = times_trans(a[...], o[...]).astype(bf)
        length = lengths[0]
        step = 128
        dkv[...] = jnp.zeros_like(dkv)
        for h in range(width // HD):
            head = slice(h * HD, (h + 1) * HD)
            for i in range(slot // step):
                at, upto = pl.ds(i * step, step), pl.ds(0, (i + 1) * step)
                probs = probabilities(q[at, head], kv[upto, :HD], length, i * step)
                d_probs = times_trans(dm[at, head], kv[upto, HD:])
                d_scores = probs * (d_probs - jnp.sum(d_probs * probs, axis=-1, keepdims=True))
                d_raw = (d_scores * HD ** (-0.5)).astype(bf)
                gp[at, head] = dot(d_raw, kv[upto, :HD]).astype(bf)
                dkv[upto, :HD] += inner_rows(d_raw, q[at, head])
                dkv[upto, HD:] += inner_rows(probs.astype(bf), dm[at, head])
            pump(1)

        def kv_cols(j):
            return pl.ds(pl.multiple_of((t ^ j) * kvt, kvt), kvt)

        dkv_send[0] = dkv[:, kv_cols(1)].astype(bf)
        dkv_send[1] = dkv[:, kv_cols(3)].astype(bf)
        copies.start("kc", lambda: dkv_send, lambda: dkv_recv, core_peer)
        copies.arrived("kc")
        dkv_x[...] = (dkv[:, kv_cols(2)] + dkv_recv[1].astype(fl)).astype(bf)
        copies.start("kx", lambda: dkv_x, lambda: dkv_rx, x_peer)
        pack_first("o", 0)
        pack_first("o", 1)
        mine = dkv[:, kv_cols(0)] + dkv_recv[0].astype(fl)
        copies.arrived("kx")
        gp[:, width:] = (mine + dkv_rx[...].astype(fl)).astype(bf)

        def part_of(j, store_part):
            at = own_rows(j)
            for n in range(0, model, 512):
                store_part(times_trans(gp[at], qkv[n : n + 512]), slice(n, n + 512))

        def into_part(i):
            def put(value, cols):
                part[i, :, cols] = value.astype(bf)

            return put

        part_of(3, into_part(0))
        part_of(1, into_part(1))
        copies.start("pc", lambda: part, lambda: precv, core_peer)

        for i, k in enumerate(pack_order):
            pk_send[i] = inner_rows(one[:, d_block(k, 1)], gp[...]).astype(bf)
            copies.start(f"yp{i}", lambda i=i: pk_send.at[i], lambda i=i: pk_recv.at[i], other)

        copies.arrived("pc")

        def into_x(value, cols):
            sendx[:, cols] = (value + precv[0, :, cols].astype(fl)).astype(bf)

        part_of(2, into_x)
        copies.start("px", lambda: sendx, lambda: recvx, x_peer)

        copies.left("bx")
        copies.left("bc")
        block_copy().wait()

        def into_own(value, cols):
            in_own[:, cols] = value + precv[1, :, cols].astype(fl)

        part_of(0, into_own)
        for i, k in enumerate(pack_order):
            pk_own[i] = inner_rows(one[:, d_block(k, 0)], gp[...]).astype(bf)
        copies.arrived("px")

    pl.run_scoped(
        attention,
        pltpu.VMEM((slot, width), bf),
        pltpu.VMEM((slot, 2 * HD), bf),
        pltpu.VMEM((slot, width), bf),
        pltpu.VMEM((model, width + kvt), bf),
        pltpu.VMEM((width, model), bf),
        pltpu.VMEM((slot, model), bf),
        pltpu.VMEM((slot, width), bf),
        pltpu.VMEM((slot, 2 * HD), fl),
    )
    pl.run_scoped(functools.partial(feed_forward_grads, 5, 8, (1, 1, 1)), *scope)

    @pl.loop(0, quarter // 16)
    def _(i):
        at = pl.ds(pl.multiple_of(i * 16, 16), 16)
        grad = in_own[at] + recvx[at].astype(fl)
        in_own[at] = d_resid[at] + norm_back(x_own[at].astype(fl), grad, 0)

    keep(in_own, input_out.at[own_rows(0)])
    copies.start("ix", in_own, input_out.at[own_rows(0)], x_peer)
    copies.start("ic", in_own, input_out.at[own_rows(0)], core_peer)

    for k in range(4):
        for j in range(2):
            if k or j:
                copies.start(
                    f"g{k}{j}", gacc.at[:, d_block(k, j)], grecv.at[2 * k + j], ((z ^ k) * 2 + (r ^ j), t)
                )
    pump(len(flows))

    pack_second("o")
    pack_first("p", 0)
    pack_first("p", 1)
    pack_second("p")
    total = gacc[:, d_block(0)]
    for k in range(4):
        for j in range(2):
            if k or j:
                copies.arrived(f"g{k}{j}")
                total += grecv[2 * k + j]
    gmine[...] = total
    for j, peer in ((1, core_peer), (2, x_peer), (3, far_peer)):
        copies.start(f"gt{j}", gmine, grecv_t.at[j], peer)
    copies.arrived("ix")
    copies.start("if", input_out.at[own_rows(2)], input_out.at[own_rows(2)], core_peer)

    for m in range(3):
        copies.arrived(f"y3{m}")
        add_y(3, m)
        keep(own_of(3, m), place(m))
    pk_sum = pk_own[3].astype(fl)
    po_sum = po_own[3].astype(fl)
    for i in (0, 2):
        copies.arrived(f"zp{i}")
        copies.arrived(f"zo{i}")
        pk_sum += pk_z[i].astype(fl)
        po_sum += po_z[i].astype(fl)
    qkv_grad[...] = pk_sum
    o_grad[...] = po_sum
    mine = pl.ds(pl.multiple_of(t * kvt, kvt), kvt)
    kv_grad[:, mine] = pk_sum[:, width:]
    for j, peer in ((1, core_peer), (2, x_peer), (3, far_peer)):
        copies.start(f"kg{j}", kv_grad.at[:, mine], kv_grad.at[:, mine], peer)
    total = gmine[...]
    for j in (1, 2, 3):
        copies.arrived(f"gt{j}")
        total += grecv_t[j]
    gains_out[...] = total
    for name in ("ic", "if", "bc", "bf", "kg1", "kg2", "kg3"):
        copies.arrived(name)
    for m in range(3):
        for i in range(3):
            pltpu.make_async_copy(place(m), place(m), zrecv.at[i, m]).wait()
            z_copy(i, m).wait_send()
    copies.all_left()
    for copy in locals_:
        copy.wait()


def backward_part(lengths, nt, dy, hgu, sums, first_gu, first_d, tokens, resid, gain, one, q, kv, mixed, qkv, o):
    group, model = nt.shape
    ff = hgu.shape[2]
    rows = model // 8
    quarter = resid.shape[0]
    slot, width = q.shape
    kvt = qkv.shape[1] - width
    n = 2 + 2 + 2 + 12 + 2 + 8 + 2 + 3 + 7 + 6 + 3 + 3
    shape = jax.ShapeDtypeStruct
    buf = pltpu.VMEM
    return pl.pallas_call(
        backward_kernel,
        out_shape=(
            shape((2, rows, ZN * ff), bf),
            shape((ZN * ff, rows), bf),
            shape((rows, width + kvt), fl),
            shape((rows, 4 * kvt), fl),
            shape((width, rows), fl),
            shape((slot, model), fl),
            shape((slot, model), fl),
            shape((8, rows), fl),
        ),
        in_specs=[pl.BlockSpec(memory_space=pltpu.SMEM)] + [ANY] * 7 + [VMEM] * 2 + [ANY] * 6,
        out_specs=(ANY, ANY, VMEM, VMEM, VMEM, ANY, ANY, VMEM),
        scratch_shapes=[
            buf((3, 2, rows, ff), bf), buf((3, ff, rows), bf),
            buf((3, 2, rows, ff), bf), buf((3, ff, rows), bf),
            buf((3, 2, rows, ff), bf), buf((3, ff, rows), bf),
            buf((slot, model), bf), buf((quarter, model), bf), buf((quarter, model), bf), buf((quarter, model), fl), buf((quarter, model), fl),
            buf((8, model), fl), buf((8, 8, rows), fl), buf((8, rows), fl), buf((4, 8, rows), fl),
            buf((slot, width + kvt), bf), buf((2, slot, kvt), bf), buf((2, slot, kvt), bf),
            buf((slot, kvt), bf), buf((slot, kvt), bf),
            buf((2, quarter, model), bf), buf((2, quarter, model), bf),
            buf((quarter, model), bf), buf((quarter, model), bf),
            buf((4, rows, width + kvt), bf), buf((4, width, rows), bf),
            buf((4, rows, width + kvt), bf), buf((4, width, rows), bf),
            buf((4, rows, width + kvt), bf), buf((4, width, rows), bf),
            buf((3, rows, width + kvt), bf), buf((3, width, rows), bf),
            pltpu.SemaphoreType.DMA((n,)),
            pltpu.SemaphoreType.DMA((n,)),
            pltpu.SemaphoreType.DMA((3, 3)),
            pltpu.SemaphoreType.DMA((3, 3)),
            pltpu.SemaphoreType.DMA((11,)),
            pltpu.SemaphoreType.DMA((8,)),
        ],
        compiler_params=remote_params(4),
        name="backward_part",
    )(lengths, nt, dy, hgu, sums, first_gu, first_d, tokens, resid, gain, one, q, kv, mixed, qkv, o)


def fast(
    tokens,
    cotangent,
    lengths,
    w_query,
    w_keyval,
    w_output,
    w_gateup,
    w_down,
    norm_gains,
    first_query,
    first_keyval,
    first_output,
    first_gateup,
    first_down,
    first_gains,
    second_query,
    second_keyval,
    second_output,
    second_gateup,
    second_down,
    second_gains,
):
    gains_low = jnp.pad(norm_gains.astype(bf).astype(fl), ((0, 6), (0, 0)))
    (
        gateup, down, dy, normed_two, resid, normed_one, query, keyval, mixed, qkv_w, output_w, gain_full,
    ) = forward_part(lengths, w_query, w_keyval, w_output, w_gateup, w_down, gains_low, tokens, cotangent)

    hgu, sums, first_gu, first_d = feed_forward(normed_two, dy, gateup, down)
    (
        gateup_grad, down_grad, qkv_grad, keyval_shard, output_shard, block_output, input_grad, gains_grad,
    ) = backward_part(
        lengths, normed_two, dy, hgu, sums, first_gu, first_d, tokens, resid, gain_full,
        normed_one, query, keyval, mixed, qkv_w, output_w,
    )
    query_shard = qkv_grad[:, : w_query.shape[1]]
    gateup_shard = gateup_grad.astype(fl)
    down_shard = down_grad.astype(fl)
    gains_shard = gains_grad[:2]

    qa = adamw(w_query, query_shard, first_query, second_query, decay_rate)
    ka = adamw(w_keyval, keyval_shard, first_keyval, second_keyval, decay_rate)
    oa = adamw(w_output, output_shard, first_output, second_output, decay_rate)
    ga = adamw(w_gateup, gateup_shard, first_gateup, second_gateup, decay_rate)
    da = adamw(w_down, down_shard, first_down, second_down, decay_rate)
    na = adamw(norm_gains, gains_shard, first_gains, second_gains, 0.0)
    return (block_output, input_grad, *qa, *ka, *oa, *ga, *da, *na)


def solution(mesh):
    query = P("dp", "tensor")
    keyval = P("dp", None)
    output = P("tensor", "dp")
    gateup = P(None, "dp", "tensor")
    gains = P(None, "dp")
    weights = (query, keyval, output, gateup, output, gains)
    return jax.shard_map(
        fast if mesh.shape["dp"] == 2 * ZN and mesh.shape["tensor"] == 4 else general,
        mesh=mesh,
        in_specs=(P("dp", None), P("dp", None), P("dp")) + weights * 3,
        out_specs=(P("dp", None), P("dp", None)) + tuple(w for w in weights for _ in range(4)),
        check_vma=False,
    )
```

```python
import functools

import jax
import jax.numpy as jnp
from jax import lax
from jax.experimental import pallas as pl
from jax.experimental.pallas import tpu as pltpu
from jax.sharding import PartitionSpec as P

HD = 256
ZN = 4

norm_eps = 1e-06
beta_first = 0.9
beta_second = 0.95
learn_rate = 0.01
decay_rate = 0.1
adam_eps = 1e-08
masked_score = -1e30

bf = jnp.bfloat16
fl = jnp.float32


def rms_scale(values, gain):
    inverse = lax.rsqrt(jnp.mean(values * values, axis=-1, keepdims=True) + norm_eps)
    return values * inverse * gain


def dot(left, right):
    return jnp.dot(left, right, preferred_element_type=fl)


def inner_rows(left, right):
    return lax.dot_general(left, right, (((0,), (0,)), ((), ())), preferred_element_type=fl)


def times_trans(left, right):
    return lax.dot_general(left, right, (((1,), (1,)), ((), ())), preferred_element_type=fl)


def slot_scores(query, keyval, length):
    slot = query.shape[0]
    heads = query.shape[1] // HD
    places = jnp.arange(slot)
    allowed = (places[None, :] <= places[:, None]) & (places[None, :] < length)
    raw = jnp.einsum(
        "qhd,kd->hqk",
        query.reshape(slot, heads, HD),
        keyval[:, :HD],
        preferred_element_type=fl,
    )
    return jnp.where(allowed[None], raw * HD ** (-0.5), masked_score)


def slot_forward(query, keyval, length):
    scores = slot_scores(query, keyval, length)
    top = jnp.max(scores, axis=-1, keepdims=True)
    expo = jnp.exp(scores - top)
    total = jnp.sum(expo, axis=-1, keepdims=True)
    probs = expo / total
    mixed = jnp.einsum(
        "hqk,kd->qhd", probs.astype(bf), keyval[:, HD:], preferred_element_type=fl
    )
    return mixed.reshape(query.shape), (top + jnp.log(total))[..., 0]


def slot_backward(query, keyval, length, logsum, grad_mixed):
    slot, width = query.shape
    heads = width // HD
    probs = jnp.exp(slot_scores(query, keyval, length) - logsum[..., None])
    grad_three = grad_mixed.reshape(slot, heads, HD)
    grad_value = jnp.einsum("hqk,qhd->kd", probs.astype(bf), grad_three, preferred_element_type=fl)
    grad_probs = jnp.einsum("qhd,kd->hqk", grad_three, keyval[:, HD:], preferred_element_type=fl)
    grad_scores = probs * (grad_probs - jnp.sum(grad_probs * probs, axis=-1, keepdims=True))
    grad_raw = (grad_scores * HD ** (-0.5)).astype(bf)
    grad_query = jnp.einsum("hqk,kd->qhd", grad_raw, keyval[:, :HD], preferred_element_type=fl)
    grad_key = jnp.einsum(
        "hqk,qhd->kd", grad_raw, query.reshape(slot, heads, HD), preferred_element_type=fl
    )
    return grad_query.reshape(slot, width), jnp.concatenate([grad_key, grad_value], axis=1)


def adamw(weight, grad, first, second, decay):
    first_new = beta_first * first + (1.0 - beta_first) * grad
    second_new = beta_second * second + (1.0 - beta_second) * grad * grad
    update = -learn_rate * (first_new / (jnp.sqrt(second_new) + adam_eps) + decay * weight)
    return (grad, first_new, second_new, update)


def swap(value, step):
    axis, bit = step
    return lax.ppermute(value, axis, [(i, i ^ bit) for i in range(lax.axis_size(axis))])


def offset(position, steps, axis):
    total = 0
    for i, (name, bit) in enumerate(steps):
        if name == axis and position >> i & 1:
            total ^= bit
    return total


def gather(value, steps):
    parts = value[None]
    for step in steps:
        parts = jnp.concatenate([parts, swap(parts, step)], axis=0)
    return parts


def reduce(parts, steps):
    for step in reversed(steps):
        half = parts.shape[0] // 2
        got = swap(parts[half:].astype(bf), step)
        parts = parts[:half].astype(fl) + got.astype(fl)
    return parts[0]


def take(array, index, axis=0):
    return lax.dynamic_index_in_dim(array, index, axis, keepdims=False)


def pick(array, me, steps, axis_name, axis=0):
    return jnp.stack(
        [take(array, me ^ offset(p, steps, axis_name), axis) for p in range(2 ** len(steps))]
    )


def place(parts, me, steps, axis_name, axis=0):
    count = parts.shape[0]
    block = parts.shape[1:]
    shape = block[:axis] + (count,) + block[axis:]
    out = jnp.zeros(shape, parts.dtype)
    for p in range(count):
        out = lax.dynamic_update_index_in_dim(
            out, parts[p], me ^ offset(p, steps, axis_name), axis
        )
    return out


def general(
    tokens,
    cotangent,
    lengths,
    w_query,
    w_keyval,
    w_output,
    w_gateup,
    w_down,
    norm_gains,
    first_query,
    first_keyval,
    first_output,
    first_gateup,
    first_down,
    first_gains,
    second_query,
    second_keyval,
    second_output,
    second_gateup,
    second_down,
    second_gains,
):
    dp = lax.axis_size("dp")
    tn = lax.axis_size("tensor")
    rn = dp // ZN
    me = lax.axis_index("dp")
    z, r = me // rn, me % rn
    t = lax.axis_index("tensor")
    z_steps = [("dp", 2 * rn), ("dp", rn)]
    r_steps = [("dp", 1 << i) for i in reversed(range(rn.bit_length() - 1))]
    t_steps = [("tensor", 1 << i) for i in reversed(range(tn.bit_length() - 1))]
    dp_steps = z_steps + r_steps
    group_steps = z_steps + t_steps

    model = tokens.shape[1]
    rows = model // dp
    slot = tokens.shape[0]
    quarter = slot // tn
    width = w_query.shape[1]
    kvt = w_keyval.shape[1] // tn
    ff = w_down.shape[0] // ZN

    gain_full = place(
        gather(norm_gains.astype(bf), dp_steps), me, dp_steps, "dp", axis=1
    ).reshape(2, model).astype(fl)
    own_keyval = lax.dynamic_slice_in_dim(w_keyval, t * kvt, kvt, 1)
    qkv_w = place(
        gather(jnp.concatenate([w_query, own_keyval], axis=1).astype(bf), dp_steps),
        me, dp_steps, "dp",
    ).reshape(model, width + kvt)
    output_w = place(
        gather(w_output.astype(bf), dp_steps), me, dp_steps, "dp", axis=1
    ).reshape(width, model)

    def zpos(k):
        return ("dp", k * rn)

    gateup_cols = w_gateup.astype(bf).reshape(2, rows, ZN, ff)
    down_rows = w_down.astype(bf).reshape(ZN, ff, rows)
    gateup_w = jnp.zeros((2, ZN, rn, rows, ff), bf)
    down_w = jnp.zeros((ff, ZN, rn, rows), bf)
    for k in range(ZN):
        block = take(gateup_cols, z ^ k, 2)
        if k:
            block = swap(block, zpos(k))
        block = place(gather(block, r_steps), r, r_steps, "dp", axis=1)
        gateup_w = lax.dynamic_update_index_in_dim(gateup_w, block, z ^ k, 1)
    for k in range(ZN):
        block = take(down_rows, z ^ k, 0)
        if k:
            block = swap(block, zpos(k))
        block = place(gather(block, r_steps), r, r_steps, "dp", axis=1)
        down_w = lax.dynamic_update_index_in_dim(down_w, block, z ^ k, 1)
    gateup_w = gateup_w.reshape(2, model, ff)
    down_w = down_w.reshape(ff, model)

    x = tokens.astype(fl)
    length = lengths[0]
    normed_one = rms_scale(x, gain_full[0]).astype(bf)
    projected = dot(normed_one, qkv_w).astype(bf)
    query = projected[:, :width]
    keyval = place(
        gather(projected[:, width:], t_steps), t, t_steps, "tensor", axis=1
    ).reshape(slot, tn * kvt)
    mixed, logsum = slot_forward(query, keyval, length)
    mixed = mixed.astype(bf)
    attn_part = dot(mixed, output_w).astype(bf).reshape(tn, quarter, model)
    attn = reduce(pick(attn_part, t, t_steps, "tensor"), t_steps)
    x_own = lax.dynamic_slice_in_dim(x, t * quarter, quarter, 0)
    resid = x_own + attn
    normed_two_own = rms_scale(resid, gain_full[1]).astype(bf)

    group = ZN * tn * quarter
    normed_two = gather(normed_two_own, group_steps).reshape(group, model)
    cot_own = lax.dynamic_slice_in_dim(cotangent, t * quarter, quarter, 0)
    valid = (t * quarter + jnp.arange(quarter) < length)[:, None]
    grad_own = jnp.where(valid, cot_own, jnp.zeros_like(cot_own))
    grad_low = gather(grad_own, group_steps).reshape(group, model)

    gate = dot(normed_two, gateup_w[0])
    upper = dot(normed_two, gateup_w[1])
    hidden = (jax.nn.gelu(gate, approximate=True) * upper).astype(bf)
    ff_part = dot(hidden, down_w).astype(bf).reshape(ZN * tn, quarter, model)
    out_own = resid + reduce(ff_part, group_steps)
    block_output = place(gather(out_own, t_steps), t, t_steps, "tensor").reshape(slot, model)

    grad_hidden = times_trans(grad_low, down_w)
    _, pull_gelu = jax.vjp(
        lambda left, right: jax.nn.gelu(left, approximate=True) * right, gate, upper
    )
    grad_gate, grad_up = pull_gelu(grad_hidden)
    grad_gate = grad_gate.astype(bf)
    grad_up = grad_up.astype(bf)
    grad_normed = (times_trans(grad_gate, gateup_w[0]) + times_trans(grad_up, gateup_w[1])).astype(bf)
    grad_normed_two = reduce(grad_normed.reshape(ZN * tn, quarter, model), group_steps)

    def columns(array, j):
        return take(array.reshape(group, ZN, rn, rows), r ^ j, 2).reshape(group, ZN * rows)

    def scatter_z(sums, axis):
        parts = []
        for k in range(ZN):
            block = take(sums, z ^ k, 0).astype(bf)
            parts.append(swap(block, zpos(k)) if k else block)
        shape = parts[0].shape
        out = jnp.zeros(shape[:axis] + (ZN,) + shape[axis:], bf)
        for k in range(ZN):
            out = lax.dynamic_update_index_in_dim(out, parts[k], z ^ k, axis)
        return out

    r_offsets = [offset(p, r_steps, "dp") for p in range(rn)]
    down_parts = jnp.stack(
        [
            inner_rows(hidden, columns(grad_low, j)).astype(bf).reshape(ff, ZN, rows)
            for j in r_offsets
        ]
    )
    down_sum = reduce(down_parts, r_steps)
    down_shard = scatter_z(jnp.moveaxis(down_sum, 1, 0), 0).reshape(ZN * ff, rows).astype(fl)

    shards_gu = []
    for grad in (grad_gate, grad_up):
        parts = jnp.stack(
            [
                inner_rows(columns(normed_two, j), grad).astype(bf).reshape(ZN, rows, ff)
                for j in r_offsets
            ]
        )
        sums = reduce(parts, r_steps)
        shards_gu.append(scatter_z(sums, 1).reshape(rows, ZN * ff).astype(fl))
    gateup_shard = jnp.stack(shards_gu)

    _, pull_second = jax.vjp(rms_scale, resid, gain_full[1])
    grad_resid_norm, grad_gain_two = pull_second(grad_normed_two)
    grad_resid = grad_own.astype(fl) + grad_resid_norm
    grad_attn = place(gather(grad_resid.astype(bf), t_steps), t, t_steps, "tensor").reshape(slot, model)

    output_grad = inner_rows(mixed, grad_attn).astype(bf)
    grad_mixed = times_trans(grad_attn, output_w).astype(bf)
    grad_query, grad_keyval = slot_backward(query, keyval, length, logsum, grad_mixed)
    keyval_parts = grad_keyval.astype(bf).reshape(slot, tn, kvt)
    keyval_low = reduce(pick(keyval_parts, t, t_steps, "tensor", axis=1), t_steps).astype(bf)
    grad_projected = jnp.concatenate([grad_query.astype(bf), keyval_low], axis=1)
    one_parts = times_trans(grad_projected, qkv_w).astype(bf).reshape(tn, quarter, model)
    grad_normed_one = reduce(pick(one_parts, t, t_steps, "tensor"), t_steps)
    qkv_grad = inner_rows(normed_one, grad_projected).astype(bf)
    _, pull_first = jax.vjp(rms_scale, x_own, gain_full[0])
    grad_x_norm, grad_gain_one = pull_first(grad_normed_one)
    input_own = grad_resid + grad_x_norm
    input_grad = place(gather(input_own, t_steps), t, t_steps, "tensor").reshape(slot, model)

    qkv_shard = reduce(
        pick(qkv_grad.reshape(dp, rows, width + kvt), me, dp_steps, "dp"), dp_steps
    )
    query_shard = qkv_shard[:, :width]
    keyval_shard = place(
        gather(qkv_shard[:, width:].astype(bf), t_steps), t, t_steps, "tensor", axis=1
    ).reshape(rows, tn * kvt).astype(fl)
    output_shard = reduce(
        pick(output_grad.reshape(width, dp, rows), me, dp_steps, "dp", axis=1), dp_steps
    )
    gains_grad = jnp.stack([grad_gain_one, grad_gain_two]).reshape(2, dp, rows)
    gains_parts = pick(gains_grad, me, dp_steps, "dp", axis=1)
    for step in reversed(dp_steps):
        half = gains_parts.shape[0] // 2
        gains_parts = gains_parts[:half] + swap(gains_parts[half:], step)
    gains_shard = gains_parts[0]
    for step in t_steps:
        gains_shard = gains_shard + swap(gains_shard, step)

    qa = adamw(w_query, query_shard, first_query, second_query, decay_rate)
    ka = adamw(w_keyval, keyval_shard, first_keyval, second_keyval, decay_rate)
    oa = adamw(w_output, output_shard, first_output, second_output, decay_rate)
    ga = adamw(w_gateup, gateup_shard, first_gateup, second_gateup, decay_rate)
    da = adamw(w_down, down_shard, first_down, second_down, decay_rate)
    na = adamw(norm_gains, gains_shard, first_gains, second_gains, 0.0)
    return (block_output, input_grad, *qa, *ka, *oa, *ga, *da, *na)


MESH = pl.DeviceIdType.MESH
ANY = pl.BlockSpec(memory_space=pl.ANY)
VMEM = pl.BlockSpec(memory_space=pltpu.VMEM)
LIMIT = 127 * 512 * 1024
WINDOW = 1
PIECES = 1


def position():
    me = lax.axis_index("dp")
    t = lax.axis_index("tensor")
    return me // 2, me % 2, t


def at_z(z, r, t, k):
    return ((z ^ k) * 2 + r, t)


def greet(partners):
    barrier = pltpu.get_barrier_semaphore()
    for device in partners:
        pl.semaphore_signal(barrier, inc=1, device_id=device, device_id_type=MESH)
    pl.semaphore_wait(barrier, len(partners))


class Copies:
    def __init__(self, send, recv):
        self.send, self.recv, self.made, self.gone = send, recv, {}, set()

    def start(self, name, src, dst, device, sent=None, got=None):
        i = len(self.made)
        make = lambda: pltpu.make_async_remote_copy(
            src_ref=src() if callable(src) else src,
            dst_ref=dst() if callable(dst) else dst,
            send_sem=self.send.at[i],
            recv_sem=self.recv.at[i],
            device_id=device,
            device_id_type=MESH,
        )
        self.made[name] = (make, sent, got)
        maybe(sent, lambda: make().start())

    def arrived(self, name):
        make, _, got = self.made[name]
        maybe(got, lambda: make().wait_recv())

    def left(self, name):
        if name not in self.gone:
            self.gone.add(name)
            make, sent, _ = self.made[name]
            maybe(sent, lambda: make().wait_send())

    def all_left(self, keep=lambda name: True):
        for name in self.made:
            if keep(name):
                self.left(name)


def maybe(condition, action):
    if condition is None:
        action()
    else:
        pl.when(condition)(action)


class Line:
    def __init__(self):
        self.z, self.r, self.t = position()

    def block(self, way, s):
        return lax.max(lax.min(self.z - way * s, 3), 0)

    def device(self, way):
        return (lax.max(lax.min(self.z + way, 3), 0) * 2 + self.r, self.t)

    def sent(self, way, s):
        if way > 0:
            return (self.z < 3) & (self.z >= s)
        return (self.z > 0) & (self.z + s <= 3)

    def got(self, way, s):
        return self.z >= 1 + s if way > 0 else self.z + 1 + s <= 3


WAYS = ((1, "u"), (-1, "d"))


def remote_params(number, limit=LIMIT):
    return pltpu.CompilerParams(
        collective_id=number, has_side_effects=True, vmem_limit_bytes=limit
    )


def block_rows(z, t, quarter):
    return pl.ds(pl.multiple_of((z * 4 + t) * quarter, quarter), quarter)


class TokenGather:
    count = 27

    def __init__(self, copies, own, out, tag):
        self.copies, self.own, self.out, self.tag = copies, own, out, tag
        self.line = Line()
        self.z, self.r, self.t = position()
        self.quarter = own.shape[0]

    def rows(self, b, j):
        return self.out.at[block_rows(b, self.t ^ j, self.quarter)]

    def send_z(self, s):
        for way, mark in WAYS:
            b = self.line.block(way, s)
            self.copies.start(
                f"{self.tag}z{mark}{s}",
                self.own if s == 0 else self.rows(b, 0),
                self.rows(b, 0),
                self.line.device(way),
                self.line.sent(way, s),
                self.line.got(way, s),
            )

    def over(self, name, src, b, j, step, got):
        self.copies.start(
            self.tag + name, src, self.rows(b, j), (self.z * 2 + self.r, self.t ^ step), got, got
        )

    def send_own(self):
        self.over("xo", self.own, self.z, 0, 2, None)
        self.over("co0", self.own, self.z, 0, 1, None)

    def take_z(self, s):
        for way, mark in WAYS:
            self.copies.arrived(f"{self.tag}z{mark}{s}")
        if s < 2:
            self.send_z(s + 1)
        for way, mark in WAYS:
            b, got = self.line.block(way, s + 1), self.line.got(way, s)
            self.over(f"x{mark}{s}", self.rows(b, 0), b, 0, 2, got)
            self.over(f"c{mark}{s}0", self.rows(b, 0), b, 0, 1, got)

    def take_own(self):
        self.copies.arrived(f"{self.tag}xo")
        self.over("co1", self.rows(self.z, 2), self.z, 2, 1, None)

    def take_x(self, s):
        for way, mark in WAYS:
            self.copies.arrived(f"{self.tag}x{mark}{s}")
            b = self.line.block(way, s + 1)
            self.over(f"c{mark}{s}1", self.rows(b, 2), b, 2, 1, self.line.got(way, s))

    def finish(self):
        for name in list(self.copies.made):
            if name.startswith(self.tag + "c"):
                self.copies.arrived(name)
        self.copies.all_left(lambda name: name.startswith(self.tag))


def partners_of(z, r, t, zs=(1, 2, 3), y=True, tensor=True):
    out = [at_z(z, r, t, k) for k in zs]
    if y:
        out.append((z * 2 + (r ^ 1), t))
    if tensor:
        out += [(z * 2 + r, t ^ 2), (z * 2 + r, t ^ 1)]
    return out


def rms_into(src, gain, dst, slab=16):
    @pl.loop(0, dst.shape[0] // slab)
    def _(i):
        rows = pl.ds(pl.multiple_of(i * slab, slab), slab)
        v = src[rows].astype(fl)
        inverse = lax.rsqrt(jnp.mean(v * v, axis=-1, keepdims=True) + norm_eps)
        dst[rows] = (v * inverse * gain).astype(bf)


def cast_into(src, dst, slab=16):
    @pl.loop(0, src.shape[0] // slab)
    def _(i):
        rows = pl.ds(pl.multiple_of(i * slab, slab), slab)
        dst[rows] = src[rows].astype(bf)


def probabilities(q, key, length, first):
    scores = times_trans(q, key) * HD ** (-0.5)
    row = first + lax.broadcasted_iota(jnp.int32, scores.shape, 0)
    col = lax.broadcasted_iota(jnp.int32, scores.shape, 1)
    scores = jnp.where((col <= row) & (col < length), scores, masked_score)
    expo = jnp.exp(scores - jnp.max(scores, axis=-1, keepdims=True))
    return expo / jnp.sum(expo, axis=-1, keepdims=True)


def forward_kernel(
    lengths, wq, wkv, wo, wgu, wd, gains, tokens, cotangent,
    gu_out, d_out, dy_out, nt_out, resid_out, one_out, q_out, kv_out, mixed_out, qkv_out, o_out, gain_out,
    wq_f, wkv_f, wo_f, gu_f, d_f, gu_b, d_b, x, qkv, o, gain, one, q, kv, mixed,
    part, recvc, sendx, recvx, resid, nt_own, dy,
    send, recv, load, store,
):
    z, r, t = position()
    me = z * 2 + r
    rows = wq.shape[0]
    slot, model = tokens.shape
    quarter = slot // 4
    width = wq.shape[1]
    kvt = qkv.shape[1] - width
    ff = d_out.shape[0]
    other = (z * 2 + (r ^ 1), t)
    x_peer, core_peer, far_peer = (me, t ^ 2), (me, t ^ 1), (me, t ^ 3)

    def d_block(k):
        return pl.ds(pl.multiple_of(((z ^ k) * 2 + r) * rows, rows), rows)

    def f_block(k):
        return pl.ds(pl.multiple_of((z ^ k) * ff, ff), ff)

    kv_cols = pl.ds(pl.multiple_of(t * kvt, kvt), kvt)
    loads = [
        pltpu.make_async_copy(wq, wq_f, load.at[0]),
        pltpu.make_async_copy(wkv.at[:, kv_cols], wkv_f, load.at[1]),
        pltpu.make_async_copy(wo, wo_f, load.at[2]),
        pltpu.make_async_copy(gains, gain.at[:, d_block(0)], load.at[3]),
        pltpu.make_async_copy(
            cotangent.at[pl.ds(pl.multiple_of(t * quarter, quarter), quarter)], dy, load.at[7]
        ),
        pltpu.make_async_copy(tokens, x, load.at[4]),
        pltpu.make_async_copy(wgu, gu_f, load.at[5]),
        pltpu.make_async_copy(wd, d_f, load.at[6]),
    ]
    for copy in loads:
        copy.start()
    stores = []

    def keep(src, dst):
        copy = pltpu.make_async_copy(src, dst, store.at[len(stores)])
        copy.start()
        stores.append(copy)

    for copy in loads[:5]:
        copy.wait()
    length = lengths[0]

    @pl.loop(0, quarter // 16)
    def _(i):
        at = pl.ds(pl.multiple_of(i * 16, 16), 16)
        row = t * quarter + i * 16 + lax.broadcasted_iota(jnp.int32, (16, model), 0)
        dy[at] = jnp.where(row < length, dy[at].astype(fl), 0.0).astype(bf)

    keep(dy, dy_out.at[block_rows(z, t, quarter)])

    @pl.loop(0, rows // 16)
    def _(i):
        own = pl.ds(pl.multiple_of(me * rows + i * 16, 16), 16)
        at = pl.ds(pl.multiple_of(i * 16, 16), 16)
        qkv[own, pl.ds(0, width)] = wq_f[at].astype(bf)
        qkv[own, pl.ds(width, kvt)] = wkv_f[at].astype(bf)

    @pl.loop(0, width // 16)
    def _(i):
        at = pl.ds(pl.multiple_of(i * 16, 16), 16)
        o[at, d_block(0)] = wo_f[at].astype(bf)

    greet(partners_of(z, r, t, zs=(1, 2, 3)) + [far_peer] + [((z ^ k) * 2 + (r ^ 1), t) for k in (1, 2, 3)])
    copies = Copies(send, recv)
    d = TokenGather(copies, dy, dy_out, "d")

    for k in range(4):
        for j in range(2):
            if k or j:
                copies.start(
                    f"g{k}{j}", gain.at[:, d_block(0)], gain.at[:, d_block(0)], ((z ^ k) * 2 + (r ^ j), t)
                )

    line = Line()

    def pack_send(tag, name, b, device, sent=None, got=None):
        at = pl.ds(pl.multiple_of((b * 2 + r) * rows, rows), rows)
        ref = qkv.at[at] if tag == "q" else o.at[:, at]
        copies.start(tag + name, ref, ref, device, sent, got)

    def pack_step(tag, s):
        for way, mark in WAYS:
            sent, got = line.sent(way, s), line.got(way, s)
            pack_send(tag, f"z{mark}{s}", line.block(way, s), line.device(way), sent, got)

    def pack_take(tag, s):
        for way, mark in WAYS:
            copies.arrived(f"{tag}z{mark}{s}")
        if s < 2:
            pack_step(tag, s + 1)
        for way, mark in WAYS:
            got = line.got(way, s)
            pack_send(tag, f"y{mark}{s}", line.block(way, s + 1), other, got, got)

    def pack_wait(tag):
        for name in ["o"] + [mark + str(s) for s in range(3) for _, mark in WAYS]:
            copies.arrived(tag + "y" + name)

    pack_step("q", 0)
    pack_send("q", "yo", z, other)
    d.send_own()

    for copy in loads[5:]:
        copy.wait()
    for m in range(2):
        cast_into(gu_f.at[m], gu_b.at[m])
    cast_into(d_f, d_b, 64)

    pieces = PIECES

    def owned(m, k, p):
        if m == 2:
            n = ff // pieces
            return d_b.at[pl.ds(pl.multiple_of((z ^ k) * ff + p * n, n), n)]
        n = rows // pieces
        return gu_b.at[m, p * n : (p + 1) * n, f_block(k)]

    def landed(m, k, p):
        if m == 2:
            n = ff // pieces
            return d_out.at[p * n : (p + 1) * n, d_block(k)]
        n = rows // pieces
        return gu_out.at[m, pl.ds(pl.multiple_of(((z ^ k) * 2 + r) * rows + p * n, n), n)]

    flows = [(m, k, p) for m in range(3) for k in (1, 3, 2) for p in range(pieces)]
    counts = [0, 0]

    def issue():
        if counts[0] < len(flows):
            m, k, p = flows[counts[0]]
            copies.start(f"wz{k}{m}{p}", owned(m, k, p), landed(m, 0, p), at_z(z, r, t, k))
            counts[0] += 1

    def forward(m, k, p):
        copies.start(f"wy{k}{m}{p}", owned(m, 0, p) if k == 0 else landed(m, k, p), landed(m, k, p), other)

    def pump(n, more=True):
        for _ in range(n):
            if counts[1] < counts[0]:
                m, k, p = flows[counts[1]]
                copies.arrived(f"wz{k}{m}{p}")
                forward(m, k, p)
                counts[1] += 1
            if more:
                issue()

    for _ in range(WINDOW):
        issue()
    for m in range(3):
        for p in range(pieces):
            keep(owned(m, 0, p), landed(m, 0, p))

    for k in range(4):
        for j in range(2):
            if k or j:
                copies.arrived(f"g{k}{j}")
    keep(gain, gain_out)
    rms_into(x, gain[0:1, :], one)
    keep(one, one_out)

    pack_take("q", 0)
    pack_take("q", 1)
    d.send_z(0)
    pack_step("o", 0)
    for _ in range(WINDOW):
        issue()
    pack_take("q", 2)
    pack_send("o", "yo", z, other)
    pack_wait("q")
    for p in range(pieces):
        forward(0, 0, p)
    keep(qkv, qkv_out)

    kv[:, kv_cols] = dot(one[...], qkv[:, width:]).astype(bf)
    for name, peer in (("k1", core_peer), ("k2", x_peer), ("k3", far_peer)):
        copies.start(name, kv.at[:, kv_cols], kv.at[:, kv_cols], peer)
    q[...] = dot(one[...], qkv[:, :width]).astype(bf)
    keep(q, q_out)
    pack_take("o", 0)
    for name in ("k1", "k2", "k3"):
        copies.arrived(name)
    keep(kv, kv_out)
    for p in range(pieces):
        forward(1, 0, p)
    step = 128
    for h in range(width // HD):
        for i in range(slot // step):
            at, upto = pl.ds(i * step, step), pl.ds(0, (i + 1) * step)
            probs = probabilities(q[at, h * HD : (h + 1) * HD], kv[upto, :HD], length, i * step)
            mixed[at, h * HD : (h + 1) * HD] = dot(probs.astype(bf), kv[upto, HD:]).astype(bf)
        if h == 0:
            pack_take("o", 1)
            pump(1)
    keep(mixed, mixed_out)
    pack_take("o", 2)
    pump(1)
    pack_wait("o")
    keep(o, o_out)
    for p in range(pieces):
        forward(2, 0, p)
    d.take_z(0)
    d.take_own()

    def part_of(j, store_part):
        at = pl.ds(pl.multiple_of((t ^ j) * quarter, quarter), quarter)
        for n in range(0, model, 512):
            store_part(dot(mixed[at], o[:, n : n + 512]), slice(n, n + 512))

    def into_part(i):
        def put(value, cols):
            part[i, :, cols] = value.astype(bf)

        return put

    part_of(3, into_part(0))
    part_of(1, into_part(1))
    copies.start("a1", part, recvc, core_peer)
    pump(1)
    copies.arrived("a1")

    def into_x(value, cols):
        sendx[:, cols] = (value + recvc[0, :, cols].astype(fl)).astype(bf)

    part_of(2, into_x)
    copies.start("a2", sendx, recvx, x_peer)

    def into_resid(value, cols):
        resid[:, cols] = value + recvc[1, :, cols].astype(fl)

    part_of(0, into_resid)
    d.take_z(1)
    d.take_x(0)
    copies.arrived("a2")
    first_row = t * quarter

    @pl.loop(0, quarter // 16)
    def _(i):
        at = pl.ds(pl.multiple_of(i * 16, 16), 16)
        mine = pl.ds(pl.multiple_of(first_row + i * 16, 16), 16)
        v = x[mine].astype(fl) + (resid[at] + recvx[at].astype(fl))
        resid[at] = v
        inverse = lax.rsqrt(jnp.mean(v * v, axis=-1, keepdims=True) + norm_eps)
        nt_own[at] = (v * inverse * gain[1:2, :]).astype(bf)

    keep(resid, resid_out)
    keep(nt_own, nt_out.at[block_rows(z, t, quarter)])
    n = TokenGather(copies, nt_own, nt_out, "n")
    n.send_z(0)
    n.send_own()
    pump(2)
    d.take_z(2)
    d.take_x(1)
    n.take_z(0)
    n.take_own()
    pump(2)
    d.take_x(2)
    n.take_z(1)
    n.take_x(0)
    pump(2)
    n.take_z(2)
    n.take_x(1)
    pump(2)
    n.take_x(2)
    pump(len(flows))
    n.finish()
    d.finish()
    for k in range(4):
        for m in range(3):
            for p in range(pieces):
                copies.arrived(f"wy{k}{m}{p}")
    copies.all_left(lambda name: name[0] not in "nd")
    for copy in stores:
        copy.wait()


def forward_part(lengths, wq, wkv, wo, wgu, wd, gains, tokens, cotangent):
    rows, width = wq.shape
    slot, model = tokens.shape
    quarter = slot // 4
    kvt = wkv.shape[1] // 4
    ff = wd.shape[0] // ZN
    n = 7 + 26 + 21 * PIECES + 3 + 2 + 2 * TokenGather.count
    shape = jax.ShapeDtypeStruct
    return pl.pallas_call(
        forward_kernel,
        out_shape=(
            shape((2, model, ff), bf),
            shape((ff, model), bf),
            shape((16 * quarter, model), bf),
            shape((16 * quarter, model), bf),
            shape((quarter, model), fl),
            shape((slot, model), bf),
            shape((slot, width), bf),
            shape((slot, 4 * kvt), bf),
            shape((slot, width), bf),
            shape((model, width + kvt), bf),
            shape((width, model), bf),
            shape((8, model), fl),
        ),
        in_specs=[pl.BlockSpec(memory_space=pltpu.SMEM)] + [ANY] * 8,
        out_specs=(ANY,) * 12,
        scratch_shapes=[
            pltpu.VMEM((rows, width), fl),
            pltpu.VMEM((rows, kvt), fl),
            pltpu.VMEM((width, rows), fl),
            pltpu.VMEM(wgu.shape, fl),
            pltpu.VMEM(wd.shape, fl),
            pltpu.VMEM(wgu.shape, bf),
            pltpu.VMEM(wd.shape, bf),
            pltpu.VMEM((slot, model), bf),
            pltpu.VMEM((model, width + kvt), bf),
            pltpu.VMEM((width, model), bf),
            pltpu.VMEM((8, model), fl),
            pltpu.VMEM((slot, model), bf),
            pltpu.VMEM((slot, width), bf),
            pltpu.VMEM((slot, 4 * kvt), bf),
            pltpu.VMEM((slot, width), bf),
            pltpu.VMEM((2, quarter, model), bf),
            pltpu.VMEM((2, quarter, model), bf),
            pltpu.VMEM((quarter, model), bf),
            pltpu.VMEM((quarter, model), bf),
            pltpu.VMEM((quarter, model), fl),
            pltpu.VMEM((quarter, model), bf),
            pltpu.VMEM((quarter, model), bf),
            pltpu.SemaphoreType.DMA((n,)),
            pltpu.SemaphoreType.DMA((n,)),
            pltpu.SemaphoreType.DMA((8,)),
            pltpu.SemaphoreType.DMA((10 + 3 * PIECES,)),
        ],
        compiler_params=remote_params(1),
        name="forward_part",
    )(lengths, wq, wkv, wo, wgu, wd, gains, tokens, cotangent)


ROOT = 0.7978845608028654
CUBE = 0.044715


def z_order(z):
    end = 1 - lax.min(lax.rem(z, 3), 1)
    return (3 - 2 * end, 2 + end, 1 + end, 0)


def block_grads(h, lhs, to_gu, to_d):
    for m, (which, n) in enumerate(((1, 0), (2, 0), (0, 1))):

        @pl.loop(0, h.shape[2] // 512)
        def _(c):
            cols = pl.ds(pl.multiple_of(c * 512, 512), 512)
            grad = inner_rows(lhs[n], h[which, :, cols])
            if m < 2:
                to_gu[m, :, cols] = grad.astype(bf)
            else:
                to_d[cols, :] = grad.T.astype(bf)


def add_to(mine, theirs):
    @pl.loop(0, mine.shape[0] // 64)
    def _(n):
        at = pl.ds(pl.multiple_of(n * 64, 64), 64)
        mine[at] = (mine[at].astype(fl) + theirs[at].astype(fl)).astype(bf)


def ff_kernel(
    nt_hbm, dy_hbm, gu_hbm, d_hbm, hgu_hbm, sums, first_gu, first_d,
    sendc, recvc, sendx, kept, recvx, recvz, recvy_gu, recvy_d,
    send, recv, zsend, zrecv, load, wload, store,
):
    z, r, t = position()
    x, c = t // 2, t % 2
    me = z * 2 + r
    quarter = sums.shape[1]
    other, x_peer, core_peer = (z * 2 + (r ^ 1), t), (me, t ^ 2), (me, t ^ 1)
    drows = recvy_d.shape[1]
    ff, model = d_hbm.shape
    tile = 256
    wide = 1024

    order = (3 * (1 - z // 2), (2 + 3 * z) % 5, 1 + z % 2, z)

    def rows(i, b):
        cc = c if i % 2 else c ^ 1
        xx = x if b else x ^ 1
        return block_rows(order[i // 2], xx * 2 + cc, quarter)

    greet(partners_of(z, r, t, zs=(1, 2)))
    copies = Copies(send, recv)

    middle = lax.min(lax.rem(z, 3), 1)

    def add_x(s, a, places):
        for place in places:
            pltpu.make_async_copy(recvz.at[place, a], recvz.at[place, a], zrecv.at[place, a]).wait()

        @pl.loop(0, model // tile)
        def _(n):
            cols = pl.ds(pl.multiple_of(n * tile, tile), tile)
            total = kept[s, a, :, cols].astype(fl) + recvx[s, a, :, cols].astype(fl)
            for place in places:
                total += recvz[place, a, :, cols].astype(fl)
            if s == 3:
                sums[a, :, cols] = total
            else:
                recvx[s, a, :, cols] = total.astype(bf)

    def z_copy(s, a):
        up = (order[s] + 4 - z) // 5
        there = z + 2 * up - 1
        same = 1 - lax.min((order[s] - there) * (order[s] - there), 1)
        place = order[s] + (1 - up) * same * (4 - order[s])
        return pltpu.make_async_remote_copy(
            src_ref=recvx.at[s, a],
            dst_ref=recvz.at[place, a],
            send_sem=zsend.at[s, a],
            recv_sem=zrecv.at[place, a],
            device_id=(there * 2 + r, t),
            device_id_type=MESH,
        )

    def take_x(s, a, mid):
        copies.arrived(f"x{s}{a}")
        if s == 3:
            low = lax.min(z, 1)
            add_x(s, a, (z, 4) if mid else (low * z + (1 - low) * 4,))
        else:
            add_x(s, a, (order[s],) if mid else ())
            z_copy(s, a).start()

    def take(at_ends, at_middle):
        for mid, parts in enumerate((at_ends, at_middle)):
            if parts:

                @pl.when(middle == mid)
                def _():
                    for s, a in parts:
                        take_x(s, a, bool(mid))

    rest = [(s, a) for s in range(4) for a in range(2)]
    takes = {
        3: (rest[:1], ()),
        4: (rest[1:2], ()),
        5: (rest[2:3], rest[:1]),
        6: (rest[3:4], rest[1:2]),
    }
    def layers(wgu, wd, dots, xin, hgu):
        loads = [pltpu.make_async_copy(gu_hbm.at[m], wgu.at[m], wload.at[m]) for m in range(2)]
        loads.append(pltpu.make_async_copy(d_hbm, wd, wload.at[2]))
        for copy in loads:
            copy.start()


        def fetch(i):
            out = []
            for a, src in enumerate((nt_hbm, dy_hbm)):
                for b in range(2):
                    copy = pltpu.make_async_copy(
                        src.at[rows(i, b)],
                        xin.at[i % 2, a, pl.ds(b * quarter, quarter)],
                        load.at[i % 2, a, b],
                    )
                    copy.start()
                    out.append(copy)
            return out

        pending = fetch(0)


        stores = {}
        for i in range(8):
            s, own = i // 2, i % 2
            for copy in pending:
                copy.wait()
            if i < 7:
                pending = fetch(i + 1)
            if i >= 2:
                for copy in stores[i - 2]:
                    copy.wait()

            if i == 0:
                loads[0].wait()
            dots[0] = dot(xin[i % 2, 0], wgu[0])
            if i == 0:
                loads[1].wait()
            dots[1] = dot(xin[i % 2, 0], wgu[1])
            if i == 0:
                loads[2].wait()
            dots[2] = times_trans(xin[i % 2, 1], wd[...])

            @pl.loop(0, 2 * quarter // 16)
            def _(n):
                at = pl.ds(pl.multiple_of(n * 16, 16), 16)
                for half in range(0, ff, 512):
                    cols = slice(half, half + 512)
                    gate, upper, dh = dots[0, at, cols], dots[1, at, cols], dots[2, at, cols]
                    square = gate * gate
                    bend = jnp.tanh(ROOT * gate * (1.0 + CUBE * square))
                    share = 0.5 * (1.0 + bend)
                    gelu = gate * share
                    slope = share + 0.5 * gate * (1.0 - bend * bend) * (ROOT * (1.0 + 3.0 * CUBE * square))
                    hgu[i % 2, 0, at, cols] = (gelu * upper).astype(bf)
                    hgu[i % 2, 1, at, cols] = (dh * upper * slope).astype(bf)
                    hgu[i % 2, 2, at, cols] = (dh * gelu).astype(bf)

            stores[i] = []
            for m in range(3):
                for b in range(2):
                    copy = pltpu.make_async_copy(
                        hgu.at[i % 2, m, pl.ds(b * quarter, quarter)],
                        hgu_hbm.at[m, rows(i, b)],
                        store.at[i % 2, m, b],
                    )
                    copy.start()
                    stores[i].append(copy)

            if own:
                copies.arrived(f"c{s}")
                if s >= 2:
                    for a in range(2):
                        copies.left(f"x{s - 2}{a}")
            elif s >= 1:
                copies.left(f"c{s - 1}")

            @pl.loop(0, model // wide)
            def _(n):
                cols = pl.ds(pl.multiple_of(n * wide, wide), wide)
                out = dot(hgu[i % 2, 0], wd[:, cols])
                back = times_trans(hgu[i % 2, 1], wgu[0, cols]) + times_trans(hgu[i % 2, 2], wgu[1, cols])
                for a, part in enumerate((out, back)):
                    if own:
                        total = part + recvc[s % 2, a, :, cols].astype(fl)
                        sendx[s % 2, a, :, cols] = total[:quarter].astype(bf)
                        kept[s, a, :, cols] = total[quarter:].astype(bf)
                    else:
                        sendc[a, :, cols] = part.astype(bf)

            if own:
                for a in range(2):
                    copies.start(
                        f"x{s}{a}",
                        lambda s=s, a=a: sendx.at[s % 2, a],
                        lambda s=s, a=a: recvx.at[s, a],
                        x_peer,
                    )
            else:
                copies.start(f"c{s}", lambda: sendc, lambda s=s: recvc.at[s % 2], core_peer)
            if i in takes:
                take(*takes[i])

        for i in (6, 7):
            for copy in stores[i]:
                copy.wait()

    pl.run_scoped(
        layers,
        pltpu.VMEM((2, model, ff), bf),
        pltpu.VMEM((ff, model), bf),
        pltpu.VMEM((3, 2 * quarter, ff), fl),
        pltpu.VMEM((2, 2, 2 * quarter, model), bf),
        pltpu.VMEM((2, 3, 2 * quarter, ff), bf),
    )

    first = z_order(z)[0]

    def first_grads(h, lhs, to_gu, to_d, own_gu, own_d):
        loads = [pltpu.make_async_copy(hgu_hbm.at[m], h.at[m], wload.at[m]) for m in range(3)]

        def fetch(j):
            block = pl.multiple_of(((z ^ first) * 2 + (r ^ j)) * drows, drows)
            made = []
            for n, src in enumerate((nt_hbm, dy_hbm)):
                copy = pltpu.make_async_copy(src.at[:, pl.ds(block, drows)], lhs.at[n], load.at[0, 0, n])
                copy.start()
                made.append(copy)
            return made

        pending = fetch(1)
        for m in (1, 2, 0):
            loads[m].start()
        take(rest[4:5], rest[2:4])
        for m in (1, 2, 0):
            loads[m].wait()
        for copy in pending:
            copy.wait()
        block_grads(h, lhs, to_gu, to_d)
        for m in range(2):
            copies.start(f"y{m}", lambda m=m: to_gu.at[m], lambda m=m: recvy_gu.at[m], other)
        copies.start("y2", lambda: to_d, lambda: recvy_d, other)
        pending = fetch(0)
        take(rest[5:6], rest[4:6])
        for copy in pending:
            copy.wait()
        block_grads(h, lhs, own_gu, own_d)
        take(rest[6:], rest[6:])
        for m in range(3):
            copies.arrived(f"y{m}")
            mine, theirs = (own_d, recvy_d) if m == 2 else (own_gu.at[m], recvy_gu.at[m])
            add_to(mine, theirs)
            copy = pltpu.make_async_copy(mine, first_d if m == 2 else first_gu.at[m], wload.at[m])
            copy.start()
        for m in range(3):
            mine = own_d if m == 2 else own_gu.at[m]
            pltpu.make_async_copy(mine, first_d if m == 2 else first_gu.at[m], wload.at[m]).wait()
            copies.left(f"y{m}")

    group = nt_hbm.shape[0]
    pl.run_scoped(
        first_grads,
        pltpu.VMEM((3, group, ff), bf),
        pltpu.VMEM((2, group, drows), bf),
        pltpu.VMEM((2, drows, ff), bf),
        pltpu.VMEM((ff, drows), bf),
        pltpu.VMEM((2, drows, ff), bf),
        pltpu.VMEM((ff, drows), bf),
    )
    for s in range(3):
        for a in range(2):
            z_copy(s, a).wait_send()
    copies.all_left()


def feed_forward(nt, dy, wgu, wd):
    group, model = nt.shape
    ff = wd.shape[0]
    quarter = group // 16
    rows = model // 8
    return pl.pallas_call(
        ff_kernel,
        out_shape=(
            jax.ShapeDtypeStruct((3, group, ff), bf),
            jax.ShapeDtypeStruct((2, quarter, model), fl),
            jax.ShapeDtypeStruct((2, rows, ff), bf),
            jax.ShapeDtypeStruct((ff, rows), bf),
        ),
        in_specs=[ANY] * 4,
        out_specs=(ANY, VMEM, ANY, ANY),
        scratch_shapes=[
            pltpu.VMEM((2, 2 * quarter, model), bf),
            pltpu.VMEM((2, 2, 2 * quarter, model), bf),
            pltpu.VMEM((2, 2, quarter, model), bf),
            pltpu.VMEM((4, 2, quarter, model), bf),
            pltpu.VMEM((4, 2, quarter, model), bf),
            pltpu.VMEM((5, 2, quarter, model), bf),
            pltpu.VMEM((2, rows, ff), bf),
            pltpu.VMEM((ff, rows), bf),
            pltpu.SemaphoreType.DMA((15,)),
            pltpu.SemaphoreType.DMA((15,)),
            pltpu.SemaphoreType.DMA((3, 2)),
            pltpu.SemaphoreType.DMA((5, 2)),
            pltpu.SemaphoreType.DMA((2, 2, 2)),
            pltpu.SemaphoreType.DMA((3,)),
            pltpu.SemaphoreType.DMA((2, 3, 2)),
        ],
        compiler_params=remote_params(3),
        name="feed_forward",
    )(nt, dy, wgu, wd)


def backward_kernel(
    lengths, nt_hbm, dy_hbm, hgu_hbm, sums, first_gu, first_d, tokens, resid, gain, one_hbm, q_hbm, kv_hbm, mixed_hbm, qkv_hbm, o_hbm,
    gu_out, d_out, qkv_grad, kv_grad, o_grad, block_out, input_out, gains_out,
    sendy_gu, sendy_d, recvy_gu, recvy_d, own_gu, own_d,
    a, dy_own, x_own, d_resid, out_own, gacc, grecv, gmine, grecv_t,
    gp, dkv_send, dkv_recv, dkv_x, dkv_rx, part, precv, sendx, recvx,
    pk_send, po_send, pk_recv, po_recv, pk_own, po_own, pk_z, po_z,
    send, recv, zsend, zrecv, load, local,
):
    z, r, t = position()
    me = z * 2 + r
    quarter, model = resid.shape
    slot = 4 * quarter
    rows = model // 8
    ff = own_d.shape[1]
    kvt = dkv_x.shape[1]
    width = gp.shape[1] - kvt
    other = (z * 2 + (r ^ 1), t)
    x_peer, core_peer, far_peer = (me, t ^ 2), (me, t ^ 1), (me, t ^ 3)

    def d_block(k, j=0):
        return pl.ds(pl.multiple_of(((z ^ k) * 2 + (r ^ j)) * rows, rows), rows)

    def own_rows(j):
        return pl.ds(pl.multiple_of((t ^ j) * quarter, quarter), quarter)

    first_loads = [
        pltpu.make_async_copy(sums.at[1], d_resid, load.at[7]),
        pltpu.make_async_copy(sums.at[0], out_own, load.at[8]),
        pltpu.make_async_copy(dy_hbm.at[block_rows(z, t, quarter)], dy_own, load.at[9]),
        pltpu.make_async_copy(tokens.at[own_rows(0)], x_own, load.at[10]),
    ]
    for copy in first_loads:
        copy.start()
    greet(partners_of(z, r, t, zs=(1, 2, 3)) + [far_peer] + [((z ^ k) * 2 + (r ^ 1), t) for k in (1, 2, 3)])
    copies = Copies(send, recv)
    locals_ = []
    counter = list(range(7))

    def keep(src, dst):
        copy = pltpu.make_async_copy(src, dst, local.at[counter.pop(0)])
        copy.start()
        locals_.append(copy)
        return copy

    def norm_back(v, grad, row):
        inverse = lax.rsqrt(jnp.mean(v * v, axis=-1, keepdims=True) + norm_eps)
        scaled = v * inverse
        gacc[row : row + 1, :] += jnp.sum(grad * scaled, axis=0, keepdims=True)
        inner = grad * gain[row : row + 1, :]
        return inverse * (inner - scaled * jnp.mean(inner * scaled, axis=-1, keepdims=True))

    gacc[...] = jnp.zeros_like(gacc)
    in_own = out_own

    zorder = z_order(z)

    def send_y(i):
        for m in range(2):
            copies.start(f"y{i}{m}", lambda m=m: sendy_gu.at[i - 1, m], lambda m=m: recvy_gu.at[i - 1, m], other)
        copies.start(f"y{i}2", lambda: sendy_d.at[i - 1], lambda: recvy_d.at[i - 1], other)

    flows = [(i, m) for i in (1, 2) for m in range(3)]
    taken = [0]

    def own_of(i, m):
        if i == 0:
            return first_d if m == 2 else first_gu.at[m]
        return own_d.at[i - 1] if m == 2 else own_gu.at[i - 1, m]

    def add_y(i, m):
        add_to(own_of(i, m), recvy_d.at[i - 1] if m == 2 else recvy_gu.at[i - 1, m])

    def place(m):
        cols = pl.ds(pl.multiple_of(z * ff, ff), ff)
        return d_out.at[cols] if m == 2 else gu_out.at[m, :, cols]

    def z_copy(i, m):
        k = zorder[i]
        return pltpu.make_async_remote_copy(
            src_ref=own_of(i, m),
            dst_ref=place(m),
            send_sem=zsend.at[i, m],
            recv_sem=zrecv.at[k - 1, m],
            device_id=at_z(z, r, t, k),
            device_id_type=MESH,
        )

    def pump(n):
        for _ in range(n):
            if taken[0] < len(flows):
                i, m = flows[taken[0]]
                copies.arrived(f"y{i}{m}")
                add_y(i, m)
                z_copy(i, m).start()
                taken[0] += 1

    def block_copy():
        return pltpu.make_async_copy(out_own, block_out.at[own_rows(0)], local.at[7])

    def second_norm():
        for copy in first_loads:
            copy.wait()

        @pl.loop(0, quarter // 16)
        def _(i):
            at = pl.ds(pl.multiple_of(i * 16, 16), 16)
            mine = pl.ds(pl.multiple_of(t * quarter + i * 16, 16), 16)
            v = resid[at]
            total = dy_own[at].astype(fl) + norm_back(v, d_resid[at], 1)
            d_resid[at] = total
            a[mine] = total.astype(bf)
            out_own[at] += v

        copies.start("ax", lambda: a.at[own_rows(0)], lambda: a.at[own_rows(0)], x_peer)
        copies.start("ac", lambda: a.at[own_rows(0)], lambda: a.at[own_rows(0)], core_peer)
        block_copy().start()
        copies.start("bx", lambda: out_own, lambda: block_out.at[own_rows(0)], x_peer)
        copies.start("bc", lambda: out_own, lambda: block_out.at[own_rows(0)], core_peer)

    def feed_forward_grads(first, last, pumps, hgu, lhs):
        loads = [pltpu.make_async_copy(hgu_hbm.at[m], hgu.at[m], load.at[m]) for m in range(3)]

        def fetch(i):
            cols = d_block(zorder[i // 2], 1 - i % 2)
            made = []
            for n, src in enumerate((nt_hbm, dy_hbm)):
                copy = pltpu.make_async_copy(src.at[:, cols], lhs.at[i % 2, n], load.at[3 + 2 * (i % 2) + n])
                copy.start()
                made.append(copy)
            return made

        pending = fetch(first)
        for m in (1, 2, 0):
            loads[m].start()
        if first == 2:
            second_norm()
        for i in range(first, last):
            for copy in pending:
                copy.wait()
            if i < last - 1:
                pending = fetch(i + 1)
            if i == first:
                for m in range(3):
                    loads[m].wait()
            to_gu, to_d = (own_gu, own_d) if i % 2 else (sendy_gu, sendy_d)
            block_grads(hgu, lhs.at[i % 2], to_gu.at[i // 2 - 1], to_d.at[i // 2 - 1])
            if i in (2, 6):
                send_y(i // 2)
            pump(pumps[i - first])

    for m in range(3):
        z_copy(0, m).start()
    group = nt_hbm.shape[0]
    scope = (pltpu.VMEM((3, group, ff), bf), pltpu.VMEM((2, 2, group, rows), bf))
    pl.run_scoped(functools.partial(feed_forward_grads, 2, 5, (0, 1, 0)), *scope)

    copies.arrived("ax")
    copies.start("af", a.at[own_rows(2)], a.at[own_rows(2)], core_peer)
    copies.arrived("bx")
    copies.start("bf", block_out.at[own_rows(2)], block_out.at[own_rows(2)], core_peer)

    pack_order = (1, 3, 2, 0)
    at_zs = [at_z(z, r, t, k) for k in range(4)]
    packs = {"p": (pk_own, pk_recv, pk_z), "o": (po_own, po_recv, po_z)}

    def add_pack(tag, i):
        own, theirs, _ = packs[tag]
        copies.arrived(f"y{tag}{i}")
        own[i] = (own[i].astype(fl) + theirs[i].astype(fl)).astype(bf)

    def send_pack(tag, i, k):
        copies.start(f"z{tag}{i}", lambda: packs[tag][0].at[i], lambda: packs[tag][2].at[i], at_zs[k])

    def pack_first(tag, i):
        add_pack(tag, i)
        send_pack(tag, i, 1)

    def pack_second(tag):
        own, _, came = packs[tag]
        add_pack(tag, 2)
        copies.arrived(f"z{tag}1")
        own[2] = (own[2].astype(fl) + came[1].astype(fl)).astype(bf)
        send_pack(tag, 2, 2)
        add_pack(tag, 3)


    def attention(q, kv, mixed, qkv, o, one, dm, dkv):
        loads = [
            pltpu.make_async_copy(src, dst, load.at[i])
            for i, (src, dst) in enumerate(
                ((o_hbm, o), (q_hbm, q), (kv_hbm, kv), (mixed_hbm, mixed), (qkv_hbm, qkv), (one_hbm, one))
            )
        ]
        for copy in loads:
            copy.start()
        copies.arrived("ac")
        copies.arrived("af")
        for copy in loads:
            copy.wait()
        for i, k in enumerate(pack_order):
            po_send[i] = inner_rows(mixed[...], a[:, d_block(k, 1)]).astype(bf)
            copies.start(f"yo{i}", lambda i=i: po_send.at[i], lambda i=i: po_recv.at[i], other)
        send_y(2)
        for i, k in enumerate(pack_order):
            po_own[i] = inner_rows(mixed[...], a[:, d_block(k, 0)]).astype(bf)
        dm[...] = times_trans(a[...], o[...]).astype(bf)
        length = lengths[0]
        step = 128
        dkv[...] = jnp.zeros_like(dkv)
        for h in range(width // HD):
            head = slice(h * HD, (h + 1) * HD)
            for i in range(slot // step):
                at, upto = pl.ds(i * step, step), pl.ds(0, (i + 1) * step)
                probs = probabilities(q[at, head], kv[upto, :HD], length, i * step)
                d_probs = times_trans(dm[at, head], kv[upto, HD:])
                d_scores = probs * (d_probs - jnp.sum(d_probs * probs, axis=-1, keepdims=True))
                d_raw = (d_scores * HD ** (-0.5)).astype(bf)
                gp[at, head] = dot(d_raw, kv[upto, :HD]).astype(bf)
                dkv[upto, :HD] += inner_rows(d_raw, q[at, head])
                dkv[upto, HD:] += inner_rows(probs.astype(bf), dm[at, head])
            pump(1)

        def kv_cols(j):
            return pl.ds(pl.multiple_of((t ^ j) * kvt, kvt), kvt)

        dkv_send[0] = dkv[:, kv_cols(1)].astype(bf)
        dkv_send[1] = dkv[:, kv_cols(3)].astype(bf)
        copies.start("kc", lambda: dkv_send, lambda: dkv_recv, core_peer)
        copies.arrived("kc")
        dkv_x[...] = (dkv[:, kv_cols(2)] + dkv_recv[1].astype(fl)).astype(bf)
        copies.start("kx", lambda: dkv_x, lambda: dkv_rx, x_peer)
        pack_first("o", 0)
        pack_first("o", 1)
        mine = dkv[:, kv_cols(0)] + dkv_recv[0].astype(fl)
        copies.arrived("kx")
        gp[:, width:] = (mine + dkv_rx[...].astype(fl)).astype(bf)

        def part_of(j, store_part):
            at = own_rows(j)
            for n in range(0, model, 512):
                store_part(times_trans(gp[at], qkv[n : n + 512]), slice(n, n + 512))

        def into_part(i):
            def put(value, cols):
                part[i, :, cols] = value.astype(bf)

            return put

        part_of(3, into_part(0))
        part_of(1, into_part(1))
        copies.start("pc", lambda: part, lambda: precv, core_peer)

        for i, k in enumerate(pack_order):
            pk_send[i] = inner_rows(one[:, d_block(k, 1)], gp[...]).astype(bf)
            copies.start(f"yp{i}", lambda i=i: pk_send.at[i], lambda i=i: pk_recv.at[i], other)

        copies.arrived("pc")

        def into_x(value, cols):
            sendx[:, cols] = (value + precv[0, :, cols].astype(fl)).astype(bf)

        part_of(2, into_x)
        copies.start("px", lambda: sendx, lambda: recvx, x_peer)

        copies.left("bx")
        copies.left("bc")
        block_copy().wait()

        def into_own(value, cols):
            in_own[:, cols] = value + precv[1, :, cols].astype(fl)

        part_of(0, into_own)
        for i, k in enumerate(pack_order):
            pk_own[i] = inner_rows(one[:, d_block(k, 0)], gp[...]).astype(bf)
        copies.arrived("px")

    pl.run_scoped(
        attention,
        pltpu.VMEM((slot, width), bf),
        pltpu.VMEM((slot, 2 * HD), bf),
        pltpu.VMEM((slot, width), bf),
        pltpu.VMEM((model, width + kvt), bf),
        pltpu.VMEM((width, model), bf),
        pltpu.VMEM((slot, model), bf),
        pltpu.VMEM((slot, width), bf),
        pltpu.VMEM((slot, 2 * HD), fl),
    )
    pl.run_scoped(functools.partial(feed_forward_grads, 5, 8, (1, 1, 1)), *scope)

    @pl.loop(0, quarter // 16)
    def _(i):
        at = pl.ds(pl.multiple_of(i * 16, 16), 16)
        grad = in_own[at] + recvx[at].astype(fl)
        in_own[at] = d_resid[at] + norm_back(x_own[at].astype(fl), grad, 0)

    keep(in_own, input_out.at[own_rows(0)])
    copies.start("ix", in_own, input_out.at[own_rows(0)], x_peer)
    copies.start("ic", in_own, input_out.at[own_rows(0)], core_peer)

    for k in range(4):
        for j in range(2):
            if k or j:
                copies.start(
                    f"g{k}{j}", gacc.at[:, d_block(k, j)], grecv.at[2 * k + j], ((z ^ k) * 2 + (r ^ j), t)
                )
    pump(len(flows))

    pack_second("o")
    for i, k in enumerate((1, 3, 2)):
        add_pack("p", i)
        send_pack("p", i, k)
    add_pack("p", 3)
    total = gacc[:, d_block(0)]
    for k in range(4):
        for j in range(2):
            if k or j:
                copies.arrived(f"g{k}{j}")
                total += grecv[2 * k + j]
    gmine[...] = total
    for j, peer in ((1, core_peer), (2, x_peer), (3, far_peer)):
        copies.start(f"gt{j}", gmine, grecv_t.at[j], peer)
    copies.arrived("ix")
    copies.start("if", input_out.at[own_rows(2)], input_out.at[own_rows(2)], core_peer)

    for m in range(3):
        copies.arrived(f"y3{m}")
        add_y(3, m)
        keep(own_of(3, m), place(m))
    pk_sum = pk_own[3].astype(fl)
    po_sum = po_own[3].astype(fl)
    for i in (0, 2):
        copies.arrived(f"zo{i}")
        po_sum += po_z[i].astype(fl)
    for i in range(3):
        copies.arrived(f"zp{i}")
        pk_sum += pk_z[i].astype(fl)
    qkv_grad[...] = pk_sum
    o_grad[...] = po_sum
    mine = pl.ds(pl.multiple_of(t * kvt, kvt), kvt)
    kv_grad[:, mine] = pk_sum[:, width:]
    for j, peer in ((1, core_peer), (2, x_peer), (3, far_peer)):
        copies.start(f"kg{j}", kv_grad.at[:, mine], kv_grad.at[:, mine], peer)
    total = gmine[...]
    for j in (1, 2, 3):
        copies.arrived(f"gt{j}")
        total += grecv_t[j]
    gains_out[...] = total
    for name in ("ic", "if", "bc", "bf", "kg1", "kg2", "kg3"):
        copies.arrived(name)
    for m in range(3):
        for i in range(3):
            pltpu.make_async_copy(place(m), place(m), zrecv.at[i, m]).wait()
            z_copy(i, m).wait_send()
    copies.all_left()
    for copy in locals_:
        copy.wait()


def backward_part(lengths, nt, dy, hgu, sums, first_gu, first_d, tokens, resid, gain, one, q, kv, mixed, qkv, o):
    group, model = nt.shape
    ff = hgu.shape[2]
    rows = model // 8
    quarter = resid.shape[0]
    slot, width = q.shape
    kvt = qkv.shape[1] - width
    n = 2 + 2 + 2 + 12 + 2 + 8 + 2 + 3 + 7 + 6 + 3 + 3
    shape = jax.ShapeDtypeStruct
    buf = pltpu.VMEM
    return pl.pallas_call(
        backward_kernel,
        out_shape=(
            shape((2, rows, ZN * ff), bf),
            shape((ZN * ff, rows), bf),
            shape((rows, width + kvt), fl),
            shape((rows, 4 * kvt), fl),
            shape((width, rows), fl),
            shape((slot, model), fl),
            shape((slot, model), fl),
            shape((8, rows), fl),
        ),
        in_specs=[pl.BlockSpec(memory_space=pltpu.SMEM)] + [ANY] * 7 + [VMEM] * 2 + [ANY] * 6,
        out_specs=(ANY, ANY, VMEM, VMEM, VMEM, ANY, ANY, VMEM),
        scratch_shapes=[
            buf((3, 2, rows, ff), bf), buf((3, ff, rows), bf),
            buf((3, 2, rows, ff), bf), buf((3, ff, rows), bf),
            buf((3, 2, rows, ff), bf), buf((3, ff, rows), bf),
            buf((slot, model), bf), buf((quarter, model), bf), buf((quarter, model), bf), buf((quarter, model), fl), buf((quarter, model), fl),
            buf((8, model), fl), buf((8, 8, rows), fl), buf((8, rows), fl), buf((4, 8, rows), fl),
            buf((slot, width + kvt), bf), buf((2, slot, kvt), bf), buf((2, slot, kvt), bf),
            buf((slot, kvt), bf), buf((slot, kvt), bf),
            buf((2, quarter, model), bf), buf((2, quarter, model), bf),
            buf((quarter, model), bf), buf((quarter, model), bf),
            buf((4, rows, width + kvt), bf), buf((4, width, rows), bf),
            buf((4, rows, width + kvt), bf), buf((4, width, rows), bf),
            buf((4, rows, width + kvt), bf), buf((4, width, rows), bf),
            buf((3, rows, width + kvt), bf), buf((3, width, rows), bf),
            pltpu.SemaphoreType.DMA((n,)),
            pltpu.SemaphoreType.DMA((n,)),
            pltpu.SemaphoreType.DMA((3, 3)),
            pltpu.SemaphoreType.DMA((3, 3)),
            pltpu.SemaphoreType.DMA((11,)),
            pltpu.SemaphoreType.DMA((8,)),
        ],
        compiler_params=remote_params(4),
        name="backward_part",
    )(lengths, nt, dy, hgu, sums, first_gu, first_d, tokens, resid, gain, one, q, kv, mixed, qkv, o)


def fast(
    tokens,
    cotangent,
    lengths,
    w_query,
    w_keyval,
    w_output,
    w_gateup,
    w_down,
    norm_gains,
    first_query,
    first_keyval,
    first_output,
    first_gateup,
    first_down,
    first_gains,
    second_query,
    second_keyval,
    second_output,
    second_gateup,
    second_down,
    second_gains,
):
    gains_low = jnp.pad(norm_gains.astype(bf).astype(fl), ((0, 6), (0, 0)))
    (
        gateup, down, dy, normed_two, resid, normed_one, query, keyval, mixed, qkv_w, output_w, gain_full,
    ) = forward_part(lengths, w_query, w_keyval, w_output, w_gateup, w_down, gains_low, tokens, cotangent)

    hgu, sums, first_gu, first_d = feed_forward(normed_two, dy, gateup, down)
    (
        gateup_grad, down_grad, qkv_grad, keyval_shard, output_shard, block_output, input_grad, gains_grad,
    ) = backward_part(
        lengths, normed_two, dy, hgu, sums, first_gu, first_d, tokens, resid, gain_full,
        normed_one, query, keyval, mixed, qkv_w, output_w,
    )
    query_shard = qkv_grad[:, : w_query.shape[1]]
    gateup_shard = gateup_grad.astype(fl)
    down_shard = down_grad.astype(fl)
    gains_shard = gains_grad[:2]

    qa = adamw(w_query, query_shard, first_query, second_query, decay_rate)
    ka = adamw(w_keyval, keyval_shard, first_keyval, second_keyval, decay_rate)
    oa = adamw(w_output, output_shard, first_output, second_output, decay_rate)
    ga = adamw(w_gateup, gateup_shard, first_gateup, second_gateup, decay_rate)
    da = adamw(w_down, down_shard, first_down, second_down, decay_rate)
    na = adamw(norm_gains, gains_shard, first_gains, second_gains, 0.0)
    return (block_output, input_grad, *qa, *ka, *oa, *ga, *da, *na)


def solution(mesh):
    query = P("dp", "tensor")
    keyval = P("dp", None)
    output = P("tensor", "dp")
    gateup = P(None, "dp", "tensor")
    gains = P(None, "dp")
    weights = (query, keyval, output, gateup, output, gains)
    return jax.shard_map(
        fast if mesh.shape["dp"] == 2 * ZN and mesh.shape["tensor"] == 4 else general,
        mesh=mesh,
        in_specs=(P("dp", None), P("dp", None), P("dp")) + weights * 3,
        out_specs=(P("dp", None), P("dp", None)) + tuple(w for w in weights for _ in range(4)),
        check_vma=False,
    )
```
